32 devices in a mesh: dp: 8 (over z, core), head: 4 (over y, x).
Axes of the slice: x: 2, y: 2, z: 4, core: 2. Of those that a mesh axis runs over, the one named last changes fastest.
Arguments:
- layer_input_rows: bfloat16 [32, 1024, 1024], P(('dp', 'head')), may hold values from -6 to 6
- lengths: int32 [32], P('dp'), may hold values from 128 to 1024, as said below
- cotangent: bfloat16 [32, 1024, 1024], P(('dp', 'head')), may hold values from -6 to 6
- frozen_projection_weight: bfloat16 [3, 1024, 1024], P(None, None, 'head'), may hold values from -0.1875 to 0.1875
- frozen_outproj_weight: bfloat16 [1024, 1024], P('head'), may hold values from -1.5 to 1.5
- frozen_up_weight: bfloat16 [1024, 4096], P(None, 'head'), may hold values from -0.1875 to 0.1875
- frozen_down_weight: bfloat16 [4096, 1024], P('head'), may hold values from -0.09375 to 0.09375
- frozen_norm_gain: float32 [2, 1024], replicated, may hold values from 0.5 to 2
- frozen_norm_bias: float32 [2, 1024], replicated, may hold values from -1.75 to 1.75
- shared_input_factors: float32 [4, 1024, 128], replicated, may hold values from -0.1875 to 0.1875
- outproj_input_factor: float32 [1024, 128], P('head'), may hold values from -1.5 to 1.5
- down_input_factor: float32 [4096, 128], P('head'), may hold values from -0.09375 to 0.09375
- projection_output_factors: float32 [3, 128, 1024], P(None, None, 'head'), may hold values from -0.5 to 0.5
- up_output_factor: float32 [128, 4096], P(None, 'head'), may hold values from -0.5 to 0.5
- output_side_factors: float32 [2, 128, 1024], replicated, may hold values from -0.5 to 0.5
- input_factor_moments: float32 [2, 4, 1024, 128], replicated, as said below
- outproj_input_factor_moments: float32 [2, 1024, 128], P(None, 'head'), as said below
- down_input_factor_moments: float32 [2, 4096, 128], P(None, 'head'), as said below
- projection_output_factor_moments: float32 [2, 3, 128, 1024], P(None, None, None, 'head'), as said below
- up_output_factor_moments: float32 [2, 128, 4096], P(None, None, 'head'), as said below
- outproj_output_factor_moments: float32 [2, 2, 128, 1024], replicated, as said below
- reset_input_factor: bfloat16 [4, 1024, 128], replicated, may hold values from -0.1875 to 0.1875
- reset_outproj_input_factor: bfloat16 [1024, 128], P('head'), may hold values from -1.5 to 1.5
- reset_down_input_factor: bfloat16 [4096, 128], P('head'), may hold values from -0.09375 to 0.09375
- component_merge_mask: int32 [128], replicated, may hold values 0 or 1
Outputs:
- layer_out: float32 [32, 1024, 1024], P(('dp', 'head'))
- grad_in: float32 [32, 1024, 1024], P(('dp', 'head'))
- new_a_in: float32 [4, 1024, 128], replicated
- new_a_out: float32 [1024, 128], P('head')
- new_a_down: float32 [4096, 128], P('head')
- new_b_qkv: float32 [3, 128, 1024], P(None, None, 'head')
- new_b_up: float32 [128, 4096], P(None, 'head')
- new_b_out: float32 [2, 128, 1024], replicated
- new_moments_a_in: float32 [2, 4, 1024, 128], replicated
- new_moments_a_out: float32 [2, 1024, 128], P(None, 'head')
- new_moments_a_down: float32 [2, 4096, 128], P(None, 'head')
- new_moments_b_qkv: float32 [2, 3, 128, 1024], P(None, None, None, 'head')
- new_moments_b_up: float32 [2, 128, 4096], P(None, None, 'head')
- new_moments_b_out: float32 [2, 2, 128, 1024], replicated
- combined_projection_weight: float32 [3, 1024, 1024], P(None, None, 'head')
- combined_outproj_weight: float32 [1024, 1024], P('head')
- combined_up_weight: float32 [1024, 4096], P(None, 'head')
- combined_down_weight: float32 [4096, 1024], P('head')
- copy_qkv: bfloat16 [3, 1024, 1024], P(None, None, 'head')
- copy_out: bfloat16 [1024, 1024], P('head')
- copy_up: bfloat16 [1024, 4096], P(None, 'head')
- copy_down: bfloat16 [4096, 1024], P('head')
The draws below stay inside these ranges and needn't reach their ends.
Inputs may be any that keep to these rules, and one draw needn't show every extreme that they name: `lengths`: in every aligned group of 4 sequences (one index of dp) one sequence, drawn from the seed, has length 1024; slots at or beyond a sequence's length are padding. `input_factor_moments`: index 0 holds first moments, index 1 second moments, which are positive. `outproj_input_factor_moments`: index 0 holds first moments, index 1 second moments, which are positive. `down_input_factor_moments`: index 0 holds first moments, index 1 second moments, which are positive. `projection_output_factor_moments`: index 0 holds first moments, index 1 second moments, which are positive. `up_output_factor_moments`: index 0 holds first moments, index 1 second moments, which are positive. `outproj_output_factor_moments`: index 0 holds first moments, index 1 second moments, which are positive.
All inputs are finite; a program needn't handle non-finite values.
Results may differ from the reference program's by a relative error of at most 0.023.
The reference program's roundings to bfloat16 on the way count: a program that leaves them out, or rounds other values in their place, can miss the bound.
Values may be sent and summed in bfloat16 or wider, within the bound.
A program may use at most 320 MiB of HBM per device.

```python
import math
import jax
import jax.numpy as jnp
from jax import lax

MODEL_WIDTH = 1024
HEADS = 16
HEAD_DIM = 64
HIDDEN_UNITS = 4096
FACTOR_RANK = 128
ROT_DIM = 16
PAD_LEN = 1024
MIN_LEN = 128
STEP = 10
SEQS_GROUP = 4
SEQS = 32


def draw_lengths(key, part):
    picked = jax.random.randint(jax.random.fold_in(key, 1), (SEQS,), MIN_LEN, PAD_LEN + 1)
    groups = SEQS // SEQS_GROUP
    longest = jax.random.randint(jax.random.fold_in(key, 2), (groups,), 0, SEQS_GROUP)
    factor_member = jnp.arange(SEQS, dtype=jnp.int32) % SEQS_GROUP
    chosen = jnp.repeat(longest, SEQS_GROUP)
    return jnp.where(factor_member == chosen, PAD_LEN, picked).astype(jnp.int32)


def moment_pair(key, dims_shape, factor):
    grad_size = factor * math.sqrt(0.5 * SEQS * (PAD_LEN + MIN_LEN))
    first_moment = jax.random.normal(jax.random.fold_in(key, 11), dims_shape, jnp.float32) * (grad_size * 0.11)
    level_factor = jnp.exp(jax.random.uniform(jax.random.fold_in(key, 12), dims_shape, jnp.float32, 0.0, math.log(4.0)))
    entry_factor = jnp.exp(jax.random.uniform(jax.random.fold_in(key, 13), dims_shape, jnp.float32, math.log(0.5), math.log(2.0)))
    second_moment = level_factor * entry_factor * (grad_size * grad_size * 0.001)
    return jnp.stack([first_moment, second_moment]).astype(jnp.float32)


def draw_input_factor_moments(key, part):
    return moment_pair(key, (4, MODEL_WIDTH, FACTOR_RANK), 0.35)


def draw_outproj_input_factor_moments(key, part):
    return moment_pair(key, (MODEL_WIDTH, FACTOR_RANK), 0.06)


def draw_down_input_factor_moments(key, part):
    return moment_pair(key, (HIDDEN_UNITS, FACTOR_RANK), 0.35)


def draw_projection_output_factor_moments(key, part):
    return moment_pair(key, (3, FACTOR_RANK, MODEL_WIDTH), 0.12)


def draw_up_output_factor_moments(key, part):
    return moment_pair(key, (FACTOR_RANK, HIDDEN_UNITS), 0.12)


def draw_outproj_output_factor_moments(key, part):
    return moment_pair(key, (2, FACTOR_RANK, MODEL_WIDTH), 0.15)


def place_ends(array, own_key, least, top_value):
    spot = [jax.random.randint(jax.random.fold_in(own_key, axis), (), 0, length) for axis, length in enumerate(array.shape)]
    widest = array.shape.index(max(array.shape))
    beside = spot[:widest] + [(spot[widest] + 1) % array.shape[widest]] + spot[widest + 1:]
    return array.at[tuple(spot)].set(least).at[tuple(beside)].set(top_value)


def block_scale(own_key, shape, split, low, high):
    loudness, own = 1.0, jax.random.fold_in(own_key, 6)
    for axis_at, parts in split:
        steps = jnp.exp(jax.random.uniform(jax.random.fold_in(own, axis_at), (parts,), jnp.float32, low / len(split), high / len(split)))
        loudness = loudness * jnp.repeat(steps, shape[axis_at] // parts).reshape([-1 if axis == axis_at else 1 for axis in range(len(shape))])
    return loudness


def noise(rng, dims, scale, reach, split=(), held_as=jnp.bfloat16):
    level = block_scale(rng, dims, split, -0.22, 0.18) if split else 1.0
    array = jax.random.normal(rng, dims, jnp.float32) * scale * level
    return jnp.minimum(jnp.maximum(array, -reach), reach).astype(held_as)


def setup_inputs(seed: int = 0) -> dict:
    key_list = jax.random.split(jax.random.key(seed), 26)
    return {
        "layer_input_rows": noise(key_list[0], (SEQS, PAD_LEN, MODEL_WIDTH), 1.0, 6.0, ((0, 32),)),
        "lengths": draw_lengths(jax.random.fold_in(key_list[25], 71), 0),
        "cotangent": noise(key_list[2], (SEQS, PAD_LEN, MODEL_WIDTH), 1.0, 6.0, ((0, 32),)),
        "frozen_projection_weight": noise(key_list[3], (3, MODEL_WIDTH, MODEL_WIDTH), MODEL_WIDTH ** -0.5, 0.1875, ((2, 4),)),
        "frozen_outproj_weight": noise(key_list[4], (MODEL_WIDTH, MODEL_WIDTH), (MODEL_WIDTH // 64) ** -0.5, 1.5, ((0, 4),)),
        "frozen_up_weight": noise(key_list[5], (MODEL_WIDTH, HIDDEN_UNITS), MODEL_WIDTH ** -0.5, 0.1875, ((1, 4),)),
        "frozen_down_weight": noise(key_list[6], (HIDDEN_UNITS, MODEL_WIDTH), HIDDEN_UNITS ** -0.5, 0.09375, ((0, 4),)),
        "frozen_norm_gain": jnp.clip(jnp.exp(jax.random.uniform(key_list[7], (2, MODEL_WIDTH), jnp.float32, math.log(0.5), math.log(2.0))), 0.5, 2.0),
        "frozen_norm_bias": noise(key_list[8], (2, MODEL_WIDTH), 0.3, 1.75, (), jnp.float32),
        "shared_input_factors": noise(key_list[9], (4, MODEL_WIDTH, FACTOR_RANK), MODEL_WIDTH ** -0.5, 0.1875, (), jnp.float32),
        "outproj_input_factor": noise(key_list[10], (MODEL_WIDTH, FACTOR_RANK), (MODEL_WIDTH // 64) ** -0.5, 1.5, ((0, 4),), jnp.float32),
        "down_input_factor": noise(key_list[11], (HIDDEN_UNITS, FACTOR_RANK), HIDDEN_UNITS ** -0.5, 0.09375, ((0, 4),), jnp.float32),
        "projection_output_factors": noise(key_list[12], (3, FACTOR_RANK, MODEL_WIDTH), FACTOR_RANK ** -0.5, 0.5, ((2, 4),), jnp.float32),
        "up_output_factor": noise(key_list[13], (FACTOR_RANK, HIDDEN_UNITS), FACTOR_RANK ** -0.5, 0.5, ((1, 4),), jnp.float32),
        "output_side_factors": noise(key_list[14], (2, FACTOR_RANK, MODEL_WIDTH), FACTOR_RANK ** -0.5, 0.5, (), jnp.float32),
        "input_factor_moments": draw_input_factor_moments(jax.random.fold_in(key_list[25], 71), 0),
        "outproj_input_factor_moments": draw_outproj_input_factor_moments(jax.random.fold_in(key_list[25], 71), 0),
        "down_input_factor_moments": draw_down_input_factor_moments(jax.random.fold_in(key_list[25], 71), 0),
        "projection_output_factor_moments": draw_projection_output_factor_moments(jax.random.fold_in(key_list[25], 71), 0),
        "up_output_factor_moments": draw_up_output_factor_moments(jax.random.fold_in(key_list[25], 71), 0),
        "outproj_output_factor_moments": draw_outproj_output_factor_moments(jax.random.fold_in(key_list[25], 71), 0),
        "reset_input_factor": noise(key_list[21], (4, MODEL_WIDTH, FACTOR_RANK), MODEL_WIDTH ** -0.5, 0.1875),
        "reset_outproj_input_factor": noise(key_list[22], (MODEL_WIDTH, FACTOR_RANK), (MODEL_WIDTH // 64) ** -0.5, 1.5, ((0, 4),)),
        "reset_down_input_factor": noise(key_list[23], (HIDDEN_UNITS, FACTOR_RANK), HIDDEN_UNITS ** -0.5, 0.09375, ((0, 4),)),
        "component_merge_mask": place_ends((jax.random.randint(key_list[24], (FACTOR_RANK,), 0, 2) < 1).astype(jnp.int32), jax.random.fold_in(key_list[24], 1), 0, 1),
    }


NORM_EPSILON = 1e-05
LOWRANK_SCALE = 0.25
LEARN_RATE = 0.15
BETA_FIRST = 0.9
BETA_SECOND = 0.999
WEIGHT_DECAY = 0.01
ADAM_EPSILON = 1e-08
ROPE_BASE = 10000.0

@jax.custom_vjp
def lowered_values(v):
    return lax.optimization_barrier(v.astype(jnp.bfloat16)).astype(jnp.float32)

@jax.custom_vjp
def lowered_backward(v):
    return v

def low_keep(v):
    return (lowered_values(v), None)

def low_pass(kept, grad):
    return (grad,)

def back_keep(v):
    return (v, None)

def back_low(kept, grad):
    return (lowered_values(grad),)
lowered_values.defvjp(low_keep, low_pass)
lowered_backward.defvjp(back_keep, back_low)

def precise_product(left_side, right_side):
    return jnp.dot(left_side, right_side, precision=lax.Precision.HIGHEST, preferred_element_type=jnp.float32)

def normalize(row_data, gain_row, bias_row):
    average = lax.optimization_barrier(jnp.mean(row_data, axis=-1, keepdims=True))
    centred = row_data - average
    spread = lax.optimization_barrier(jnp.mean(centred * centred, axis=-1, keepdims=True))
    return centred * lax.rsqrt(spread + NORM_EPSILON) * gain_row + bias_row

def rotate(positions, values_in):
    half_dim = ROT_DIM // 2
    frequency = ROPE_BASE ** (-2.0 * jnp.arange(half_dim, dtype=jnp.float32) / ROT_DIM)
    angles = positions.astype(jnp.float32)[:, None] * frequency[None, :]
    cosine_table = jnp.concatenate([jnp.cos(angles), jnp.cos(angles)], axis=-1)[:, None, :]
    sine_table = jnp.concatenate([jnp.sin(angles), jnp.sin(angles)], axis=-1)[:, None, :]
    turned = values_in[..., :ROT_DIM]
    lower_half = turned[..., :half_dim]
    upper_half = turned[..., half_dim:]
    swapped = jnp.concatenate([-upper_half, lower_half], axis=-1)
    return jnp.concatenate([turned * cosine_table + swapped * sine_table, values_in[..., ROT_DIM:]], axis=-1)

def attend_ref(queries, keys_rot, values, length):
    block_rows = min(512, PAD_LEN)
    block_count = PAD_LEN // block_rows
    key_pos = jnp.arange(PAD_LEN, dtype=jnp.int32)
    score_scale = HEAD_DIM ** (-0.5)

    def one_block(block_start):
        query_rows = lax.dynamic_slice_in_dim(queries, block_start, block_rows, 0)
        scores = jnp.einsum('qhd,khd->hqk', query_rows, keys_rot, precision=lax.Precision.HIGHEST, preferred_element_type=jnp.float32)
        scores = lowered_backward(score_scale * scores)
        query_pos = block_start + jnp.arange(block_rows, dtype=jnp.int32)
        allowed = (key_pos[None, :] <= query_pos[:, None]) & (key_pos[None, :] < length)
        scores = jnp.where(allowed[None], scores, -1e+30)
        weights = lowered_values(jax.nn.softmax(scores, axis=-1))
        return jnp.einsum('hqk,khd->qhd', weights, values, precision=lax.Precision.HIGHEST, preferred_element_type=jnp.float32)
    starts = jnp.arange(block_count, dtype=jnp.int32) * block_rows
    blocks = lax.map(jax.checkpoint(one_block), starts)
    return blocks.reshape(PAD_LEN, HEADS * HEAD_DIM)

def layer_forward(factor_collection, frozen, sequence, length):
    shared_input_factors, outproj_input_factor, down_input_factor, projection_output_factors, up_output_factor, output_side_factors = factor_collection
    frozen_projection_weight, frozen_outproj_weight, frozen_up_weight, frozen_down_weight, frozen_norm_gain, frozen_norm_bias = frozen
    positions = jnp.arange(PAD_LEN, dtype=jnp.int32)
    first_normalized = lowered_values(normalize(sequence, frozen_norm_gain[0], frozen_norm_bias[0]))
    second_normalized = lowered_values(normalize(sequence, frozen_norm_gain[1], frozen_norm_bias[1]))
    input_factor_lowp = lowered_values(shared_input_factors)
    projection_output_factor_lowp = lowered_values(projection_output_factors)
    outproj_output_factor_lowp = lowered_values(output_side_factors)
    projection_result = []
    for factor_member in range(3):
        rank_latent = lowered_values(lowered_backward(precise_product(first_normalized, input_factor_lowp[factor_member])))
        frozen_contribution = precise_product(first_normalized, frozen_projection_weight[factor_member]) + LOWRANK_SCALE * precise_product(rank_latent, projection_output_factor_lowp[factor_member])
        projection_result.append(lowered_backward(frozen_contribution).reshape(PAD_LEN, HEADS, HEAD_DIM))
    up_rank_latent = lowered_values(lowered_backward(precise_product(second_normalized, input_factor_lowp[3])))
    queries = lowered_values(rotate(positions, projection_result[0]))
    keys_rot = lowered_values(rotate(positions, projection_result[1]))
    values = lowered_values(projection_result[2])
    attention_context = lowered_values(lowered_backward(attend_ref(queries, keys_rot, values, length)))
    outproj_rank_latent = lowered_values(lowered_backward(precise_product(attention_context, lowered_values(outproj_input_factor))))
    attention_path = precise_product(attention_context, frozen_outproj_weight) + LOWRANK_SCALE * precise_product(outproj_rank_latent, outproj_output_factor_lowp[0])
    hidden_linear = lowered_backward(precise_product(second_normalized, frozen_up_weight) + LOWRANK_SCALE * precise_product(up_rank_latent, lowered_values(up_output_factor)))
    hidden_activation = lowered_values(jax.nn.gelu(hidden_linear, approximate=False))
    down_rank_latent = lowered_values(lowered_backward(precise_product(hidden_activation, lowered_values(down_input_factor))))
    perceptron_path = precise_product(hidden_activation, frozen_down_weight) + LOWRANK_SCALE * precise_product(down_rank_latent, outproj_output_factor_lowp[1])
    return sequence + attention_path + perceptron_path

def adamw(weight, moment, gradient):
    first_moment = BETA_FIRST * moment[0] + (1.0 - BETA_FIRST) * gradient
    second_moment = BETA_SECOND * moment[1] + (1.0 - BETA_SECOND) * gradient * gradient
    corrected_first = first_moment / (1.0 - BETA_FIRST ** STEP)
    corrected_second = second_moment / (1.0 - BETA_SECOND ** STEP)
    updated = weight - LEARN_RATE * (corrected_first / (jnp.sqrt(corrected_second) + ADAM_EPSILON) + WEIGHT_DECAY * weight)
    return (updated, first_moment, second_moment)

def apply_update(factor_collection, moments, gradients, fresh, component_merge_mask, frozen_weights):
    merge_indicators = component_merge_mask.astype(jnp.float32)
    keep_cols = 1.0 - merge_indicators
    keep_rows = keep_cols[:, None]
    stepped = [adamw(weight, moment, gradient) for weight, moment, gradient in zip(factor_collection, moments, gradients)]
    input_factor_stepped, outproj_input_factor_stepped, down_input_factor_stepped, projection_output_factor_stepped, up_output_factor_stepped, outproj_output_factor_stepped = [triple[0] for triple in stepped]
    frozen_projection_weight, frozen_outproj_weight, frozen_up_weight, frozen_down_weight = frozen_weights
    combined_projection_weight = frozen_projection_weight.astype(jnp.float32) + LOWRANK_SCALE * jnp.einsum('czs,cso->czo', input_factor_stepped[:3] * merge_indicators, projection_output_factor_stepped, precision=lax.Precision.HIGHEST, preferred_element_type=jnp.float32)
    combined_outproj_weight = frozen_outproj_weight.astype(jnp.float32) + LOWRANK_SCALE * precise_product(outproj_input_factor_stepped * merge_indicators, outproj_output_factor_stepped[0])
    combined_up_weight = frozen_up_weight.astype(jnp.float32) + LOWRANK_SCALE * precise_product(input_factor_stepped[3] * merge_indicators, up_output_factor_stepped)
    combined_down_weight = frozen_down_weight.astype(jnp.float32) + LOWRANK_SCALE * precise_product(down_input_factor_stepped * merge_indicators, outproj_output_factor_stepped[1])
    fresh_in, fresh_out, fresh_down = fresh
    new_factors = (jnp.where(merge_indicators > 0.5, fresh_in.astype(jnp.float32), input_factor_stepped), jnp.where(merge_indicators > 0.5, fresh_out.astype(jnp.float32), outproj_input_factor_stepped), jnp.where(merge_indicators > 0.5, fresh_down.astype(jnp.float32), down_input_factor_stepped), projection_output_factor_stepped * keep_rows, up_output_factor_stepped * keep_rows, outproj_output_factor_stepped * keep_rows)
    keeps = (keep_cols, keep_cols, keep_cols, keep_rows, keep_rows, keep_rows)
    new_moments = tuple((jnp.stack([triple[1] * keeper, triple[2] * keeper]) for triple, keeper in zip(stepped, keeps)))
    merged = (combined_projection_weight, combined_outproj_weight, combined_up_weight, combined_down_weight)
    copies = tuple((weight.astype(jnp.bfloat16) for weight in merged))
    return (new_factors, new_moments, merged, copies)

def reference(layer_input_rows, lengths, cotangent, frozen_projection_weight, frozen_outproj_weight, frozen_up_weight, frozen_down_weight, frozen_norm_gain, frozen_norm_bias, shared_input_factors, outproj_input_factor, down_input_factor, projection_output_factors, up_output_factor, output_side_factors, input_factor_moments, outproj_input_factor_moments, down_input_factor_moments, projection_output_factor_moments, up_output_factor_moments, outproj_output_factor_moments, reset_input_factor, reset_outproj_input_factor, reset_down_input_factor, component_merge_mask):
    frozen = (frozen_projection_weight.astype(jnp.float32), frozen_outproj_weight.astype(jnp.float32), frozen_up_weight.astype(jnp.float32), frozen_down_weight.astype(jnp.float32), frozen_norm_gain, frozen_norm_bias)
    factor_collection = (shared_input_factors, outproj_input_factor, down_input_factor, projection_output_factors, up_output_factor, output_side_factors)
    positions = jnp.arange(PAD_LEN, dtype=jnp.int32)

    def per_sequence(totals, seq_items):
        sequence, length, grad_rows = seq_items
        live_rows = (positions < length).astype(jnp.float32)[:, None]

        def forward(factor_set, layer_rows):
            return layer_forward(factor_set, frozen, layer_rows, length)
        output_rows, pullback = jax.vjp(forward, factor_collection, sequence.astype(jnp.float32))
        factor_grads, row_grads = pullback(grad_rows.astype(jnp.float32) * live_rows)
        return (jax.tree.map(jnp.add, totals, factor_grads), (output_rows, row_grads))
    zero_set = jax.tree.map(jnp.zeros_like, factor_collection)
    factor_totals, (layer_out, grad_in) = lax.scan(per_sequence, zero_set, (layer_input_rows, lengths, cotangent))
    moments = (input_factor_moments, outproj_input_factor_moments, down_input_factor_moments, projection_output_factor_moments, up_output_factor_moments, outproj_output_factor_moments)
    new_factors, new_moments, merged, copies = apply_update(factor_collection, moments, factor_totals, (reset_input_factor, reset_outproj_input_factor, reset_down_input_factor), component_merge_mask, (frozen_projection_weight, frozen_outproj_weight, frozen_up_weight, frozen_down_weight))
    return (layer_out, grad_in, new_factors[0], new_factors[1], new_factors[2], new_factors[3], new_factors[4], new_factors[5], new_moments[0], new_moments[1], new_moments[2], new_moments[3], new_moments[4], new_moments[5], merged[0], merged[1], merged[2], merged[3], copies[0], copies[1], copies[2], copies[3])
```

```python
from functools import partial

import jax
import jax.numpy as jnp
import numpy as np
from jax import lax
from jax.experimental import pallas as pl
from jax.experimental.pallas import tpu as pltpu
from jax.sharding import PartitionSpec as P

HEAD_DIM = 64
ROT_DIM = 16
STEP = 10
RANK = 128
LANES = 128
QROWS = 256


NORM_EPSILON = 1e-05
LOWRANK_SCALE = 0.25
LEARN_RATE = 0.15
BETA_FIRST = 0.9
BETA_SECOND = 0.999
WEIGHT_DECAY = 0.01
ADAM_EPSILON = 1e-08
ROPE_BASE = 10000.0

BF = jnp.bfloat16
F32 = jnp.float32
ANY = pl.BlockSpec(memory_space=pltpu.HBM)
VMEM = pl.BlockSpec(memory_space=pltpu.VMEM)
SMEM = pl.BlockSpec(memory_space=pltpu.SMEM)
NN = (((1,), (0,)), ((), ()))
NT = (((1,), (1,)), ((), ()))
TN = (((0,), (0,)), ((), ()))


def dot(left, right, dims=NN):
    return lax.dot_general(left, right, dims, preferred_element_type=F32)


def params(mib=60):
    return pltpu.CompilerParams(vmem_limit_bytes=mib * 1024 * 1024)


def cost(micros, nbytes):
    return pl.CostEstimate(flops=int(micros * 1.15e9), bytes_accessed=nbytes, transcendentals=0)


def rows_of(block, size):
    return pl.ds(pl.multiple_of(block * size, size), size)


def pack_kernel(kind, shape, core_ref, *refs):
    width, depth, parts = shape
    part = width // parts
    w1, w2, b, a, packed, b_low, a_low, w1_s, w2_s, load, sems = refs
    core = core_ref[0]
    loads = [
        pltpu.make_async_copy(src, dst, load.at[at])
        for at, (src, dst) in enumerate(((w1, w1_s), (w2, w2_s)))
    ]
    for copy in loads:
        copy.start()
    copies = []

    def start(src, dst):
        copy = pltpu.make_async_copy(src, dst, sems.at[len(copies)])
        copy.start()
        copies.append(copy)

    lanes = pl.ds(pl.multiple_of(core * part, part), part)
    b_low[...] = (b[...] * LOWRANK_SCALE).astype(BF)
    a_low[...] = a[...].astype(BF)
    many = 3 if kind == "attn" else 1
    loads[0].wait()
    for j in range(many):
        src = (w1_s.at[j], b_low.at[j]) if kind == "attn" else (w1_s, b_low)
        start(src[0].at[:, lanes], packed.at[pl.ds(j * depth, depth), :])
        start(src[1].at[:, lanes], packed.at[pl.ds((many + 1) * depth + j * RANK, RANK), :])
    at = (many + 1) * depth + many * RANK
    for m in range(part // RANK):
        start(
            a_low.at[pl.ds(pl.multiple_of(core * part + m * RANK, RANK), RANK), :],
            packed.at[pl.ds(at, RANK), pl.ds(m * RANK, RANK)],
        )
    loads[1].wait()
    for m in range(depth // part):
        start(w2_s.at[lanes, pl.ds(m * part, part)], packed.at[pl.ds(many * depth + m * part, part), :])
    for copy in copies:
        copy.wait()


def pack(kind, core, w1, w2, b, a, parts):
    depth, width = w1.shape[-2:]
    part = width // parts
    many = 3 if kind == "attn" else 1
    count = 2 * many + part // RANK + depth // part
    return pl.pallas_call(
        partial(pack_kernel, kind, (width, depth, parts)),
        out_shape=(
            jax.ShapeDtypeStruct(((many + 1) * depth + (many + 1) * RANK, part), BF),
            jax.ShapeDtypeStruct(b.shape, BF),
            jax.ShapeDtypeStruct(a.shape, BF),
        ),
        in_specs=[SMEM, ANY, ANY, VMEM, VMEM],
        out_specs=(ANY, VMEM, VMEM),
        scratch_shapes=[
            pltpu.VMEM(w1.shape, BF),
            pltpu.VMEM(w2.shape, BF),
            pltpu.SemaphoreType.DMA((2,)),
            pltpu.SemaphoreType.DMA((count,)),
        ],
        compiler_params=params(),
        cost_estimate=cost(3, 4 << 20),
        name="pack_" + kind,
    )(core, w1, w2, b, a)


def norm_stats(x):
    mean = jnp.mean(x, axis=-1, keepdims=True)
    centred = x - mean
    spread = jnp.mean(centred * centred, axis=-1, keepdims=True)
    return centred, lax.rsqrt(spread + NORM_EPSILON)


def prologue_kernel(which, length, x, cot, gain, bias, a_in, b_out, u, z, dz, acat, bcat, *g):
    step = pl.program_id(0)

    @pl.when(step == 0)
    def _():
        for j in range(a_in.shape[0]):
            acat[:, j * RANK : (j + 1) * RANK] = a_in[j].astype(BF)
        bcat[...] = (b_out[0] * LOWRANK_SCALE).astype(BF)

    rows = x.shape[0]
    centred, scale = norm_stats(x[...].astype(F32))
    low = (centred * scale * gain[which : which + 1, :] + bias[which : which + 1, :]).astype(BF)
    u[...] = low
    z[...] = dot(low, acat[...]).astype(BF)
    if g:
        place = step * rows + lax.broadcasted_iota(jnp.int32, (rows, 1), 0)
        live = (place < length[0]).astype(F32)
        grad = (cot[...].astype(F32) * live).astype(BF)
        g[0][...] = grad
    else:
        grad = cot[...]
    dz[...] = dot(grad, bcat[...], NT).astype(BF)


def prologue(which, length, x, cot, gain, bias, a_in, b_out):
    full, depth = x.shape
    rows = 256
    many = 3 if which == 0 else 1
    blk = lambda cols: pl.BlockSpec((rows, cols), lambda i: (i, 0))
    const = lambda shape: pl.BlockSpec(shape, lambda i: (0,) * len(shape))
    shape = jax.ShapeDtypeStruct
    out_shape = [
        shape((full, depth), BF),
        shape((full, many * RANK), BF),
        shape((full, RANK), BF),
        shape((depth, many * RANK), BF),
        shape((RANK, depth), BF),
    ]
    out_specs = [blk(depth), blk(many * RANK), blk(RANK), const((depth, many * RANK)), const((RANK, depth))]
    if which == 0:
        out_shape.append(shape((full, depth), BF))
        out_specs.append(blk(depth))
    return pl.pallas_call(
        partial(prologue_kernel, which),
        grid=(full // rows,),
        out_shape=out_shape,
        in_specs=[
            SMEM, blk(depth), blk(depth), const(gain.shape), const(bias.shape),
            pl.BlockSpec((many, depth, RANK), lambda i: (which, 0, 0) if which == 0 else (3, 0, 0)),
            pl.BlockSpec((1, RANK, depth), lambda i: (which, 0, 0)),
        ],
        out_specs=out_specs,
        compiler_params=params(),
        cost_estimate=cost(4, 12 << 20),
        name=("prologue_attn", "prologue_mlp")[which],
    )(length, x, cot, gain, bias, a_in, b_out)


def turn(x, cosine, low, high, sign):
    done = []
    for at in range(0, x.shape[1], LANES):
        part = x[:, at : at + LANES]
        shifted = pltpu.roll(part, LANES - ROT_DIM // 2, 1) * low
        shifted = shifted + pltpu.roll(part, ROT_DIM // 2, 1) * high
        done.append(part * cosine + shifted if sign > 0 else part * cosine - shifted)
    return done[0] if len(done) == 1 else jnp.concatenate(done, axis=1)


def attention_kernel(cfg, *refs):
    own, shards, carried, width, depth, full, parts = cfg
    wp = width // parts
    it = iter(refs)
    take = lambda count: [next(it) for _ in range(count)]
    length, core_ref, u_h, z_h, g_h, dz_h, cos_h, low_h, high_h = take(9)
    sources = take(4) if own else [take(parts) for _ in range(shards)]
    acc_h = take(4) if carried else None
    out_h = take(4)
    (grads,) = take(1)
    (u_s, z_s, g_s, dz_s, cos_s, low_s, high_s) = take(7)
    wq_s, wo_s, b_s, a_s = take(4)
    acc_s = take(4)
    q_s, k_s, v_s, dc_s, c_s, dp_s, dk_s, dv_s = take(8)
    sem_in, sem_w, sem_acc, sem_out = take(4)
    acc_o, acc_u, acc_z, acc_dz = acc_s

    ins = [
        pltpu.make_async_copy(src, dst, sem_in.at[at])
        for at, (src, dst) in enumerate(
            zip(
                [u_h, z_h, g_h, dz_h, cos_h, low_h, high_h],
                [u_s, z_s, g_s, dz_s, cos_s, low_s, high_s],
            )
        )
    ]

    def weight_copies(shard):
        slot = shard % 2
        made = []

        def add(src, dst):
            made.append(pltpu.make_async_copy(src, dst, sem_w.at[slot, len(made)]))

        if own:
            for src, dst in zip(sources, (wq_s, wo_s, b_s, a_s)):
                add(src, dst.at[slot])
        else:
            for p in range(parts):
                ref = sources[shard][p]
                dst = pl.ds(p * wp, wp)
                for j in range(3):
                    add(ref.at[pl.ds(j * depth, depth), :], wq_s.at[slot, j, :, dst])
                for m in range(depth // wp):
                    add(
                        ref.at[pl.ds(3 * depth + m * wp, wp), :],
                        wo_s.at[slot, dst, pl.ds(m * wp, wp)],
                    )
                for j in range(3):
                    add(ref.at[pl.ds(4 * depth + j * RANK, RANK), :], b_s.at[slot, j, :, dst])
                add(ref.at[pl.ds(4 * depth + 3 * RANK, wp), :], a_s.at[slot, dst, :])
        return made

    for copy in weight_copies(0):
        copy.start()
    for copy in ins:
        copy.start()
    if carried:
        acc_in = [
            pltpu.make_async_copy(src, dst, sem_acc.at[at])
            for at, (src, dst) in enumerate(zip(acc_h, acc_s))
        ]
        for copy in acc_in:
            copy.start()
    big = 512
    key_place = lax.broadcasted_iota(jnp.int32, (1, full), 1)
    key_bias = jnp.where(key_place < length[0], 0.0, -1e30).astype(F32)
    lane_place = lax.broadcasted_iota(jnp.int32, (1, LANES), 1)
    masks = [
        (lane_place // HEAD_DIM == h).astype(F32).astype(BF) for h in range(LANES // HEAD_DIM)
    ]
    causal = lax.broadcasted_iota(jnp.int32, (QROWS, QROWS), 1) <= lax.broadcasted_iota(
        jnp.int32, (QROWS, QROWS), 0
    )
    for copy in ins:
        copy.wait()

    def out_copies(block):
        rows = pl.ds(block * big, big)
        return [
            pltpu.make_async_copy(src.at[rows, :], dst.at[rows, :], sem_out.at[block, at])
            for at, (src, dst) in enumerate(zip(acc_s, out_h))
        ]

    def place(p):
        if not own or parts == 1:
            return p
        return core_ref[0] if p == 0 else 1 - core_ref[0]

    def one_shard(s, slot, first_shard, last_shard):
        def project(block, carry):
            rows = rows_of(block, big)
            ub = u_s[rows, :]
            cosine, low, high = cos_s[rows, :], low_s[rows, :], high_s[rows, :]
            for j, dst in enumerate((q_s, k_s, v_s)):
                value = dot(ub, wq_s[slot, j]) + dot(z_s[rows, pl.ds(j * RANK, RANK)], b_s[slot, j])
                if j < 2:
                    value = turn(value, cosine, low, high, 1)
                if j == 0:
                    value = value * HEAD_DIM ** (-0.5)
                dst[rows, :] = value.astype(BF)
            dc_s[rows, :] = (
                dot(g_s[rows, :], wo_s[slot], NT) + dot(dz_s[rows, :], a_s[slot], NT)
            ).astype(BF)
            return carry

        lax.fori_loop(0, full // big, project, 0)

        def pair(at, carry):
            lanes = pl.ds(pl.multiple_of(at * LANES, LANES), LANES)
            for i in range(full // QROWS):
                begin, end = i * QROWS, (i + 1) * QROWS
                rows = pl.ds(begin, QROWS)
                qb, db = q_s[rows, lanes], dc_s[rows, lanes]
                keys, vals = k_s[pl.ds(0, end), lanes], v_s[pl.ds(0, end), lanes]
                context = dq = dk = dv = None
                plus = lambda total, term: term if total is None else total + term
                for mask in masks:
                    qm, dm = qb * mask, db * mask
                    scores = dot(qm, keys, NT) + key_bias[:, :end]
                    diag = jnp.where(causal, scores[:, begin:], -1e30)
                    scores = diag if i == 0 else jnp.concatenate([scores[:, :begin], diag], axis=1)
                    peak = jnp.max(scores, axis=-1, keepdims=True)
                    raised = jnp.exp(scores - peak)
                    total = jnp.sum(raised, axis=-1, keepdims=True)
                    weights = raised * (1.0 / total)
                    low_weights = weights.astype(BF)
                    grad = dot(dm, vals, NT)
                    inner = jnp.sum(weights * grad, axis=-1, keepdims=True)
                    grad_scores = (weights * (grad - inner)).astype(BF)
                    context = plus(context, dot(low_weights, vals * mask))
                    dq = plus(dq, dot(grad_scores, keys * mask))
                    dk = plus(dk, dot(grad_scores, qm, TN))
                    dv = plus(dv, dot(low_weights, dm, TN))
                c_s[rows, lanes] = context.astype(BF)
                dp_s[0, rows, lanes] = turn(
                    dq * HEAD_DIM ** (-0.5), cos_s[rows, :], low_s[rows, :], high_s[rows, :], -1
                ).astype(BF)
                if i > 0:
                    past = pl.ds(0, begin)
                    dk_s[past, :] += dk[:begin]
                    dv_s[past, :] += dv[:begin]
                dk_s[rows, :] = dk[begin:]
                dv_s[rows, :] = dv[begin:]
            dp_s[1, :, lanes] = turn(dk_s[...], cos_s[...], low_s[...], high_s[...], -1).astype(BF)
            dp_s[2, :, lanes] = dv_s[...].astype(BF)
            return carry

        lax.fori_loop(0, width // LANES, pair, 0)

        ga = dot(c_s[...], dz_s[...], TN)
        for p in range(parts):
            grads[s, place(p), 3] = ga[p * wp : (p + 1) * wp].astype(BF)
        for j in range(3):
            gb = LOWRANK_SCALE * dot(dp_s[j], z_s[:, pl.ds(j * RANK, RANK)], TN)
            for p in range(parts):
                grads[s, place(p), j] = gb[p * wp : (p + 1) * wp].astype(BF)

        if carried:

            @pl.when(first_shard)
            def _():
                for copy in acc_in:
                    copy.wait()

        for block in range(full // big):
            rows = pl.ds(block * big, big)

            def put(ref, where, value):
                ref[where] = ref[where] + value if carried else value

            cb = c_s[rows, :]
            put(acc_o, (rows, slice(None)), dot(cb, wo_s[slot]))
            put(acc_z, (rows, slice(None)), dot(cb, a_s[slot]))
            du = None
            for j in range(3):
                grad = dp_s[j, rows, :]
                term = dot(grad, wq_s[slot, j], NT)
                du = term if du is None else du + term
                put(acc_dz, (rows, pl.ds(j * RANK, RANK)), dot(grad, b_s[slot, j], NT))
            put(acc_u, (rows, slice(None)), du)

            @pl.when(last_shard)
            def _():
                for copy in out_copies(block):
                    copy.start()

    def body(s, carry):
        for k in range(shards):

            @pl.when(s == k)
            def _():
                for copy in weight_copies(k):
                    copy.wait()
                if k + 1 < shards:
                    for copy in weight_copies(k + 1):
                        copy.start()

        one_shard(s, lax.rem(s, 2), s == 0, s == shards - 1)
        return carry

    lax.fori_loop(0, shards, body, 0)
    for block in range(full // big):
        for copy in out_copies(block):
            copy.wait()


def attention(length, core, acts, tables, sources, acc, own, width, parts):
    u1, z, g, dz = acts
    full, depth = u1.shape
    shards = 1 if own else len(sources)
    flat = list(sources) if own else [part for source in sources for part in source]
    wp = width // parts
    copies = 4 if own else (7 + depth // wp) * parts
    slots = min(2, shards)
    acc_shapes = [
        jax.ShapeDtypeStruct((full, depth), F32),
        jax.ShapeDtypeStruct((full, depth), F32),
        jax.ShapeDtypeStruct((full, RANK), F32),
        jax.ShapeDtypeStruct((full, 3 * RANK), F32),
    ]
    carried = acc is not None
    operands = [length, core, u1, z, g, dz, *tables, *flat, *(acc or ())]
    first_acc = len(operands) - 4
    return pl.pallas_call(
        partial(attention_kernel, (own, shards, carried, width, depth, full, parts)),
        out_shape=(*acc_shapes, jax.ShapeDtypeStruct((shards, parts, 4, wp, RANK), BF)),
        in_specs=[SMEM, SMEM] + [ANY] * (len(operands) - 2),
        out_specs=(ANY, ANY, ANY, ANY, VMEM),
        input_output_aliases={first_acc + i: i for i in range(4)} if carried else {},
        scratch_shapes=[
            pltpu.VMEM((full, depth), BF),
            pltpu.VMEM((full, 3 * RANK), BF),
            pltpu.VMEM((full, depth), BF),
            pltpu.VMEM((full, RANK), BF),
            pltpu.VMEM((full, LANES), F32),
            pltpu.VMEM((full, LANES), F32),
            pltpu.VMEM((full, LANES), F32),
            pltpu.VMEM((slots, 3, depth, width), BF),
            pltpu.VMEM((slots, width, depth), BF),
            pltpu.VMEM((slots, 3, RANK, width), BF),
            pltpu.VMEM((slots, width, RANK), BF),
            pltpu.VMEM((full, depth), F32),
            pltpu.VMEM((full, depth), F32),
            pltpu.VMEM((full, RANK), F32),
            pltpu.VMEM((full, 3 * RANK), F32),
            pltpu.VMEM((full, width), BF),
            pltpu.VMEM((full, width), BF),
            pltpu.VMEM((full, width), BF),
            pltpu.VMEM((full, width), BF),
            pltpu.VMEM((full, width), BF),
            pltpu.VMEM((3, full, width), BF),
            pltpu.VMEM((full, LANES), F32),
            pltpu.VMEM((full, LANES), F32),
            pltpu.SemaphoreType.DMA((7,)),
            pltpu.SemaphoreType.DMA((slots, copies)),
            pltpu.SemaphoreType.DMA((4,)),
            pltpu.SemaphoreType.DMA((full // 512, 4)),
        ],
        compiler_params=params(),
        cost_estimate=cost(24 * shards, 8 << 20),
        name="attention",
    )(*operands)


def gelu_pair(x):
    size = jnp.abs(x)
    t = 1.0 / (1.0 + (0.3275911 * 2.0**-0.5) * size)
    poly = 1.061405429 * t - 1.453152027
    poly = poly * t + 1.421413741
    poly = poly * t - 0.284496736
    poly = (poly * t + 0.254829592) * t
    bell = jnp.exp(-0.5 * x * x)
    tail = 0.5 * poly * bell
    below = jnp.where(x >= 0.0, 1.0 - tail, tail)
    return x * below, below + x * bell * (2.0 * np.pi) ** -0.5


def mlp_kernel(cfg, *refs):
    own, shards, carried, hidden, depth, full, parts = cfg
    fp = hidden // parts
    it = iter(refs)
    take = lambda count: [next(it) for _ in range(count)]
    core_ref, u_h, z_h, g_h, dz_h = take(5)
    sources = take(4) if own else [take(parts) for _ in range(shards)]
    acc_h = take(4) if carried else None
    out_h = take(4)
    (grads,) = take(1)
    u_s, z_s, g_s, dz_s = take(4)
    wu_s, wd_s, b_s, a_s = take(4)
    acc_s = take(4)
    ga_s, gb_s = take(2)
    sem_in, sem_w, sem_acc, sem_out = take(4)
    acc_o, acc_u, acc_z, acc_dz = acc_s

    ins = [
        pltpu.make_async_copy(src, dst, sem_in.at[at])
        for at, (src, dst) in enumerate(
            zip(
                [u_h, z_h, g_h, dz_h],
                [u_s, z_s, g_s, dz_s],
            )
        )
    ]

    def weight_copies(shard):
        slot = shard % 2
        made = []

        def add(src, dst):
            made.append(pltpu.make_async_copy(src, dst, sem_w.at[slot, len(made)]))

        if own:
            for src, dst in zip(sources, (wu_s, wd_s, b_s, a_s)):
                add(src, dst.at[slot])
        else:
            for p in range(parts):
                ref = sources[shard][p]
                dst = pl.ds(p * fp, fp)
                add(ref.at[pl.ds(0, depth), :], wu_s.at[slot, :, dst])
                for m in range(depth // fp):
                    add(
                        ref.at[pl.ds(depth + m * fp, fp), :],
                        wd_s.at[slot, dst, pl.ds(m * fp, fp)],
                    )
                add(ref.at[pl.ds(2 * depth, RANK), :], b_s.at[slot, :, dst])
                for m in range(fp // RANK):
                    add(
                        ref.at[pl.ds(2 * depth + RANK, RANK), pl.ds(m * RANK, RANK)],
                        a_s.at[slot, pl.ds(p * fp + m * RANK, RANK), :],
                    )
        return made

    for copy in weight_copies(0):
        copy.start()
    for copy in ins:
        copy.start()
    if carried:
        acc_in = [
            pltpu.make_async_copy(src, dst, sem_acc.at[at])
            for at, (src, dst) in enumerate(zip(acc_h, acc_s))
            if src is not None
        ]
        for copy in acc_in:
            copy.start()
    elif shards > 1:
        for ref in acc_s:
            ref[...] = jnp.zeros_like(ref)
    for copy in ins:
        copy.wait()
    rows_in = 256
    chunk = min(512, hidden)

    def out_copies(block, dynamic=False):
        rows = rows_of(block, rows_in) if dynamic else pl.ds(block * rows_in, rows_in)
        return [
            pltpu.make_async_copy(src.at[rows, :], dst.at[rows, :], sem_out.at[block, at])
            for at, (src, dst) in enumerate(zip(acc_s, out_h))
        ]

    def place(p):
        if not own or parts == 1:
            return p
        return core_ref[0] if p == 0 else 1 - core_ref[0]

    def one_shard(s, slot, first_shard, last_shard):
        def block_step(block, carry):
            rows = rows_of(block, rows_in)
            ub, zb, gb, db = u_s[rows, :], z_s[rows, :], g_s[rows, :], dz_s[rows, :]
            out = du = zd = dz = None
            plus = lambda total, term: term if total is None else total + term
            for at in range(0, hidden, chunk):
                cols = pl.ds(at, chunk)
                linear = dot(ub, wu_s[slot, :, cols]) + dot(zb, b_s[slot, :, cols])
                grad = dot(gb, wd_s[slot, cols, :], NT) + dot(db, a_s[slot, cols, :], NT)
                active, slope = gelu_pair(linear)
                active = active.astype(BF)
                grad = (grad * slope).astype(BF)
                out = plus(out, dot(active, wd_s[slot, cols, :]))
                zd = plus(zd, dot(active, a_s[slot, cols, :]))
                du = plus(du, dot(grad, wu_s[slot, :, cols], NT))
                dz = plus(dz, dot(grad, b_s[slot, :, cols], NT))
                ga = dot(active, db, TN)
                gu = dot(grad, zb, TN)
                ga_s[cols, :] += ga
                gb_s[cols, :] += gu

            if carried:

                @pl.when(jnp.logical_and(first_shard, block == 0))
                def _():
                    for copy in acc_in:
                        copy.wait()

            def put(ref, value):
                ref[rows, :] = ref[rows, :] + value if carried or shards > 1 else value

            put(acc_o, out)
            put(acc_u, du)
            put(acc_z, zd)
            put(acc_dz, dz)

            @pl.when(last_shard)
            def _():
                for copy in out_copies(block, True):
                    copy.start()

            return carry

        ga_s[...] = jnp.zeros_like(ga_s)
        gb_s[...] = jnp.zeros_like(gb_s)
        lax.fori_loop(0, full // rows_in, block_step, 0)
        for p in range(parts):
            grads[s, place(p), 0] = ga_s[pl.ds(p * fp, fp), :].astype(BF)
            grads[s, place(p), 1] = (LOWRANK_SCALE * gb_s[pl.ds(p * fp, fp), :]).astype(BF)

    def body(s, carry):
        for k in range(shards):

            @pl.when(s == k)
            def _():
                for copy in weight_copies(k):
                    copy.wait()
                if k + 1 < shards:
                    for copy in weight_copies(k + 1):
                        copy.start()

        one_shard(s, lax.rem(s, 2), s == 0, s == shards - 1)
        return carry

    lax.fori_loop(0, shards, body, 0)
    for block in range(full // rows_in):
        for copy in out_copies(block):
            copy.wait()


def mlp(core, acts, sources, acc, own, hidden, parts):
    u2, z, g, dz = acts
    full, depth = u2.shape
    shards = 1 if own else len(sources)
    flat = list(sources) if own else [part for source in sources for part in source]
    fp = hidden // parts
    copies = 4 if own else (2 + depth // fp + fp // RANK) * parts
    slots = min(2, shards)
    carried = acc is not None
    operands = [core, u2, z, g, dz, *flat, *(acc or ())]
    first_acc = len(operands) - 4
    return pl.pallas_call(
        partial(mlp_kernel, (own, shards, carried, hidden, depth, full, parts)),
        out_shape=(
            jax.ShapeDtypeStruct((full, depth), F32),
            jax.ShapeDtypeStruct((full, depth), F32),
            jax.ShapeDtypeStruct((full, RANK), F32),
            jax.ShapeDtypeStruct((full, RANK), F32),
            jax.ShapeDtypeStruct((shards, parts, 2, fp, RANK), BF),
        ),
        in_specs=[SMEM] + [ANY] * (len(operands) - 1),
        out_specs=(ANY, ANY, ANY, ANY, VMEM),
        input_output_aliases={first_acc + i: i for i in range(4)} if carried else {},
        scratch_shapes=[
            pltpu.VMEM((full, depth), BF),
            pltpu.VMEM((full, RANK), BF),
            pltpu.VMEM((full, depth), BF),
            pltpu.VMEM((full, RANK), BF),
            pltpu.VMEM((slots, depth, hidden), BF),
            pltpu.VMEM((slots, hidden, depth), BF),
            pltpu.VMEM((slots, RANK, hidden), BF),
            pltpu.VMEM((slots, hidden, RANK), BF),
            pltpu.VMEM((full, depth), F32),
            pltpu.VMEM((full, depth), F32),
            pltpu.VMEM((full, RANK), F32),
            pltpu.VMEM((full, RANK), F32),
            pltpu.VMEM((hidden, RANK), F32),
            pltpu.VMEM((hidden, RANK), F32),
            pltpu.SemaphoreType.DMA((4,)),
            pltpu.SemaphoreType.DMA((slots, copies)),
            pltpu.SemaphoreType.DMA((4,)),
            pltpu.SemaphoreType.DMA((full // 256, 4)),
        ],
        compiler_params=params(),
        cost_estimate=cost(19 * shards, 8 << 20),
        name="mlp",
    )(*operands)


def latent_kernel(zsum, dzsum, u, g, zb, dzb, sums):
    depth = u.shape[1]
    low = zsum[...].astype(BF)
    zb[...] = low
    back = dzsum[...].astype(BF)
    dzb[...] = back
    many = back.shape[1] // RANK
    ga = dot(u[...], back, TN)
    for j in range(many):
        sums[pl.ds(j * depth, depth), :] = ga[:, j * RANK : (j + 1) * RANK].astype(sums.dtype)
    gb = LOWRANK_SCALE * dot(g[...], low, TN)
    sums[pl.ds(many * depth, depth), :] = gb.astype(sums.dtype)


def latent(zsum, dzsum, u, g, kept):
    full, depth = u.shape
    cols = dzsum.shape[1]
    return pl.pallas_call(
        latent_kernel,
        out_shape=(
            jax.ShapeDtypeStruct((full, RANK), BF),
            jax.ShapeDtypeStruct((full, cols), BF),
            jax.ShapeDtypeStruct((depth * (cols // RANK + 1), RANK), kept),
        ),
        in_specs=[VMEM] * 4,
        out_specs=(VMEM,) * 3,
        compiler_params=params(),
        cost_estimate=cost(4, 6 << 20),
        name="latent",
    )(zsum, dzsum, u, g)


def reduce_kernel(cfg, *refs):
    heads, planes, p_rows, q_rows = cfg
    hp, hq = sum(p_rows), sum(q_rows)
    p_sets = [refs[at * heads : (at + 1) * heads] for at in range(len(p_rows))]
    refs = refs[len(p_rows) * heads :]
    q_refs, refs = refs[: len(q_rows)], refs[len(q_rows) :]
    out_p, out_q = refs[:2]
    (
        keep_p, keep_q, send1, recv1, send2, recv2, sum2, send3, recv3, gather,
        s1, r1, s2, r2, s3, r3, s4, r4, s5, r5, s6, r6, s7, r7,
    ) = refs[2:]
    qp = hq // heads
    pz, qz = hp // planes, qp // planes
    dp, head = lax.axis_index("dp"), lax.axis_index("head")
    core, plane = lax.rem(dp, 2), lax.div(dp, 2)
    flip = lambda at, o: at + o - 2 * sum(
        (lax.rem(lax.div(at, 1 << k), 2) * (1 << k) for k in range(6) if o >> k & 1), 0
    )
    sibling = {"dp": plane * 2 + 1 - core}
    head_peer = lambda o: {"head": flip(head, o)}
    plane_peer = lambda o: {"dp": flip(plane, o) * 2 + core}
    peers = [sibling] + [head_peer(o) for o in range(1, heads)]
    peers += [plane_peer(o) for o in range(1, planes)]
    mesh_id = pl.DeviceIdType.MESH
    barrier = pltpu.get_barrier_semaphore()
    for peer in peers:
        pl.semaphore_signal(barrier, inc=1, device_id=peer, device_id_type=mesh_id)

    def send(src, dst, ssem, rsem, peer):
        copy = pltpu.make_async_remote_copy(
            src_ref=src, dst_ref=dst, send_sem=ssem, recv_sem=rsem,
            device_id=peer, device_id_type=mesh_id,
        )
        copy.start()
        return copy

    at = 0
    for rows, refs_p in zip(p_rows, p_sets):
        for slot in range(2):
            total = refs_p[0][slot].astype(F32)
            for ref in refs_p[1:]:
                total = total + ref[slot].astype(F32)
            if slot == 0:
                keep_p[pl.ds(at, rows), :] = total
            else:
                send1[pl.ds(at, rows), :] = total.astype(BF)
        at += rows
    at = 0
    for rows, ref in zip(q_rows, q_refs):
        send1[pl.ds(hp + at, rows), :] = ref[rows_of(1 - core, rows), :].astype(BF)
        keep_q[pl.ds(at, rows), :] = ref[rows_of(core, rows), :].astype(F32)
        at += rows
    pl.semaphore_wait(barrier, len(peers))
    copy = send(send1, recv1, s1, r1, sibling)
    copy.wait()
    total_q = keep_q[...] + recv1[pl.ds(hp, hq), :].astype(F32)
    keep_q[...] = total_q
    send2[...] = total_q.astype(BF)
    copies = [
        send(
            send2.at[rows_of(flip(head, o), qp), :], recv2.at[o - 1], s2.at[o - 1], r2.at[o - 1], head_peer(o)
        )
        for o in range(1, heads)
    ]
    total_p = keep_p[...] + recv1[pl.ds(0, hp), :].astype(F32)
    keep_p[...] = total_p
    for k in range(planes):
        send3[k, pl.ds(0, pz), :] = total_p[k * pz : (k + 1) * pz].astype(BF)
    for copy in copies:
        copy.wait()
    piece = keep_q[rows_of(head, qp), :]
    for o in range(1, heads):
        piece = piece + recv2[o - 1].astype(F32)
    sum2[...] = piece
    for k in range(planes):
        send3[k, pl.ds(pz, qz), :] = piece[k * qz : (k + 1) * qz].astype(BF)
    copies = [
        send(send3.at[flip(plane, o)], recv3.at[o - 1], s3.at[o - 1], r3.at[o - 1], plane_peer(o))
        for o in range(1, planes)
    ]
    for copy in copies:
        copy.wait()
    mine_p = keep_p[rows_of(plane, pz), :]
    mine_q = sum2[rows_of(plane, qz), :]
    for o in range(1, planes):
        mine_p = mine_p + recv3[o - 1, pl.ds(0, pz), :].astype(F32)
        mine_q = mine_q + recv3[o - 1, pl.ds(pz, qz), :].astype(F32)
    gather[plane, pl.ds(0, pz), :] = mine_p.astype(BF)
    gather[plane, pl.ds(pz, qz), :] = mine_q.astype(BF)
    copies = [
        send(gather.at[plane], gather.at[plane], s4.at[o - 1], r4.at[o - 1], plane_peer(o))
        for o in range(1, planes)
    ]
    for copy in copies:
        copy.wait()
    for k in range(planes):
        out_q[core, rows_of(head * planes + k, qz), :] = gather[k, pl.ds(pz, qz), :]
        out_p[core, pl.ds(k * pz, pz), :] = gather[k, pl.ds(0, pz), :]
    mine = rows_of(head, qp)
    copies = [
        send(out_q.at[core, mine, :], out_q.at[core, mine, :], s5.at[o - 1], r5.at[o - 1], head_peer(o))
        for o in range(1, heads)
    ]
    copies.append(send(out_p.at[core], out_p.at[core], s6, r6, sibling))
    for copy in copies:
        copy.wait()
    send(out_q.at[core], out_q.at[core], s7, r7, sibling).wait()


def reduce_all(p_sets, q_sets, heads, planes):
    p_rows = [p[0].shape[1] for p in p_sets]
    q_rows = [q.shape[0] // 2 for q in q_sets]
    hp, hq = sum(p_rows), sum(q_rows)
    qp = hq // heads
    pz, qz = hp // planes, qp // planes
    one = pltpu.SemaphoreType.DMA
    return pl.pallas_call(
        partial(reduce_kernel, (heads, planes, p_rows, q_rows)),
        out_shape=(
            jax.ShapeDtypeStruct((2, hp, RANK), BF),
            jax.ShapeDtypeStruct((2, hq, RANK), BF),
        ),
        in_specs=[VMEM] * (heads * len(p_sets) + len(q_sets)),
        out_specs=(VMEM, VMEM),
        scratch_shapes=[
            pltpu.VMEM((hp, RANK), F32),
            pltpu.VMEM((hq, RANK), F32),
            pltpu.VMEM((hp + hq, RANK), BF),
            pltpu.VMEM((hp + hq, RANK), BF),
            pltpu.VMEM((hq, RANK), BF),
            pltpu.VMEM((heads - 1, qp, RANK), BF),
            pltpu.VMEM((qp, RANK), F32),
            pltpu.VMEM((planes, pz + qz, RANK), BF),
            pltpu.VMEM((planes - 1, pz + qz, RANK), BF),
            pltpu.VMEM((planes, pz + qz, RANK), BF),
            one, one,
            one((heads - 1,)), one((heads - 1,)),
            one((planes - 1,)), one((planes - 1,)),
            one((planes - 1,)), one((planes - 1,)),
            one((heads - 1,)), one((heads - 1,)),
            one, one, one, one,
        ],
        compiler_params=pltpu.CompilerParams(
            collective_id=0, has_side_effects=True, vmem_limit_bytes=60 << 20
        ),
        name="reduce",
    )(*[array for p in p_sets for array in p], *q_sets)


def update_kernel(cfg, *refs):
    factors, merges, tensors, slots = cfg
    it = iter(refs)
    take = lambda count: [next(it) for _ in range(count)]
    count, wide = len(factors), max(slots) + 1
    (mask,) = take(1)
    grads = take(2)
    w_h, m_h = dict(zip(tensors, take(len(tensors)))), dict(zip(tensors, take(len(tensors))))
    resets = {t: next(it) for t in tensors if t[0] == "a"}
    frozen = take(wide)
    new_w, new_m = dict(zip(tensors, take(len(tensors)))), dict(zip(tensors, take(len(tensors))))
    out_c, out_l = take(wide), take(wide)
    w_s, m_s, n_s = take(count), take(count), take(count)
    r_s = {i: next(it) for i in range(count) if factors[i][0] == "a"}
    frozen_s, c_s, l_s = take(len(merges)), take(len(merges)), take(len(merges))
    sem_in, sem_out = take(2)
    loads, stores = [], []

    def load(src, dst):
        copy = pltpu.make_async_copy(src, dst, sem_in.at[len(loads)])
        copy.start()
        loads.append(copy)
        return copy

    def store(src, dst):
        copy = pltpu.make_async_copy(src, dst, sem_out.at[len(stores)])
        copy.start()
        stores.append(copy)

    pick = lambda ref, index: ref if index is None else ref.at[index]
    pick2 = lambda ref, k, index: ref.at[k] if index is None else ref.at[k, index]
    flag = mask[...].astype(F32)
    flag_col = jnp.broadcast_to(flag, (RANK, RANK)).T[:, :1]

    def load_factor(i):
        kind, tensor, index, _ = factors[i]
        mine = [load(pick(w_h[tensor], index), w_s[i])]
        mine += [load(pick2(m_h[tensor], k, index), m_s[i].at[k]) for k in range(2)]
        if kind == "a":
            mine.append(load(pick(resets[tensor], index), r_s[i]))
        return mine

    def step(i):
        kind, tensor, index, (source, spans) = factors[i]
        parts = [grads[source][pl.ds(at, size), :].astype(F32) for at, size in spans]
        grad = parts[0] if len(parts) == 1 else jnp.concatenate(parts, axis=0)
        if kind == "b":
            grad = grad.T
        keep = 1.0 - (flag if kind == "a" else flag_col)
        first = BETA_FIRST * m_s[i][0] + (1.0 - BETA_FIRST) * grad
        second = BETA_SECOND * m_s[i][1] + (1.0 - BETA_SECOND) * grad * grad
        scaled = first * (1.0 / (1.0 - BETA_FIRST**STEP))
        root = jnp.sqrt(second * (1.0 / (1.0 - BETA_SECOND**STEP)))
        weight = w_s[i][...]
        weight = weight - LEARN_RATE * (scaled / (root + ADAM_EPSILON) + WEIGHT_DECAY * weight)
        w_s[i][...] = weight
        m_s[i][0] = first * keep
        m_s[i][1] = second * keep
        for k in range(2):
            store(m_s[i].at[k], pick2(new_m[tensor], k, index))
        if kind == "a":
            n_s[i][...] = jnp.where(flag > 0.5, r_s[i][...].astype(F32), weight)
        else:
            n_s[i][...] = weight * keep
        store(n_s[i], pick(new_w[tensor], index))

    def split(value):
        high = value.astype(BF)
        return high, (value - high.astype(F32)).astype(BF)

    def merge(i):
        left, right, index = merges[i]
        right_high, right_low = split(w_s[right][...])
        right_all = jnp.concatenate([right_high, right_low, right_high], axis=0)
        total = w_s[left].shape[0]
        block = min(256, total)
        for at in range(0, total, block):
            rows = pl.ds(at, block)
            high, low = split(w_s[left][rows, :] * (LOWRANK_SCALE * flag))
            merged = frozen_s[i][rows, :].astype(F32) + dot(
                jnp.concatenate([high, high, low], axis=1), right_all
            )
            c_s[i][rows, :] = merged
            l_s[i][rows, :] = merged.astype(BF)
            store(c_s[i].at[rows, :], pick(out_c[slots[i]], index).at[rows, :])
            store(l_s[i].at[rows, :], pick(out_l[slots[i]], index).at[rows, :])

    waits = []
    for i, (left, right, index) in enumerate(merges):
        waits.append(load_factor(left) + load_factor(right))
        waits[-1].append(load(pick(frozen[slots[i]], index), frozen_s[i]))
    for i, (left, right, index) in enumerate(merges):
        for copy in waits[i]:
            copy.wait()
        step(left)
        step(right)
        merge(i)
    for copy in stores:
        copy.wait()


def update(mask, grads, factors, weights, merges, frozen):
    shape = jax.ShapeDtypeStruct
    tensors = sorted(weights)
    inner = lambda array, index: array.shape if index is None else array.shape[1:]
    shapes = [inner(weights[f[1]][0], f[2]) for f in factors]
    picked = [inner(w, m[2]) for m, w in zip(merges, frozen)]
    unique, slots = [], []
    for w in frozen:
        hit = [k for k, u in enumerate(unique) if u is w]
        if not hit:
            unique.append(w)
        slots.append(hit[0] if hit else len(unique) - 1)
    out_shape = [shape(weights[t][k].shape, F32) for k in range(2) for t in tensors]
    out_shape += [shape(u.shape, kind) for kind in (F32, BF) for u in unique]
    operands = [mask, *grads] + [weights[t][k] for k in range(2) for t in tensors]
    operands += [weights[t][2] for t in tensors if t[0] == "a"] + unique
    kinds = [f[0] for f in factors]
    scratch = [pltpu.VMEM(s, F32) for s in shapes]
    scratch += [pltpu.VMEM((2, *s), F32) for s in shapes]
    scratch += [pltpu.VMEM(s, F32) for s in shapes]
    scratch += [pltpu.VMEM(s, BF) for s, k in zip(shapes, kinds) if k == "a"]
    scratch += [pltpu.VMEM(s, kind) for kind in (BF, F32, BF) for s in picked]
    loads = 3 * len(factors) + kinds.count("a") + len(frozen)
    stores = 3 * len(factors) + sum(2 * (-(-s[0] // 256)) for s in picked)
    scratch += [pltpu.SemaphoreType.DMA((loads,)), pltpu.SemaphoreType.DMA((stores,))]
    return pl.pallas_call(
        partial(update_kernel, (factors, merges, tensors, slots)),
        out_shape=out_shape,
        in_specs=[VMEM, VMEM, VMEM] + [ANY] * (len(operands) - 3),
        out_specs=[ANY] * len(out_shape),
        scratch_shapes=scratch,
        compiler_params=params(),
        cost_estimate=cost(18, 60 << 20),
        name="update",
    )(*operands)


def finish_kernel(
    x, g, gain, a1, a2, b1, b2, attn, branch, du1, du2, zo, zd, dzq, dzu, layer_out, grad_in
):
    rows = x[...].astype(F32)
    side = dot(zo[...], b1[...]) + dot(zd[...], b2[...])
    layer_out[...] = rows + attn[...] + branch[...] + side
    one = (du1[...] + dot(dzq[...], a1[...], NT)) * gain[0:1, :]
    two = (du2[...] + dot(dzu[...], a2[...], NT)) * gain[1:2, :]
    centred, scale = norm_stats(rows)
    hat = centred * scale
    both = one + two
    mean = jnp.mean(both, axis=-1, keepdims=True)
    match = jnp.mean(both * hat, axis=-1, keepdims=True)
    grad_in[...] = g[...].astype(F32) + scale * (both - mean - hat * match)


def finish(x, g, gain, a1, a2, b1, b2, attn, branch, du1, du2, zo, zd, dzq, dzu):
    full, depth = x.shape
    rows = 256
    blk = lambda array: pl.BlockSpec((rows, array.shape[1]), lambda i: (i, 0))
    const = lambda array: pl.BlockSpec(array.shape, lambda i: (0, 0))
    return pl.pallas_call(
        finish_kernel,
        grid=(full // rows,),
        out_shape=(jax.ShapeDtypeStruct((full, depth), F32),) * 2,
        in_specs=[
            blk(x), blk(g), const(gain), const(a1), const(a2), const(b1), const(b2), blk(attn), blk(branch),
            blk(du1), blk(du2), blk(zo), blk(zd), blk(dzq), blk(dzu),
        ],
        out_specs=(pl.BlockSpec((rows, depth), lambda i: (i, 0)),) * 2,
        compiler_params=params(),
        cost_estimate=cost(9, 30 << 20),
        name="finish",
    )(x, g, gain, a1, a2, b1, b2, attn, branch, du1, du2, zo, zd, dzq, dzu)


def rotary_tables(full):
    half = ROT_DIM // 2
    frequency = np.float32(ROPE_BASE) ** (-2.0 * np.arange(half, dtype=np.float32) / ROT_DIM)
    angles = np.arange(full, dtype=np.float32)[:, None] * frequency.astype(np.float32)[None, :]
    cosine = np.ones((full, HEAD_DIM), np.float32)
    low = np.zeros((full, HEAD_DIM), np.float32)
    high = np.zeros((full, HEAD_DIM), np.float32)
    cosine[:, :half] = cosine[:, half:ROT_DIM] = np.cos(angles)
    low[:, :half] = -np.sin(angles)
    high[:, half:ROT_DIM] = np.sin(angles)
    return tuple(jnp.asarray(np.tile(t, (1, LANES // HEAD_DIM))) for t in (cosine, low, high))


def per_device(
    layer_input_rows,
    lengths,
    cotangent,
    frozen_projection_weight,
    frozen_outproj_weight,
    frozen_up_weight,
    frozen_down_weight,
    frozen_norm_gain,
    frozen_norm_bias,
    shared_input_factors,
    outproj_input_factor,
    down_input_factor,
    projection_output_factors,
    up_output_factor,
    output_side_factors,
    input_factor_moments,
    outproj_input_factor_moments,
    down_input_factor_moments,
    projection_output_factor_moments,
    up_output_factor_moments,
    outproj_output_factor_moments,
    reset_input_factor,
    reset_outproj_input_factor,
    reset_down_input_factor,
    component_merge_mask,
):
    full, depth = layer_input_rows.shape[1:]
    x, cot = layer_input_rows[0], cotangent[0]
    width, hidden = frozen_outproj_weight.shape[0], frozen_down_weight.shape[0]
    heads, groups = lax.axis_size("head"), lax.axis_size("dp")
    parts = 2 if width % (2 * LANES) == 0 else 1
    place = lax.axis_index("head")
    core = lax.rem(lax.axis_index("dp"), 2)
    core_at = (core if parts == 2 else jnp.zeros_like(core)).reshape(1).astype(jnp.int32)
    length = lax.dynamic_slice_in_dim(lengths, place, 1)
    tables = rotary_tables(full)

    def over_head(value, offset):
        return lax.ppermute(value, "head", [(i, i ^ offset) for i in range(heads)])

    def over_core(value):
        return lax.ppermute(value, "dp", [(i, i ^ 1) for i in range(groups)])

    def relay(by_x, by_y):
        sent = jnp.where(core == 0, by_y, by_x)
        pairs = [
            (d * heads + h, d * heads + (h ^ (1 if d % 2 == 0 else 2)))
            for d in range(groups)
            for h in range(heads)
        ]
        return lax.ppermute(sent, ("dp", "head"), pairs)

    def both(value):
        return [value, over_core(value)] if parts == 2 else [value]

    pa, b4q, aob = pack(
        "attn", core_at, frozen_projection_weight, frozen_outproj_weight, projection_output_factors,
        outproj_input_factor, parts,
    )
    got_a = {o: over_head(pa, o) for o in (1, 2)}
    u1, z1, dz1, acat1, bcat1, g = prologue(
        0, length, x, cot, frozen_norm_gain, frozen_norm_bias, shared_input_factors, output_side_factors
    )
    acts1 = (u1, z1, g, dz1)
    pm, b4up, adb = pack(
        "mlp", core_at, frozen_up_weight, frozen_down_weight, up_output_factor, down_input_factor, parts
    )
    *acc_a, grads_a0 = attention(
        length, core_at, acts1, tables,
        (frozen_projection_weight, frozen_outproj_weight, b4q, aob), None, True, width, parts,
    )
    got_a[1], got_a[2], g_after, grads_a0 = lax.optimization_barrier(
        (got_a[1], got_a[2], g, grads_a0)
    )
    if heads == 4 and parts == 2:
        got_a[3] = relay(got_a[1], got_a[2])
    else:
        for o in range(3, heads):
            got_a[o] = over_head(pa, o)
    pairs_a = {o: both(got_a[o]) for o in (1, 2)}
    u2, z2, dz2, acat2, bcat2 = prologue(
        1, length, x, g_after, frozen_norm_gain, frozen_norm_bias, shared_input_factors, output_side_factors
    )
    acts2 = (u2, z2, g, dz2)
    acc_a[2], _ = lax.optimization_barrier((acc_a[2], dz2))
    grads_a = {0: grads_a0[0]}
    for o in range(1, heads):
        if o >= 2 and o + 1 < heads:
            got_a[o + 1], pm, acc_a[2] = lax.optimization_barrier((got_a[o + 1], pm, acc_a[2]))
            pairs_a[o + 1] = both(got_a[o + 1])
        if o == 2:
            got_m = {o: over_head(pm, o) for o in (1, 2)}
        *acc_a, grad = attention(
            length, core_at, acts1, tables, [pairs_a[o]], acc_a, False, width, parts
        )
        grads_a[o] = grad[0]
    got_m[1], got_m[2], acc_a[2] = lax.optimization_barrier((got_m[1], got_m[2], acc_a[2]))
    pairs_m = {o: both(got_m[o]) for o in (1, 2)}
    attn, du1, zo, dzq = acc_a
    zo_low, dzq_low, q_attn = latent(zo, dzq, u1, g, BF)
    acts2 = lax.optimization_barrier((acts2, zo_low))[0]
    if heads == 4 and parts == 2:
        got_m[3] = relay(got_m[1], got_m[2])
    else:
        for o in range(3, heads):
            got_m[o] = over_head(pm, o)
    acc_m, grads_m = None, {}
    for o in range(1, heads):
        if o >= 2 and o + 1 < heads:
            got_m[o + 1], acc_m[2] = lax.optimization_barrier((got_m[o + 1], acc_m[2]))
            pairs_m[o + 1] = both(got_m[o + 1])
        *acc_m, grad = mlp(core_at, acts2, [pairs_m[o]], acc_m, False, hidden, parts)
        grads_m[o] = grad[0]
    *acc_m, grad = mlp(
        core_at, acts2, (frozen_up_weight, frozen_down_weight, b4up, adb), acc_m, True, hidden, parts,
    )
    grads_m[0] = grad[0]
    branch, du2, zd, dzu = acc_m
    zd_low, dzu_low, q_mlp = latent(zd, dzu, u2, g, F32)
    layer_out, grad_in = finish(
        x, g, frozen_norm_gain, acat1, acat2, bcat1, bcat2, attn, branch, du1, du2, zo_low, zd_low, dzq_low, dzu_low
    )

    def gather(grads):
        flat = {o: grad.reshape(grad.shape[0], -1, RANK) for o, grad in grads.items()}
        return flat[0], [over_head(flat[o], o) for o in range(1, heads)]

    def over_groups(own, rest):
        total = own.astype(F32)
        for other in rest:
            total = total + other.astype(F32)
        if parts == 2:
            total = jnp.where(core == 0, total, total[::-1])
        return lax.psum(total.astype(BF), "dp")

    set_a = gather(grads_a)
    set_m = gather(grads_m)
    planes = groups // 2
    wp, fp = width // parts, hidden // parts
    rows_a, rows_m = 4 * wp, 2 * fp
    if parts == 2 and (q_attn.shape[0] + q_mlp.shape[0]) // (2 * heads * planes) % 16 == 0:
        p_all, q_all = reduce_all(
            [[set_a[0], *set_a[1]], [set_m[0], *set_m[1]]], [q_attn, q_mlp], heads, planes
        )
    else:
        p_all = jnp.concatenate([over_groups(*set_a), over_groups(*set_m)], axis=1)
        q_all = jnp.stack(
            [
                jnp.concatenate([q_attn[: 2 * depth], q_mlp[:depth]]),
                jnp.concatenate([q_attn[2 * depth :], q_mlp[depth:]]),
            ]
        )
        q_all = lax.psum(q_all, ("dp", "head"))
    p_rows, q_rows = rows_a + rows_m, 3 * depth
    mask = component_merge_mask.reshape(1, RANK)
    from_a = lambda k: (0, tuple((p * p_rows + k * wp, wp) for p in range(parts)))
    from_m = lambda k: (0, tuple((p * p_rows + rows_a + k * fp, fp) for p in range(parts)))
    from_q = lambda half, k: (1, ((half * q_rows + k * depth, depth),))
    factors = (
        ("a", "a_in", 0, from_q(0, 0)),
        ("b", "b_qkv", 0, from_a(0)),
        ("a", "a_in", 1, from_q(0, 1)),
        ("b", "b_qkv", 1, from_a(1)),
        ("a", "a_in", 2, from_q(1, 0)),
        ("b", "b_qkv", 2, from_a(2)),
        ("a", "a_out", None, from_a(3)),
        ("b", "b_out", 0, from_q(1, 1)),
        ("a", "a_in", 3, from_q(0, 2)),
        ("b", "b_up", None, from_m(1)),
        ("a", "a_down", None, from_m(0)),
        ("b", "b_out", 1, from_q(1, 2)),
    )
    weights = {
        "a_in": (shared_input_factors, input_factor_moments, reset_input_factor),
        "a_out": (outproj_input_factor, outproj_input_factor_moments, reset_outproj_input_factor),
        "a_down": (down_input_factor, down_input_factor_moments, reset_down_input_factor),
        "b_qkv": (projection_output_factors, projection_output_factor_moments, None),
        "b_up": (up_output_factor, up_output_factor_moments, None),
        "b_out": (output_side_factors, outproj_output_factor_moments, None),
    }
    (
        new_a_down, new_a_in, new_a_out, new_b_out, new_b_qkv, new_b_up,
        new_m_a_down, new_m_a_in, new_m_a_out, new_m_b_out, new_m_b_qkv, new_m_b_up,
        comb_qkv, comb_out, comb_up, comb_down, copy_qkv, copy_out, copy_up, copy_down,
    ) = update(
        mask, (p_all.reshape(-1, RANK), q_all.reshape(-1, RANK)), factors, weights,
        ((0, 1, 0), (2, 3, 1), (4, 5, 2), (6, 7, None), (8, 9, None), (10, 11, None)),
        (frozen_projection_weight,) * 3
        + (frozen_outproj_weight, frozen_up_weight, frozen_down_weight),
    )
    return (
        layer_out[None], grad_in[None],
        new_a_in, new_a_out, new_a_down, new_b_qkv, new_b_up, new_b_out,
        new_m_a_in, new_m_a_out, new_m_a_down, new_m_b_qkv, new_m_b_up, new_m_b_out,
        comb_qkv, comb_out, comb_up, comb_down, copy_qkv, copy_out, copy_up, copy_down,
    )


def solution(mesh):
    return jax.shard_map(
        per_device,
        mesh=mesh,
        in_specs=(
            P(("dp", "head"), None, None),
            P("dp"),
            P(("dp", "head"), None, None),
            P(None, None, "head"),
            P("head", None),
            P(None, "head"),
            P("head", None),
            P(),
            P(),
            P(),
            P("head", None),
            P("head", None),
            P(None, None, "head"),
            P(None, "head"),
            P(),
            P(),
            P(None, "head", None),
            P(None, "head", None),
            P(None, None, None, "head"),
            P(None, None, "head"),
            P(),
            P(),
            P("head", None),
            P("head", None),
            P(),
        ),
        out_specs=(
            P(("dp", "head"), None, None),
            P(("dp", "head"), None, None),
            P(),
            P("head", None),
            P("head", None),
            P(None, None, "head"),
            P(None, "head"),
            P(),
            P(),
            P(None, "head", None),
            P(None, "head", None),
            P(None, None, None, "head"),
            P(None, None, "head"),
            P(),
            P(None, None, "head"),
            P("head", None),
            P(None, "head"),
            P("head", None),
            P(None, None, "head"),
            P("head", None),
            P(None, "head"),
            P("head", None),
        ),
        check_vma=False,
    )
```

```python
from functools import partial

import jax
import jax.numpy as jnp
import numpy as np
from jax import lax
from jax.experimental import pallas as pl
from jax.experimental.pallas import tpu as pltpu
from jax.sharding import PartitionSpec as P

HEAD_DIM = 64
ROT_DIM = 16
STEP = 10
RANK = 128
LANES = 128
QROWS = 256


NORM_EPSILON = 1e-05
LOWRANK_SCALE = 0.25
LEARN_RATE = 0.15
BETA_FIRST = 0.9
BETA_SECOND = 0.999
WEIGHT_DECAY = 0.01
ADAM_EPSILON = 1e-08
ROPE_BASE = 10000.0

BF = jnp.bfloat16
F32 = jnp.float32
ANY = pl.BlockSpec(memory_space=pltpu.HBM)
VMEM = pl.BlockSpec(memory_space=pltpu.VMEM)
SMEM = pl.BlockSpec(memory_space=pltpu.SMEM)
NN = (((1,), (0,)), ((), ()))
NT = (((1,), (1,)), ((), ()))
TN = (((0,), (0,)), ((), ()))


def dot(left, right, dims=NN):
    return lax.dot_general(left, right, dims, preferred_element_type=F32)


def params(mib=60):
    return pltpu.CompilerParams(vmem_limit_bytes=mib * 1024 * 1024)


def cost(micros, nbytes):
    return pl.CostEstimate(flops=int(micros * 1.15e9), bytes_accessed=nbytes, transcendentals=0)


def rows_of(block, size):
    return pl.ds(pl.multiple_of(block * size, size), size)


def pack_kernel(kind, shape, core_ref, *refs):
    width, depth, parts = shape
    part = width // parts
    w1, w2, b, a, packed, b_low, a_low, w1_s, w2_s, load, sems = refs
    core = core_ref[0]
    loads = [
        pltpu.make_async_copy(src, dst, load.at[at])
        for at, (src, dst) in enumerate(((w1, w1_s), (w2, w2_s)))
    ]
    for copy in loads:
        copy.start()
    copies = []

    def start(src, dst):
        copy = pltpu.make_async_copy(src, dst, sems.at[len(copies)])
        copy.start()
        copies.append(copy)

    lanes = pl.ds(pl.multiple_of(core * part, part), part)
    b_low[...] = (b[...] * LOWRANK_SCALE).astype(BF)
    a_low[...] = a[...].astype(BF)
    many = 3 if kind == "attn" else 1
    loads[0].wait()
    for j in range(many):
        src = (w1_s.at[j], b_low.at[j]) if kind == "attn" else (w1_s, b_low)
        start(src[0].at[:, lanes], packed.at[pl.ds(j * depth, depth), :])
        start(src[1].at[:, lanes], packed.at[pl.ds((many + 1) * depth + j * RANK, RANK), :])
    at = (many + 1) * depth + many * RANK
    for m in range(part // RANK):
        start(
            a_low.at[pl.ds(pl.multiple_of(core * part + m * RANK, RANK), RANK), :],
            packed.at[pl.ds(at, RANK), pl.ds(m * RANK, RANK)],
        )
    loads[1].wait()
    for m in range(depth // part):
        start(w2_s.at[lanes, pl.ds(m * part, part)], packed.at[pl.ds(many * depth + m * part, part), :])
    for copy in copies:
        copy.wait()


def pack(kind, core, w1, w2, b, a, parts):
    depth, width = w1.shape[-2:]
    part = width // parts
    many = 3 if kind == "attn" else 1
    count = 2 * many + part // RANK + depth // part
    return pl.pallas_call(
        partial(pack_kernel, kind, (width, depth, parts)),
        out_shape=(
            jax.ShapeDtypeStruct(((many + 1) * depth + (many + 1) * RANK, part), BF),
            jax.ShapeDtypeStruct(b.shape, BF),
            jax.ShapeDtypeStruct(a.shape, BF),
        ),
        in_specs=[SMEM, ANY, ANY, VMEM, VMEM],
        out_specs=(ANY, VMEM, VMEM),
        scratch_shapes=[
            pltpu.VMEM(w1.shape, BF),
            pltpu.VMEM(w2.shape, BF),
            pltpu.SemaphoreType.DMA((2,)),
            pltpu.SemaphoreType.DMA((count,)),
        ],
        compiler_params=params(),
        cost_estimate=cost(3, 4 << 20),
        name="pack_" + kind,
    )(core, w1, w2, b, a)


def norm_stats(x):
    mean = jnp.mean(x, axis=-1, keepdims=True)
    centred = x - mean
    spread = jnp.mean(centred * centred, axis=-1, keepdims=True)
    return centred, lax.rsqrt(spread + NORM_EPSILON)


def prologue_kernel(which, length, x, cot, gain, bias, a_in, b_out, u, z, dz, acat, bcat, *g):
    step = pl.program_id(0)

    @pl.when(step == 0)
    def _():
        for j in range(a_in.shape[0]):
            acat[:, j * RANK : (j + 1) * RANK] = a_in[j].astype(BF)
        bcat[...] = (b_out[0] * LOWRANK_SCALE).astype(BF)

    rows = x.shape[0]
    centred, scale = norm_stats(x[...].astype(F32))
    low = (centred * scale * gain[which : which + 1, :] + bias[which : which + 1, :]).astype(BF)
    u[...] = low
    z[...] = dot(low, acat[...]).astype(BF)
    if g:
        place = step * rows + lax.broadcasted_iota(jnp.int32, (rows, 1), 0)
        live = (place < length[0]).astype(F32)
        grad = (cot[...].astype(F32) * live).astype(BF)
        g[0][...] = grad
    else:
        grad = cot[...]
    dz[...] = dot(grad, bcat[...], NT).astype(BF)


def prologue(which, length, x, cot, gain, bias, a_in, b_out):
    full, depth = x.shape
    rows = 256
    many = 3 if which == 0 else 1
    blk = lambda cols: pl.BlockSpec((rows, cols), lambda i: (i, 0))
    const = lambda shape: pl.BlockSpec(shape, lambda i: (0,) * len(shape))
    shape = jax.ShapeDtypeStruct
    out_shape = [
        shape((full, depth), BF),
        shape((full, many * RANK), BF),
        shape((full, RANK), BF),
        shape((depth, many * RANK), BF),
        shape((RANK, depth), BF),
    ]
    out_specs = [blk(depth), blk(many * RANK), blk(RANK), const((depth, many * RANK)), const((RANK, depth))]
    if which == 0:
        out_shape.append(shape((full, depth), BF))
        out_specs.append(blk(depth))
    return pl.pallas_call(
        partial(prologue_kernel, which),
        grid=(full // rows,),
        out_shape=out_shape,
        in_specs=[
            SMEM, blk(depth), blk(depth), const(gain.shape), const(bias.shape),
            pl.BlockSpec((many, depth, RANK), lambda i: (which, 0, 0) if which == 0 else (3, 0, 0)),
            pl.BlockSpec((1, RANK, depth), lambda i: (which, 0, 0)),
        ],
        out_specs=out_specs,
        compiler_params=params(),
        cost_estimate=cost(4, 12 << 20),
        name=("prologue_attn", "prologue_mlp")[which],
    )(length, x, cot, gain, bias, a_in, b_out)


def turn(x, cosine, sine, sign):
    lower = lax.rem(lax.broadcasted_iota(jnp.int32, (1, LANES), 1), HEAD_DIM) < ROT_DIM // 2
    done = []
    for at in range(0, x.shape[1], LANES):
        part = x[:, at : at + LANES]
        other = jnp.where(
            lower, pltpu.roll(part, LANES - ROT_DIM // 2, 1), pltpu.roll(part, ROT_DIM // 2, 1)
        )
        shifted = other * sine
        done.append(part * cosine + shifted if sign > 0 else part * cosine - shifted)
    return done[0] if len(done) == 1 else jnp.concatenate(done, axis=1)


def weight_copies(source, own, dsts, add, depth, wp):
    wq_s, b_s, wo_s, a_s = dsts
    width = wo_s.shape[0]
    if own:
        w1, w2, b1, a1 = source
        for j in range(3):
            add(w1.at[j], wq_s.at[:, pl.ds(j * width, width)])
            add(b1.at[j], b_s.at[:, pl.ds(j * width, width)])
        add(w2, wo_s)
        add(a1, a_s)
        return 6
    for p, ref in enumerate(source):
        for j in range(3):
            dst = pl.ds(j * width + p * wp, wp)
            add(ref.at[pl.ds(j * depth, depth), :], wq_s.at[:, dst])
            add(ref.at[pl.ds(4 * depth + j * RANK, RANK), :], b_s.at[:, dst])
    for p, ref in enumerate(source):
        dst = pl.ds(p * wp, wp)
        for m in range(depth // wp):
            add(ref.at[pl.ds(3 * depth + m * wp, wp), :], wo_s.at[dst, pl.ds(m * wp, wp)])
        add(ref.at[pl.ds(4 * depth + 3 * RANK, wp), :], a_s.at[dst, :])
    return 6 * len(source)


def weight_count(own, parts, depth, wp):
    return 8 if own else (7 + depth // wp) * parts


def weight_space(depth, width):
    return [
        pltpu.VMEM((depth, 3 * width), BF),
        pltpu.VMEM((RANK, 3 * width), BF),
        pltpu.VMEM((width, depth), BF),
        pltpu.VMEM((width, RANK), BF),
    ]


def attention_kernel(cfg, *refs):
    own, others, width, depth, full, parts = cfg
    final = others > 0
    wp = width // parts
    it = iter(refs)
    take = lambda count: [next(it) for _ in range(count)]
    length, core_ref, u_h, z_h, g_h, dz_h, cos_h, sin_h = take(8)
    source = take(4 if own else parts)
    if final:
        gain, acat, bcat = take(3)
        other_sources = [take(4 if s == 0 else parts) for s in range(others)]
        made_h = [take(2) for _ in range(others)]
        out_h, e_h, sums, grads = take(4)
    else:
        c_out, dp_out, grads = take(3)
    u_s, z_s, g_s, dz_s, cos_s, sin_s = take(6)
    mine_s = take(4)
    wq_s, b_s, wo_s, a_s = mine_s
    q_s, k_s, v_s, dc_s, c_s, dp_s, dk_s, dv_s = take(8)
    if final:
        weights_s = [take(4) for _ in range(others)]
        made_s = [take(2) for _ in range(others)]
        out_s, e_s, sums_s = take(3)
        sem_o = take(1)[0]
    sem_in, sem_w, sem_out = take(3)
    big, size = 512, 256
    ins = []

    def fetch(src, dst):
        ins.append(pltpu.make_async_copy(src, dst, sem_in.at[len(ins)]))

    for src, dst in ((z_h, z_s), (cos_h, cos_s), (sin_h, sin_s)):
        fetch(src, dst)
    for block in range(full // big):
        rows = pl.ds(block * big, big)
        fetch(u_h.at[rows, :], u_s.at[rows, :])
    for src, dst in ((g_h, g_s), (dz_h, dz_s)):
        fetch(src, dst)
    made = []

    def add(src, dst):
        made.append(pltpu.make_async_copy(src, dst, sem_w.at[len(made)]))

    early = weight_copies(source, own, mine_s, add, depth, wp)
    for copy in made[:early] + ins[:4]:
        copy.start()
    key_place = lax.broadcasted_iota(jnp.int32, (1, full), 1)
    key_bias = jnp.where(key_place < length[0], 0.0, -1e30).astype(F32)
    lane_place = lax.broadcasted_iota(jnp.int32, (1, LANES), 1)
    masks = [
        (lane_place // HEAD_DIM == h).astype(F32).astype(BF) for h in range(LANES // HEAD_DIM)
    ]
    causal = lax.broadcasted_iota(jnp.int32, (QROWS, QROWS), 1) <= lax.broadcasted_iota(
        jnp.int32, (QROWS, QROWS), 0
    )
    for copy in made[:early] + ins[:4]:
        copy.wait()
    for copy in ins[4:] + made[early:]:
        copy.start()

    def place(p):
        if not own or parts == 1:
            return p
        return core_ref[0] if p == 0 else 1 - core_ref[0]

    for block in range(full // big):
        rows = pl.ds(block * big, big)
        if block > 0:
            ins[3 + block].wait()
        ub = u_s[rows, :]
        cosine, sine = cos_s[rows, :], sin_s[rows, :]
        for j, dst in enumerate((q_s, k_s, v_s)):
            lanes = pl.ds(j * width, width)
            value = dot(ub, wq_s[:, lanes]) + dot(z_s[rows, pl.ds(j * RANK, RANK)], b_s[:, lanes])
            if j < 2:
                value = turn(value, cosine, sine, 1)
            if j == 0:
                value = value * HEAD_DIM ** (-0.5)
            dst[rows, :] = value.astype(BF)
    for copy in ins[3 + full // big :] + made[early:]:
        copy.wait()
    if final:
        other_made = []
        for s in range(others):
            mine = []

            def add_other(src, dst):
                mine.append(pltpu.make_async_copy(src, dst, sem_o.at[s, len(mine)]))

            for src, dst in zip(made_h[s], made_s[s]):
                add_other(src, dst)
            weight_copies(other_sources[s], s == 0, weights_s[s], add_other, depth, wp)
            for copy in mine:
                copy.start()
            other_made += mine

    def project_back(block, carry):
        rows = rows_of(block, big)
        dc_s[rows, :] = (
            dot(g_s[rows, :], wo_s[...], NT) + dot(dz_s[rows, :], a_s[...], NT)
        ).astype(BF)
        return carry

    lax.fori_loop(0, full // big, project_back, 0)

    def pair(at, carry):
        lanes = pl.ds(pl.multiple_of(at * LANES, LANES), LANES)
        for i in range(full // QROWS):
            begin, end = i * QROWS, (i + 1) * QROWS
            rows = pl.ds(begin, QROWS)
            qb, db = q_s[rows, lanes], dc_s[rows, lanes]
            keys, vals = k_s[pl.ds(0, end), lanes], v_s[pl.ds(0, end), lanes]
            context = dq = dk = dv = None
            plus = lambda total, term: term if total is None else total + term
            for mask in masks:
                qm, dm = qb * mask, db * mask
                scores = dot(qm, keys, NT) + key_bias[:, :end]
                diag = jnp.where(causal, scores[:, begin:], -1e30)
                scores = diag if i == 0 else jnp.concatenate([scores[:, :begin], diag], axis=1)
                peak = jnp.max(scores, axis=-1, keepdims=True)
                raised = jnp.exp(scores - peak)
                total = jnp.sum(raised, axis=-1, keepdims=True)
                weights = raised * (1.0 / total)
                low_weights = weights.astype(BF)
                grad = dot(dm, vals, NT)
                inner = jnp.sum(weights * grad, axis=-1, keepdims=True)
                grad_scores = (weights * (grad - inner)).astype(BF)
                context = plus(context, dot(low_weights, vals * mask))
                dq = plus(dq, dot(grad_scores, keys * mask))
                dk = plus(dk, dot(grad_scores, qm, TN))
                dv = plus(dv, dot(low_weights, dm, TN))
            c_s[rows, lanes] = context.astype(BF)
            dp_s[rows, lanes] = turn(
                dq * HEAD_DIM ** (-0.5), cos_s[rows, :], sin_s[rows, :], -1
            ).astype(BF)
            if i > 0:
                past = pl.ds(0, begin)
                dk_s[past, :] += dk[:begin]
                dv_s[past, :] += dv[:begin]
            dk_s[rows, :] = dk[begin:]
            dv_s[rows, :] = dv[begin:]
        dp_s[:, pl.ds(pl.multiple_of(width + at * LANES, LANES), LANES)] = turn(dk_s[...], cos_s[...], sin_s[...], -1).astype(BF)
        dp_s[:, pl.ds(pl.multiple_of(2 * width + at * LANES, LANES), LANES)] = dv_s[...].astype(BF)
        return carry

    lax.fori_loop(0, width // LANES, pair, 0)
    outs = []
    if not final:
        outs = [
            pltpu.make_async_copy(c_s, c_out, sem_out.at[0, 0]),
            pltpu.make_async_copy(dp_s, dp_out, sem_out.at[0, 1]),
        ]
        for copy in outs:
            copy.start()
    ga = dot(c_s[...], dz_s[...], TN)
    for p in range(parts):
        grads[place(p), 3] = ga[p * wp : (p + 1) * wp].astype(BF)
    for j in range(3):
        gb = LOWRANK_SCALE * dot(
            dp_s[:, pl.ds(j * width, width)], z_s[:, pl.ds(j * RANK, RANK)], TN
        )
        for p in range(parts):
            grads[place(p), j] = gb[p * wp : (p + 1) * wp].astype(BF)
    if final:
        for copy in other_made:
            copy.wait()
        everything = [(c_s, dp_s, mine_s)] + [(*made_s[s], weights_s[s]) for s in range(others)]
        plus = lambda total, term: term if total is None else total + term
        for block in range(full // size):
            rows = pl.ds(block * size, size)
            out = du = zo = None
            dz = [None] * 3
            for cs, ds, (wq, b, wo, a) in everything:
                cb = cs[rows, :]
                out = plus(out, dot(cb, wo[...]))
                zo = plus(zo, dot(cb, a[...]))
                du = plus(du, dot(ds[rows, :], wq[...], NT))
                for j in range(3):
                    lanes = pl.ds(j * width, width)
                    dz[j] = plus(dz[j], dot(ds[rows, lanes], b[:, lanes], NT))
            zo = zo.astype(BF)
            dz = jnp.concatenate(dz, axis=1).astype(BF)
            out_s[rows, :] = out + dot(zo, bcat[...])
            e_s[rows, :] = (du + dot(dz, acat[...], NT)) * gain[0:1, :]
            ga = dot(u_s[rows, :], dz, TN)
            gb = dot(g_s[rows, :], zo, TN)
            for j in range(4):
                where = pl.ds(j * depth, depth)
                term = gb if j == 3 else ga[:, j * RANK : (j + 1) * RANK]
                sums_s[where, :] = term if block == 0 else sums_s[where, :] + term
            for at, (src, dst) in enumerate(((out_s, out_h), (e_s, e_h))):
                outs.append(
                    pltpu.make_async_copy(src.at[rows, :], dst.at[rows, :], sem_out.at[block, at])
                )
                outs[-1].start()
        first = pl.ds(0, 3 * depth)
        sums[first, :] = sums_s[first, :].astype(sums.dtype)
        last = pl.ds(3 * depth, depth)
        sums[last, :] = (LOWRANK_SCALE * sums_s[last, :]).astype(sums.dtype)
    for copy in outs:
        copy.wait()


def attention(length, core, acts, tables, source, own, last, width, parts):
    u1, z, g, dz = acts
    full, depth = u1.shape
    wp = width // parts
    operands = [length, core, u1, z, g, dz, *tables, *source]
    shape, vmem = jax.ShapeDtypeStruct, pltpu.VMEM
    grads = shape((parts, 4, wp, RANK), BF)
    in_specs = [SMEM, SMEM] + [ANY] * (len(operands) - 2)
    scratch = [
        vmem((full, depth), BF), vmem((full, 3 * RANK), BF), vmem((full, depth), BF),
        vmem((full, RANK), BF), vmem((full, LANES), F32), vmem((full, LANES), F32),
        *weight_space(depth, width),
        *[vmem((full, width), BF)] * 5,
        vmem((full, 3 * width), BF), vmem((full, LANES), F32), vmem((full, LANES), F32),
    ]
    if last is None:
        others = 0
        out_shape = (shape((full, width), BF), shape((full, 3 * width), BF), grads)
        out_specs = (ANY, ANY, VMEM)
    else:
        side, sources, made = last
        others = len(sources)
        more = [r for s in sources for r in s] + [m for two in made for m in two]
        operands += [*side, *more]
        in_specs += [VMEM] * 3 + [ANY] * len(more)
        out_shape = (
            shape((full, depth), F32), shape((full, depth), F32), shape((4 * depth, RANK), BF), grads,
        )
        out_specs = (ANY, ANY, VMEM, VMEM)
        for _ in range(others):
            scratch += weight_space(depth, width)
        for _ in range(others):
            scratch += [vmem((full, width), BF), vmem((full, 3 * width), BF)]
        scratch += [vmem((full, depth), F32), vmem((full, depth), F32), vmem((4 * depth, RANK), F32)]
        copies = 2 + max(8, weight_count(False, parts, depth, wp))
        scratch.append(pltpu.SemaphoreType.DMA((others, copies)))
    scratch += [
        pltpu.SemaphoreType.DMA((5 + full // 512,)),
        pltpu.SemaphoreType.DMA((weight_count(own, parts, depth, wp),)),
        pltpu.SemaphoreType.DMA((full // 256, 2)),
    ]
    return pl.pallas_call(
        partial(attention_kernel, (own, others, width, depth, full, parts)),
        out_shape=out_shape,
        in_specs=in_specs,
        out_specs=out_specs,
        scratch_shapes=scratch,
        compiler_params=params(),
        cost_estimate=cost(18 if last is None else 36, 8 << 20),
        name="attention" if last is None else "attention_last",
    )(*operands)


def gelu_pair(x):
    size = jnp.abs(x)
    t = 1.0 / (1.0 + (0.3275911 * 2.0**-0.5) * size)
    poly = 1.061405429 * t - 1.453152027
    poly = poly * t + 1.421413741
    poly = poly * t - 0.284496736
    poly = (poly * t + 0.254829592) * t
    bell = jnp.exp(-0.5 * x * x)
    tail = 0.5 * poly * bell
    below = jnp.where(x >= 0.0, 1.0 - tail, tail)
    return x * below, below + x * bell * (2.0 * np.pi) ** -0.5


def mlp_kernel(cfg, *refs):
    kinds, carried, final, hidden, depth, full, parts = cfg
    fp, shards = hidden // parts, len(kinds)
    it = iter(refs)
    take = lambda count: [next(it) for _ in range(count)]
    core_ref, u_h, z_h, g_h, dz_h = take(5)
    sources = [take(4 if own else parts) for own in kinds]
    acc_h = take(4) if carried else None
    if final:
        x_h, attn_h, e_h, gain, acat, bcat = take(6)
    out_h = take(2 if final else 4)
    (grads,) = take(1)
    if final:
        (sums,) = take(1)
    u_s, z_s, g_s, dz_s = take(4)
    wu_s, wd_s, b_s, a_s = take(4)
    acc_s = take(4)
    ga_s, gb_s = take(2)
    if final:
        x_s, attn_s, e_s, sums_s = take(4)
    sem_in, sem_w, sem_acc, sem_out = take(4)
    acc_o, acc_u, acc_z, acc_dz = acc_s
    size = 256
    chunk = min(1024, hidden)
    blocks = full // size

    def copies_of(pairs, sems):
        return [pltpu.make_async_copy(src, dst, sems.at[at]) for at, (src, dst) in enumerate(pairs)]

    def begin(copies):
        for copy in copies:
            copy.start()

    def finish_copies(copies):
        for copy in copies:
            copy.wait()

    ins = copies_of(zip((u_h, z_h, g_h, dz_h), (u_s, z_s, g_s, dz_s)), sem_in)

    def weights(shard):
        slot = shard % 2
        made = []

        def add(src, dst):
            made.append(pltpu.make_async_copy(src, dst, sem_w.at[slot, len(made)]))

        if kinds[shard]:
            for src, dst in zip(sources[shard], (wu_s, wd_s, b_s, a_s)):
                add(src, dst.at[slot])
            return made
        for p, ref in enumerate(sources[shard]):
            dst = pl.ds(p * fp, fp)
            add(ref.at[pl.ds(0, depth), :], wu_s.at[slot, :, dst])
            for m in range(depth // fp):
                add(ref.at[pl.ds(depth + m * fp, fp), :], wd_s.at[slot, dst, pl.ds(m * fp, fp)])
            add(ref.at[pl.ds(2 * depth, RANK), :], b_s.at[slot, :, dst])
            for m in range(fp // RANK):
                add(
                    ref.at[pl.ds(2 * depth + RANK, RANK), pl.ds(m * RANK, RANK)],
                    a_s.at[slot, pl.ds(p * fp + m * RANK, RANK), :],
                )
        return made

    first = weights(0)
    half = len(first) // 2 if not kinds[0] and hidden == 2 * chunk and parts == 2 else len(first)
    begin([*ins, *first[:half]])
    loads, outs = [], []
    for block in range(blocks):
        rows = pl.ds(block * size, size)
        pairs = list(zip(acc_h, acc_s)) if carried else []
        if final:
            pairs += [(x_h, x_s), (attn_h, attn_s), (e_h, e_s)]
        loads.append(copies_of([(src.at[rows, :], dst.at[rows, :]) for src, dst in pairs], sem_acc.at[block]))
    finish_copies([*ins, *first[:half]])
    begin(first[half:])
    for copies in loads:
        begin(copies)
    plus = lambda total, term: term if total is None else total + term
    for s in range(shards):
        slot = s % 2
        if s > 0:
            finish_copies(weights(s))
        if s + 1 < shards:
            begin(weights(s + 1))
        ga_s[...] = jnp.zeros_like(ga_s)
        gb_s[...] = jnp.zeros_like(gb_s)

        def place(p):
            if not kinds[s] or parts == 1:
                return p
            return core_ref[0] if p == 0 else 1 - core_ref[0]

        pieces = hidden // chunk

        def expand(step):
            block, at = step // pieces, step % pieces * chunk
            if s == 0 and block == 0 and at == chunk:
                finish_copies(first[half:])
            rows, cols = pl.ds(block * size, size), pl.ds(at, chunk)
            linear = dot(u_s[rows, :], wu_s[slot, :, cols]) + dot(z_s[rows, :], b_s[slot, :, cols])
            grad = dot(g_s[rows, :], wd_s[slot, cols, :], NT) + dot(
                dz_s[rows, :], a_s[slot, cols, :], NT
            )
            return linear, grad

        ahead = expand(0)
        for step in range(blocks * pieces):
            block, at = step // pieces, step % pieces * chunk
            rows = pl.ds(block * size, size)
            ub, zb, gb, db = u_s[rows, :], z_s[rows, :], g_s[rows, :], dz_s[rows, :]
            linear, grad = ahead
            if step + 1 < blocks * pieces:
                ahead = expand(step + 1)
            if at == 0:
                out = du = zd = dz = None
            cols = pl.ds(at, chunk)
            active, slope = gelu_pair(linear)
            active = active.astype(BF)
            grad = (grad * slope).astype(BF)
            out = plus(out, dot(active, wd_s[slot, cols, :]))
            zd = plus(zd, dot(active, a_s[slot, cols, :]))
            du = plus(du, dot(grad, wu_s[slot, :, cols], NT))
            dz = plus(dz, dot(grad, b_s[slot, :, cols], NT))
            ga_s[cols, :] += dot(active, db, TN)
            gb_s[cols, :] += dot(grad, zb, TN)
            if at + chunk < hidden:
                continue
            if s == 0:
                finish_copies(loads[block])
            new = []
            for ref, value in zip(acc_s, (out, du, zd, dz)):
                new.append(ref[rows, :] + value if carried or s > 0 else value)
            if final and s == shards - 1:
                out, du, zd, dz = new
                zd, dz = zd.astype(BF), dz.astype(BF)
                x = x_s[rows, :].astype(F32)
                acc_o[rows, :] = x + attn_s[rows, :] + out + dot(zd, bcat[...])
                both = e_s[rows, :] + (du + dot(dz, acat[...], NT)) * gain[1:2, :]
                centred, scale = norm_stats(x)
                hat = centred * scale
                mean = jnp.mean(both, axis=-1, keepdims=True)
                match = jnp.mean(both * hat, axis=-1, keepdims=True)
                acc_u[rows, :] = gb.astype(F32) + scale * (both - mean - hat * match)
                for k, term in enumerate((dot(ub, dz, TN), dot(gb, zd, TN))):
                    where = pl.ds(k * depth, depth)
                    sums_s[where, :] = term if block == 0 else sums_s[where, :] + term
            else:
                for ref, value in zip(acc_s, new):
                    ref[rows, :] = value
            if s == shards - 1:
                outs.append(
                    copies_of(
                        [(src.at[rows, :], dst.at[rows, :]) for src, dst in zip(acc_s, out_h)],
                        sem_out.at[block],
                    )
                )
                begin(outs[-1])
        for p in range(parts):
            grads[s, place(p), 0] = ga_s[pl.ds(p * fp, fp), :].astype(BF)
            grads[s, place(p), 1] = (LOWRANK_SCALE * gb_s[pl.ds(p * fp, fp), :]).astype(BF)
    if final:
        sums[pl.ds(0, depth), :] = sums_s[pl.ds(0, depth), :].astype(sums.dtype)
        sums[pl.ds(depth, depth), :] = (LOWRANK_SCALE * sums_s[pl.ds(depth, depth), :]).astype(
            sums.dtype
        )
    for copies in outs:
        finish_copies(copies)


def mlp(core, acts, sources, kinds, acc, last, hidden, parts):
    u2, z, g, dz = acts
    full, depth = u2.shape
    shards, fp = len(kinds), hidden // parts
    flat = [part for source in sources for part in source]
    copies = max(4, (2 + depth // fp + fp // RANK) * parts)
    slots = min(2, shards)
    carried, final = acc is not None, last is not None
    operands = [core, u2, z, g, dz, *flat, *(acc or ()), *(last or ())]
    shape = jax.ShapeDtypeStruct
    first_acc = 5 + len(flat)
    out_shape = [shape((full, depth), F32), shape((full, depth), F32)]
    if not final:
        out_shape += [shape((full, RANK), F32), shape((full, RANK), F32)]
    out_specs = [ANY] * len(out_shape) + [VMEM] * (2 if final else 1)
    out_shape.append(shape((shards, parts, 2, fp, RANK), BF))
    if final:
        out_shape.append(shape((2 * depth, RANK), F32))
    in_specs = [SMEM] + [ANY] * (len(operands) - 1)
    if final:
        in_specs[-3:] = [VMEM] * 3
    scratch = [
        pltpu.VMEM((full, depth), BF),
        pltpu.VMEM((full, RANK), BF),
        pltpu.VMEM((full, depth), BF),
        pltpu.VMEM((full, RANK), BF),
        pltpu.VMEM((slots, depth, hidden), BF),
        pltpu.VMEM((slots, hidden, depth), BF),
        pltpu.VMEM((slots, RANK, hidden), BF),
        pltpu.VMEM((slots, hidden, RANK), BF),
        pltpu.VMEM((full, depth), F32),
        pltpu.VMEM((full, depth), F32),
        pltpu.VMEM((full, RANK), F32),
        pltpu.VMEM((full, RANK), F32),
        pltpu.VMEM((hidden, RANK), F32),
        pltpu.VMEM((hidden, RANK), F32),
    ]
    if final:
        scratch += [
            pltpu.VMEM((full, depth), BF),
            pltpu.VMEM((full, depth), F32),
            pltpu.VMEM((full, depth), F32),
            pltpu.VMEM((2 * depth, RANK), F32),
        ]
    scratch += [
        pltpu.SemaphoreType.DMA((4,)),
        pltpu.SemaphoreType.DMA((slots, copies)),
        pltpu.SemaphoreType.DMA((full // 256, 7)),
        pltpu.SemaphoreType.DMA((full // 256, 4)),
    ]
    aliases = {first_acc + i: i for i in range(4)} if carried and not final else {}
    return pl.pallas_call(
        partial(mlp_kernel, (kinds, carried, final, hidden, depth, full, parts)),
        out_shape=out_shape,
        in_specs=in_specs,
        out_specs=out_specs,
        input_output_aliases=aliases,
        scratch_shapes=scratch,
        compiler_params=params(),
        cost_estimate=cost(17 * shards, 8 << 20),
        name="mlp",
    )(*operands)


def reduce_kernel(cfg, *refs):
    heads, planes, sets = cfg
    it = iter(refs)
    take = lambda count: [next(it) for _ in range(count)]
    ins = [(take(heads), *take(1)) for _ in sets]
    outs = [take(2) for _ in sets]
    spaces = [take(24) for _ in sets]
    dp, head = lax.axis_index("dp"), lax.axis_index("head")
    core, plane = lax.rem(dp, 2), lax.div(dp, 2)
    flip = lambda at, o: at + o - 2 * sum(
        (lax.rem(lax.div(at, 1 << k), 2) * (1 << k) for k in range(6) if o >> k & 1), 0
    )
    sibling = {"dp": plane * 2 + 1 - core}
    head_peer = lambda o: {"head": flip(head, o)}
    plane_peer = lambda o: {"dp": flip(plane, o) * 2 + core}
    peers = [sibling] + [head_peer(o) for o in range(1, heads)]
    peers += [plane_peer(o) for o in range(1, planes)]
    mesh_id = pl.DeviceIdType.MESH
    barrier = pltpu.get_barrier_semaphore()
    for peer in peers:
        pl.semaphore_signal(barrier, inc=1, device_id=peer, device_id_type=mesh_id)

    def send(src, dst, ssem, rsem, peer):
        copy = pltpu.make_async_remote_copy(
            src_ref=src, dst_ref=dst, send_sem=ssem, recv_sem=rsem,
            device_id=peer, device_id_type=mesh_id,
        )
        copy.start()
        return copy

    def flow(rows, own, q, out_p, out_q, space):
        hp, hq = rows
        (
            keep_p, keep_q, send1, recv1, send2, recv2, sum2, send3, recv3, gather,
            s1, r1, s2, r2, s3, r3, s4, r4, s5, r5, s6, r6, s7, r7,
        ) = space
        qp = hq // heads
        pz, qz = hp // planes, qp // planes
        for slot in range(2):
            total = own[0][slot].astype(F32)
            for ref in own[1:]:
                total = total + ref[slot].astype(F32)
            if slot == 0:
                keep_p[...] = total
            else:
                send1[pl.ds(0, hp), :] = total.astype(BF)
        send1[pl.ds(hp, hq), :] = q[rows_of(1 - core, hq), :].astype(BF)
        keep_q[...] = q[rows_of(core, hq), :].astype(F32)
        yield
        copy = send(send1, recv1, s1, r1, sibling)
        yield
        copy.wait()
        total_q = keep_q[...] + recv1[pl.ds(hp, hq), :].astype(F32)
        keep_q[...] = total_q
        send2[...] = total_q.astype(BF)
        copies = [
            send(
                send2.at[rows_of(flip(head, o), qp), :], recv2.at[o - 1], s2.at[o - 1], r2.at[o - 1],
                head_peer(o),
            )
            for o in range(1, heads)
        ]
        total_p = keep_p[...] + recv1[pl.ds(0, hp), :].astype(F32)
        keep_p[...] = total_p
        for k in range(planes):
            send3[k, pl.ds(0, pz), :] = total_p[k * pz : (k + 1) * pz].astype(BF)
        yield
        for copy in copies:
            copy.wait()
        piece = keep_q[rows_of(head, qp), :]
        for o in range(1, heads):
            piece = piece + recv2[o - 1].astype(F32)
        sum2[...] = piece
        for k in range(planes):
            send3[k, pl.ds(pz, qz), :] = piece[k * qz : (k + 1) * qz].astype(BF)
        copies = [
            send(send3.at[flip(plane, o)], recv3.at[o - 1], s3.at[o - 1], r3.at[o - 1], plane_peer(o))
            for o in range(1, planes)
        ]
        yield
        for copy in copies:
            copy.wait()
        mine_p = keep_p[rows_of(plane, pz), :]
        mine_q = sum2[rows_of(plane, qz), :]
        for o in range(1, planes):
            mine_p = mine_p + recv3[o - 1, pl.ds(0, pz), :].astype(F32)
            mine_q = mine_q + recv3[o - 1, pl.ds(pz, qz), :].astype(F32)
        gather[plane, pl.ds(0, pz), :] = mine_p.astype(BF)
        gather[plane, pl.ds(pz, qz), :] = mine_q.astype(BF)
        copies = [
            send(gather.at[plane], gather.at[plane], s4.at[o - 1], r4.at[o - 1], plane_peer(o))
            for o in range(1, planes)
        ]
        yield
        for copy in copies:
            copy.wait()
        for k in range(planes):
            out_q[core, rows_of(head * planes + k, qz), :] = gather[k, pl.ds(pz, qz), :]
            out_p[core, pl.ds(k * pz, pz), :] = gather[k, pl.ds(0, pz), :]
        mine = rows_of(head, qp)
        copies = [
            send(out_q.at[core, mine, :], out_q.at[core, mine, :], s5.at[o - 1], r5.at[o - 1], head_peer(o))
            for o in range(1, heads)
        ]
        copies.append(send(out_p.at[core], out_p.at[core], s6, r6, sibling))
        yield
        for copy in copies:
            copy.wait()
        copy = send(out_q.at[core], out_q.at[core], s7, r7, sibling)
        yield
        copy.wait()

    flows = [
        flow(rows, *two, *out, space) for rows, two, out, space in zip(sets, ins, outs, spaces)
    ]
    for one in flows:
        next(one)
    pl.semaphore_wait(barrier, len(peers))
    done = object()
    while flows:
        flows = [one for one in flows if next(one, done) is not done]


def reduce_all(sets, heads, planes):
    one = pltpu.SemaphoreType.DMA
    shape, vmem = jax.ShapeDtypeStruct, pltpu.VMEM
    sizes, scratch, out_shape, operands = [], [], [], []
    for own, rest, q in sets:
        hp, hq = own.shape[1], q.shape[0] // 2
        qp = hq // heads
        pz, qz = hp // planes, qp // planes
        sizes.append((hp, hq))
        operands += [own, *rest, q]
        out_shape += [shape((2, hp, RANK), BF), shape((2, hq, RANK), BF)]
        scratch += [
            vmem((hp, RANK), F32), vmem((hq, RANK), F32),
            vmem((hp + hq, RANK), BF), vmem((hp + hq, RANK), BF),
            vmem((hq, RANK), BF), vmem((heads - 1, qp, RANK), BF), vmem((qp, RANK), F32),
            vmem((planes, pz + qz, RANK), BF), vmem((planes - 1, pz + qz, RANK), BF),
            vmem((planes, pz + qz, RANK), BF),
            one, one,
            one((heads - 1,)), one((heads - 1,)),
            one((planes - 1,)), one((planes - 1,)),
            one((planes - 1,)), one((planes - 1,)),
            one((heads - 1,)), one((heads - 1,)),
            one, one, one, one,
        ]
    return pl.pallas_call(
        partial(reduce_kernel, (heads, planes, sizes)),
        out_shape=out_shape,
        in_specs=[VMEM] * len(operands),
        out_specs=[VMEM] * len(out_shape),
        scratch_shapes=scratch,
        compiler_params=pltpu.CompilerParams(
            collective_id=0, has_side_effects=True, vmem_limit_bytes=60 << 20
        ),
        name="reduce",
    )(*operands)


def update_kernel(cfg, *refs):
    factors, merges, tensors, slots = cfg
    it = iter(refs)
    take = lambda count: [next(it) for _ in range(count)]
    count, wide = len(factors), max(slots) + 1
    (mask,) = take(1)
    grads = take(4)
    w_h, m_h = dict(zip(tensors, take(len(tensors)))), dict(zip(tensors, take(len(tensors))))
    resets = {t: next(it) for t in tensors if t[0] == "a"}
    frozen = take(wide)
    new_w, new_m = dict(zip(tensors, take(len(tensors)))), dict(zip(tensors, take(len(tensors))))
    out_c, out_l = take(wide), take(wide)
    w_s, m_s, n_s = take(count), take(count), take(count)
    r_s = {i: next(it) for i in range(count) if factors[i][0] == "a"}
    frozen_s, c_s, l_s = take(len(merges)), take(len(merges)), take(len(merges))
    sem_in, sem_out = take(2)
    loads, stores = [], []

    def load(src, dst):
        copy = pltpu.make_async_copy(src, dst, sem_in.at[len(loads)])
        copy.start()
        loads.append(copy)
        return copy

    def store(src, dst):
        copy = pltpu.make_async_copy(src, dst, sem_out.at[len(stores)])
        copy.start()
        stores.append(copy)

    pick = lambda ref, index: ref if index is None else ref.at[index]
    pick2 = lambda ref, k, index: ref.at[k] if index is None else ref.at[k, index]
    flag = mask[...].astype(F32)
    flag_col = jnp.broadcast_to(flag, (RANK, RANK)).T[:, :1]

    def load_factor(i):
        kind, tensor, index, _ = factors[i]
        mine = [load(pick(w_h[tensor], index), w_s[i])]
        mine += [load(pick2(m_h[tensor], k, index), m_s[i].at[k]) for k in range(2)]
        if kind == "a":
            mine.append(load(pick(resets[tensor], index), r_s[i]))
        return mine

    def step(i):
        kind, tensor, index, (source, spans) = factors[i]
        parts = [grads[source][pl.ds(at, size), :].astype(F32) for at, size in spans]
        grad = parts[0] if len(parts) == 1 else jnp.concatenate(parts, axis=0)
        if kind == "b":
            grad = grad.T
        keep = 1.0 - (flag if kind == "a" else flag_col)
        first = BETA_FIRST * m_s[i][0] + (1.0 - BETA_FIRST) * grad
        second = BETA_SECOND * m_s[i][1] + (1.0 - BETA_SECOND) * grad * grad
        scaled = first * (1.0 / (1.0 - BETA_FIRST**STEP))
        root = jnp.sqrt(second * (1.0 / (1.0 - BETA_SECOND**STEP)))
        weight = w_s[i][...]
        weight = weight - LEARN_RATE * (scaled / (root + ADAM_EPSILON) + WEIGHT_DECAY * weight)
        w_s[i][...] = weight
        m_s[i][0] = first * keep
        m_s[i][1] = second * keep
        for k in range(2):
            store(m_s[i].at[k], pick2(new_m[tensor], k, index))
        if kind == "a":
            n_s[i][...] = jnp.where(flag > 0.5, r_s[i][...].astype(F32), weight)
        else:
            n_s[i][...] = weight * keep
        store(n_s[i], pick(new_w[tensor], index))

    def split(value):
        high = value.astype(BF)
        return high, (value - high.astype(F32)).astype(BF)

    def merge(i):
        left, right, index = merges[i]
        right_high, right_low = split(w_s[right][...])
        right_all = jnp.concatenate([right_high, right_low, right_high], axis=0)
        total = w_s[left].shape[0]
        block = min(256, total)
        for at in range(0, total, block):
            rows = pl.ds(at, block)
            high, low = split(w_s[left][rows, :] * (LOWRANK_SCALE * flag))
            merged = frozen_s[i][rows, :].astype(F32) + dot(
                jnp.concatenate([high, high, low], axis=1), right_all
            )
            c_s[i][rows, :] = merged
            l_s[i][rows, :] = merged.astype(BF)
            store(c_s[i].at[rows, :], pick(out_c[slots[i]], index).at[rows, :])
            store(l_s[i].at[rows, :], pick(out_l[slots[i]], index).at[rows, :])

    waits = []
    for i, (left, right, index) in enumerate(merges):
        waits.append(load_factor(left) + load_factor(right))
        waits[-1].append(load(pick(frozen[slots[i]], index), frozen_s[i]))
    for i, (left, right, index) in enumerate(merges):
        for copy in waits[i]:
            copy.wait()
        step(left)
        step(right)
        merge(i)
    for copy in stores:
        copy.wait()


def update(mask, grads, factors, weights, merges, frozen):
    shape = jax.ShapeDtypeStruct
    tensors = sorted(weights)
    inner = lambda array, index: array.shape if index is None else array.shape[1:]
    shapes = [inner(weights[f[1]][0], f[2]) for f in factors]
    picked = [inner(w, m[2]) for m, w in zip(merges, frozen)]
    unique, slots = [], []
    for w in frozen:
        hit = [k for k, u in enumerate(unique) if u is w]
        if not hit:
            unique.append(w)
        slots.append(hit[0] if hit else len(unique) - 1)
    out_shape = [shape(weights[t][k].shape, F32) for k in range(2) for t in tensors]
    out_shape += [shape(u.shape, kind) for kind in (F32, BF) for u in unique]
    operands = [mask, *grads] + [weights[t][k] for k in range(2) for t in tensors]
    operands += [weights[t][2] for t in tensors if t[0] == "a"] + unique
    kinds = [f[0] for f in factors]
    scratch = [pltpu.VMEM(s, F32) for s in shapes]
    scratch += [pltpu.VMEM((2, *s), F32) for s in shapes]
    scratch += [pltpu.VMEM(s, F32) for s in shapes]
    scratch += [pltpu.VMEM(s, BF) for s, k in zip(shapes, kinds) if k == "a"]
    scratch += [pltpu.VMEM(s, kind) for kind in (BF, F32, BF) for s in picked]
    loads = 3 * len(factors) + kinds.count("a") + len(frozen)
    stores = 3 * len(factors) + sum(2 * (-(-s[0] // 256)) for s in picked)
    scratch += [pltpu.SemaphoreType.DMA((loads,)), pltpu.SemaphoreType.DMA((stores,))]
    return pl.pallas_call(
        partial(update_kernel, (factors, merges, tensors, slots)),
        out_shape=out_shape,
        in_specs=[VMEM] * 5 + [ANY] * (len(operands) - 5),
        out_specs=[ANY] * len(out_shape),
        scratch_shapes=scratch,
        compiler_params=params(),
        cost_estimate=cost(18, 60 << 20),
        name="update",
    )(*operands)


def rotary_tables(full):
    half = ROT_DIM // 2
    frequency = np.float32(ROPE_BASE) ** (-2.0 * np.arange(half, dtype=np.float32) / ROT_DIM)
    angles = np.arange(full, dtype=np.float32)[:, None] * frequency.astype(np.float32)[None, :]
    cosine = np.ones((full, HEAD_DIM), np.float32)
    sine = np.zeros((full, HEAD_DIM), np.float32)
    cosine[:, :half] = cosine[:, half:ROT_DIM] = np.cos(angles)
    sine[:, :half] = -np.sin(angles)
    sine[:, half:ROT_DIM] = np.sin(angles)
    return tuple(jnp.asarray(np.tile(t, (1, LANES // HEAD_DIM))) for t in (cosine, sine))


def per_device(
    layer_input_rows,
    lengths,
    cotangent,
    frozen_projection_weight,
    frozen_outproj_weight,
    frozen_up_weight,
    frozen_down_weight,
    frozen_norm_gain,
    frozen_norm_bias,
    shared_input_factors,
    outproj_input_factor,
    down_input_factor,
    projection_output_factors,
    up_output_factor,
    output_side_factors,
    input_factor_moments,
    outproj_input_factor_moments,
    down_input_factor_moments,
    projection_output_factor_moments,
    up_output_factor_moments,
    outproj_output_factor_moments,
    reset_input_factor,
    reset_outproj_input_factor,
    reset_down_input_factor,
    component_merge_mask,
):
    full, depth = layer_input_rows.shape[1:]
    x, cot = layer_input_rows[0], cotangent[0]
    width, hidden = frozen_outproj_weight.shape[0], frozen_down_weight.shape[0]
    heads, groups = lax.axis_size("head"), lax.axis_size("dp")
    parts = 2 if width % (2 * LANES) == 0 else 1
    place = lax.axis_index("head")
    core = lax.rem(lax.axis_index("dp"), 2)
    core_at = (core if parts == 2 else jnp.zeros_like(core)).reshape(1).astype(jnp.int32)
    length = lax.dynamic_slice_in_dim(lengths, place, 1)
    tables = rotary_tables(full)

    def over_head(value, offset):
        return lax.ppermute(value, "head", [(i, i ^ offset) for i in range(heads)])

    def over_core(value):
        return lax.ppermute(value, "dp", [(i, i ^ 1) for i in range(groups)])

    def relay(by_x, by_y):
        sent = jnp.where(core == 0, by_y, by_x)
        pairs = [
            (d * heads + h, d * heads + (h ^ (1 if d % 2 == 0 else 2)))
            for d in range(groups)
            for h in range(heads)
        ]
        return lax.ppermute(sent, ("dp", "head"), pairs)

    def both(value):
        return [value, over_core(value)] if parts == 2 else [value]

    pa, b4q, aob = pack(
        "attn", core_at, frozen_projection_weight, frozen_outproj_weight, projection_output_factors,
        outproj_input_factor, parts,
    )
    got_a = {o: over_head(pa, o) for o in (1, 2)}
    u1, z1, dz1, acat1, bcat1, g = prologue(
        0, length, x, cot, frozen_norm_gain, frozen_norm_bias, shared_input_factors, output_side_factors
    )
    acts1 = (u1, z1, g, dz1)
    own_a = (frozen_projection_weight, frozen_outproj_weight, b4q, aob)
    after = lax.optimization_barrier
    made, grads_a = {}, {}
    *made[0], grads_a[0] = attention(
        length, core_at, acts1, tables, own_a, True, None, width, parts
    )
    got_a[1], got_a[2], pm_in, grads_a[0] = after((got_a[1], got_a[2], frozen_up_weight, grads_a[0]))
    pm, b4up, adb = pack(
        "mlp", core_at, pm_in, frozen_down_weight, up_output_factor, down_input_factor, parts
    )
    own_m = (frozen_up_weight, frozen_down_weight, b4up, adb)
    pairs_a = {o: both(got_a[o]) for o in (1, 2)}
    acts1 = (u1, z1, g, after((dz1, pm))[0])
    if heads == 4 and parts == 2:
        got_a[3] = relay(got_a[1], got_a[2])
    else:
        for o in range(3, heads):
            got_a[o] = over_head(pa, o)
    got_m = {o: over_head(pm, o) for o in (1, 2)}
    g_in = g
    for o in range(1, heads):
        if o == 3:
            got_a[3], g_in = after((got_a[3], grads_a[2]))[0], after((g, grads_a[2]))[0]
            pairs_a[3] = both(got_a[3])
        elif o > 3:
            pairs_a[o] = both(got_a[o])
        if o == min(3, heads - 1):
            u2, z2, dz2, acat2, bcat2 = prologue(
                1, length, x, g_in, frozen_norm_gain, frozen_norm_bias, shared_input_factors,
                output_side_factors,
            )
            acts1 = (u1, z1, g, after((acts1[3], dz2))[0])
        pairs_a[o][0] = after((pairs_a[o][0], grads_a[o - 1]))[0]
        last = None
        if o == heads - 1:
            last = (
                (frozen_norm_gain, acat1, bcat1),
                [own_a] + [pairs_a[k] for k in range(1, o)],
                [made[k] for k in range(o)],
            )
        *made[o], grads_a[o] = attention(
            length, core_at, acts1, tables, pairs_a[o], False, last, width, parts
        )
    attn, e_one, q_attn = made[heads - 1]
    got_m[1], got_m[2], z2 = after((got_m[1], got_m[2], after((z2, q_attn))[0]))
    acts2 = (u2, z2, g, dz2)
    pairs_m = {o: both(got_m[o]) for o in (1, 2)}
    if heads == 4 and parts == 2:
        got_m[3] = relay(got_m[1], got_m[2])
    else:
        for o in range(3, heads):
            got_m[o] = over_head(pm, o)
    grads_m = {}
    *acc_m, grad = mlp(
        core_at, acts2, [pairs_m[1], pairs_m[2]], (False, False), None, None, hidden, parts
    )
    grads_m[1], grads_m[2] = grad[0], grad[1]
    for o in range(3, heads):
        got_m[o], acc_m[2] = after((got_m[o], acc_m[2]))
        *acc_m, grad = mlp(core_at, acts2, [both(got_m[o])], (False,), acc_m, None, hidden, parts)
        grads_m[o] = grad[0]
    layer_out, grad_in, grad, q_mlp = mlp(
        core_at, acts2, [own_m], (True,), acc_m, (x, attn, e_one, frozen_norm_gain, acat2, bcat2),
        hidden, parts,
    )
    grads_m[0] = grad[0]

    def gather(grads):
        flat = {o: grad.reshape(grad.shape[0], -1, RANK) for o, grad in grads.items()}
        return flat[0], [over_head(flat[o], o) for o in range(1, heads)]

    def over_head_sum(own, rest):
        total = own.astype(F32)
        for other in rest:
            total = total + other.astype(F32)
        if parts == 2:
            total = jnp.where(core == 0, total, total[::-1])
        return total.astype(BF)

    set_a = gather(grads_a)
    set_m = gather(grads_m)
    planes = groups // 2
    wp, fp = width // parts, hidden // parts
    rows_a, rows_m = 4 * wp, 2 * fp
    pieces = 2 * heads * planes
    if parts == 2 and q_attn.shape[0] // pieces % 16 == 0 and q_mlp.shape[0] // pieces % 16 == 0:
        p_attn, q_attn, p_mlp, q_mlp = reduce_all(
            [(*set_a, q_attn), (*set_m, q_mlp)], heads, planes
        )
    else:
        p_attn = lax.psum(over_head_sum(*set_a), "dp")
        p_mlp = lax.psum(over_head_sum(*set_m), "dp")
        q_attn, q_mlp = lax.psum((q_attn, q_mlp.astype(BF)), ("dp", "head"))
    mask = component_merge_mask.reshape(1, RANK)
    from_a = lambda k: (0, tuple((p * rows_a + k * wp, wp) for p in range(parts)))
    from_m = lambda k: (2, tuple((p * rows_m + k * fp, fp) for p in range(parts)))
    from_q = lambda half, k: (1, (((2 * half + k) * depth, depth),))
    from_r = lambda k: (3, ((k * depth, depth),))
    factors = (
        ("a", "a_in", 0, from_q(0, 0)),
        ("b", "b_qkv", 0, from_a(0)),
        ("a", "a_in", 1, from_q(0, 1)),
        ("b", "b_qkv", 1, from_a(1)),
        ("a", "a_in", 2, from_q(1, 0)),
        ("b", "b_qkv", 2, from_a(2)),
        ("a", "a_out", None, from_a(3)),
        ("b", "b_out", 0, from_q(1, 1)),
        ("a", "a_in", 3, from_r(0)),
        ("b", "b_up", None, from_m(1)),
        ("a", "a_down", None, from_m(0)),
        ("b", "b_out", 1, from_r(1)),
    )
    weights = {
        "a_in": (shared_input_factors, input_factor_moments, reset_input_factor),
        "a_out": (outproj_input_factor, outproj_input_factor_moments, reset_outproj_input_factor),
        "a_down": (down_input_factor, down_input_factor_moments, reset_down_input_factor),
        "b_qkv": (projection_output_factors, projection_output_factor_moments, None),
        "b_up": (up_output_factor, up_output_factor_moments, None),
        "b_out": (output_side_factors, outproj_output_factor_moments, None),
    }
    (
        new_a_down, new_a_in, new_a_out, new_b_out, new_b_qkv, new_b_up,
        new_m_a_down, new_m_a_in, new_m_a_out, new_m_b_out, new_m_b_qkv, new_m_b_up,
        comb_qkv, comb_out, comb_up, comb_down, copy_qkv, copy_out, copy_up, copy_down,
    ) = update(
        mask, [v.reshape(-1, RANK) for v in (p_attn, q_attn, p_mlp, q_mlp)], factors, weights,
        ((0, 1, 0), (2, 3, 1), (4, 5, 2), (6, 7, None), (8, 9, None), (10, 11, None)),
        (frozen_projection_weight,) * 3
        + (frozen_outproj_weight, frozen_up_weight, frozen_down_weight),
    )
    return (
        layer_out[None], grad_in[None],
        new_a_in, new_a_out, new_a_down, new_b_qkv, new_b_up, new_b_out,
        new_m_a_in, new_m_a_out, new_m_a_down, new_m_b_qkv, new_m_b_up, new_m_b_out,
        comb_qkv, comb_out, comb_up, comb_down, copy_qkv, copy_out, copy_up, copy_down,
    )


def solution(mesh):
    return jax.shard_map(
        per_device,
        mesh=mesh,
        in_specs=(
            P(("dp", "head"), None, None),
            P("dp"),
            P(("dp", "head"), None, None),
            P(None, None, "head"),
            P("head", None),
            P(None, "head"),
            P("head", None),
            P(),
            P(),
            P(),
            P("head", None),
            P("head", None),
            P(None, None, "head"),
            P(None, "head"),
            P(),
            P(),
            P(None, "head", None),
            P(None, "head", None),
            P(None, None, None, "head"),
            P(None, None, "head"),
            P(),
            P(),
            P("head", None),
            P("head", None),
            P(),
        ),
        out_specs=(
            P(("dp", "head"), None, None),
            P(("dp", "head"), None, None),
            P(),
            P("head", None),
            P("head", None),
            P(None, None, "head"),
            P(None, "head"),
            P(),
            P(),
            P(None, "head", None),
            P(None, "head", None),
            P(None, None, None, "head"),
            P(None, None, "head"),
            P(),
            P(None, None, "head"),
            P("head", None),
            P(None, "head"),
            P("head", None),
            P(None, None, "head"),
            P("head", None),
            P(None, "head"),
            P("head", None),
        ),
        check_vma=False,
    )
```

```python
from functools import partial

import jax
import jax.numpy as jnp
import numpy as np
from jax import lax
from jax.experimental import pallas as pl
from jax.experimental.pallas import tpu as pltpu
from jax.sharding import PartitionSpec as P

HEAD_DIM = 64
ROT_DIM = 16
STEP = 10
RANK = 128
LANES = 128
QROWS = 256


NORM_EPSILON = 1e-05
LOWRANK_SCALE = 0.25
LEARN_RATE = 0.15
BETA_FIRST = 0.9
BETA_SECOND = 0.999
WEIGHT_DECAY = 0.01
ADAM_EPSILON = 1e-08
ROPE_BASE = 10000.0

BF = jnp.bfloat16
F32 = jnp.float32
ANY = pl.BlockSpec(memory_space=pltpu.HBM)
VMEM = pl.BlockSpec(memory_space=pltpu.VMEM)
SMEM = pl.BlockSpec(memory_space=pltpu.SMEM)
NN = (((1,), (0,)), ((), ()))
NT = (((1,), (1,)), ((), ()))
TN = (((0,), (0,)), ((), ()))


def dot(left, right, dims=NN):
    return lax.dot_general(left, right, dims, preferred_element_type=F32)


def params(mib=60):
    return pltpu.CompilerParams(vmem_limit_bytes=mib * 1024 * 1024)


def cost(micros, nbytes):
    return pl.CostEstimate(flops=int(micros * 1.15e9), bytes_accessed=nbytes, transcendentals=0)


def rows_of(block, size):
    return pl.ds(pl.multiple_of(block * size, size), size)


def pack_kernel(kind, shape, core_ref, *refs):
    width, depth, parts = shape
    part = width // parts
    w1, w2, b, a, packed, b_low, a_low, w1_s, w2_s, load, sems = refs
    core = core_ref[0]
    loads = [
        pltpu.make_async_copy(src, dst, load.at[at])
        for at, (src, dst) in enumerate(((w1, w1_s), (w2, w2_s)))
    ]
    for copy in loads:
        copy.start()
    copies = []

    def start(src, dst):
        copy = pltpu.make_async_copy(src, dst, sems.at[len(copies)])
        copy.start()
        copies.append(copy)

    lanes = pl.ds(pl.multiple_of(core * part, part), part)
    b_low[...] = (b[...] * LOWRANK_SCALE).astype(BF)
    a_low[...] = a[...].astype(BF)
    many = 3 if kind == "attn" else 1
    loads[0].wait()
    for j in range(many):
        src = (w1_s.at[j], b_low.at[j]) if kind == "attn" else (w1_s, b_low)
        start(src[0].at[:, lanes], packed.at[pl.ds(j * depth, depth), :])
        start(src[1].at[:, lanes], packed.at[pl.ds((many + 1) * depth + j * RANK, RANK), :])
    at = (many + 1) * depth + many * RANK
    for m in range(part // RANK):
        start(
            a_low.at[pl.ds(pl.multiple_of(core * part + m * RANK, RANK), RANK), :],
            packed.at[pl.ds(at, RANK), pl.ds(m * RANK, RANK)],
        )
    loads[1].wait()
    for m in range(depth // part):
        start(w2_s.at[lanes, pl.ds(m * part, part)], packed.at[pl.ds(many * depth + m * part, part), :])
    for copy in copies:
        copy.wait()


def pack(kind, core, w1, w2, b, a, parts):
    depth, width = w1.shape[-2:]
    part = width // parts
    many = 3 if kind == "attn" else 1
    count = 2 * many + part // RANK + depth // part
    return pl.pallas_call(
        partial(pack_kernel, kind, (width, depth, parts)),
        out_shape=(
            jax.ShapeDtypeStruct(((many + 1) * depth + (many + 1) * RANK, part), BF),
            jax.ShapeDtypeStruct(b.shape, BF),
            jax.ShapeDtypeStruct(a.shape, BF),
        ),
        in_specs=[SMEM, ANY, ANY, VMEM, VMEM],
        out_specs=(ANY, VMEM, VMEM),
        scratch_shapes=[
            pltpu.VMEM(w1.shape, BF),
            pltpu.VMEM(w2.shape, BF),
            pltpu.SemaphoreType.DMA((2,)),
            pltpu.SemaphoreType.DMA((count,)),
        ],
        compiler_params=params(),
        cost_estimate=cost(3, 4 << 20),
        name="pack_" + kind,
    )(core, w1, w2, b, a)


def norm_stats(x):
    mean = jnp.mean(x, axis=-1, keepdims=True)
    centred = x - mean
    spread = jnp.mean(centred * centred, axis=-1, keepdims=True)
    return centred, lax.rsqrt(spread + NORM_EPSILON)


def prologue_kernel(which, length, x, cot, gain, bias, a_in, b_out, u, z, dz, acat, bcat, *g):
    step = pl.program_id(0)

    @pl.when(step == 0)
    def _():
        for j in range(a_in.shape[0]):
            acat[:, j * RANK : (j + 1) * RANK] = a_in[j].astype(BF)
        bcat[...] = (b_out[0] * LOWRANK_SCALE).astype(BF)

    rows = x.shape[0]
    centred, scale = norm_stats(x[...].astype(F32))
    low = (centred * scale * gain[which : which + 1, :] + bias[which : which + 1, :]).astype(BF)
    u[...] = low
    z[...] = dot(low, acat[...]).astype(BF)
    if g:
        place = step * rows + lax.broadcasted_iota(jnp.int32, (rows, 1), 0)
        live = (place < length[0]).astype(F32)
        grad = (cot[...].astype(F32) * live).astype(BF)
        g[0][...] = grad
    else:
        grad = cot[...]
    dz[...] = dot(grad, bcat[...], NT).astype(BF)


def prologue(which, length, x, cot, gain, bias, a_in, b_out):
    full, depth = x.shape
    rows = 256
    many = 3 if which == 0 else 1
    blk = lambda cols: pl.BlockSpec((rows, cols), lambda i: (i, 0))
    const = lambda shape: pl.BlockSpec(shape, lambda i: (0,) * len(shape))
    shape = jax.ShapeDtypeStruct
    out_shape = [
        shape((full, depth), BF),
        shape((full, many * RANK), BF),
        shape((full, RANK), BF),
        shape((depth, many * RANK), BF),
        shape((RANK, depth), BF),
    ]
    out_specs = [blk(depth), blk(many * RANK), blk(RANK), const((depth, many * RANK)), const((RANK, depth))]
    if which == 0:
        out_shape.append(shape((full, depth), BF))
        out_specs.append(blk(depth))
    return pl.pallas_call(
        partial(prologue_kernel, which),
        grid=(full // rows,),
        out_shape=out_shape,
        in_specs=[
            SMEM, blk(depth), blk(depth), const(gain.shape), const(bias.shape),
            pl.BlockSpec((many, depth, RANK), lambda i: (which, 0, 0) if which == 0 else (3, 0, 0)),
            pl.BlockSpec((1, RANK, depth), lambda i: (which, 0, 0)),
        ],
        out_specs=out_specs,
        compiler_params=params(),
        cost_estimate=cost(4, 12 << 20),
        name=("prologue_attn", "prologue_mlp")[which],
    )(length, x, cot, gain, bias, a_in, b_out)


def turn(x, cosine, sine, sign):
    lower = lax.rem(lax.broadcasted_iota(jnp.int32, (1, LANES), 1), HEAD_DIM) < ROT_DIM // 2
    done = []
    for at in range(0, x.shape[1], LANES):
        part = x[:, at : at + LANES]
        other = jnp.where(
            lower, pltpu.roll(part, LANES - ROT_DIM // 2, 1), pltpu.roll(part, ROT_DIM // 2, 1)
        )
        shifted = other * sine
        done.append(part * cosine + shifted if sign > 0 else part * cosine - shifted)
    return done[0] if len(done) == 1 else jnp.concatenate(done, axis=1)


def weight_copies(source, own, dsts, add, depth, wp):
    wq_s, b_s, wo_s, a_s = dsts
    width = wo_s.shape[0]
    if own:
        w1, w2, b1, a1 = source
        for j in range(3):
            add(w1.at[j], wq_s.at[:, pl.ds(j * width, width)])
            add(b1.at[j], b_s.at[:, pl.ds(j * width, width)])
        add(w2, wo_s)
        add(a1, a_s)
        return 6
    for p, ref in enumerate(source):
        for j in range(3):
            dst = pl.ds(j * width + p * wp, wp)
            add(ref.at[pl.ds(j * depth, depth), :], wq_s.at[:, dst])
            add(ref.at[pl.ds(4 * depth + j * RANK, RANK), :], b_s.at[:, dst])
    for p, ref in enumerate(source):
        dst = pl.ds(p * wp, wp)
        for m in range(depth // wp):
            add(ref.at[pl.ds(3 * depth + m * wp, wp), :], wo_s.at[dst, pl.ds(m * wp, wp)])
        add(ref.at[pl.ds(4 * depth + 3 * RANK, wp), :], a_s.at[dst, :])
    return 6 * len(source)


def weight_count(own, parts, depth, wp):
    return 8 if own else (7 + depth // wp) * parts


def weight_space(depth, width):
    return [
        pltpu.VMEM((depth, 3 * width), BF),
        pltpu.VMEM((RANK, 3 * width), BF),
        pltpu.VMEM((width, depth), BF),
        pltpu.VMEM((width, RANK), BF),
    ]


def attention_kernel(cfg, *refs):
    own, others, width, depth, full, parts = cfg
    final = others > 0
    wp = width // parts
    it = iter(refs)
    take = lambda count: [next(it) for _ in range(count)]
    length, core_ref, u_h, z_h, g_h, dz_h, cos_h, sin_h = take(8)
    source = take(4 if own else parts)
    if final:
        gain, acat, bcat = take(3)
        other_sources = [take(4 if s == 0 else parts) for s in range(others)]
        made_h = [take(2) for _ in range(others)]
        out_h, e_h, sums, grads = take(4)
    else:
        c_out, dp_out, grads = take(3)
    u_s, z_s, g_s, dz_s, cos_s, sin_s = take(6)
    mine_s = take(4)
    wq_s, b_s, wo_s, a_s = mine_s
    q_s, k_s, v_s, dc_s, c_s, dp_s, dk_s, dv_s = take(8)
    if final:
        weights_s = [take(4) for _ in range(others)]
        made_s = [take(2) for _ in range(others)]
        out_s, e_s, sums_s = take(3)
        sem_o = take(1)[0]
    sem_in, sem_w, sem_out = take(3)
    big, size = 512, 256
    ins = []

    def fetch(src, dst):
        ins.append(pltpu.make_async_copy(src, dst, sem_in.at[len(ins)]))

    for src, dst in ((z_h, z_s), (cos_h, cos_s), (sin_h, sin_s)):
        fetch(src, dst)
    for block in range(full // big):
        rows = pl.ds(block * big, big)
        fetch(u_h.at[rows, :], u_s.at[rows, :])
    for src, dst in ((g_h, g_s), (dz_h, dz_s)):
        fetch(src, dst)
    made = []

    def add(src, dst):
        made.append(pltpu.make_async_copy(src, dst, sem_w.at[len(made)]))

    early = weight_copies(source, own, mine_s, add, depth, wp)
    for copy in made[:early] + ins[:4]:
        copy.start()
    key_place = lax.broadcasted_iota(jnp.int32, (1, full), 1)
    key_bias = jnp.where(key_place < length[0], 0.0, -1e30).astype(F32)
    lane_place = lax.broadcasted_iota(jnp.int32, (1, LANES), 1)
    masks = [
        (lane_place // HEAD_DIM == h).astype(F32).astype(BF) for h in range(LANES // HEAD_DIM)
    ]
    causal = lax.broadcasted_iota(jnp.int32, (QROWS, QROWS), 1) <= lax.broadcasted_iota(
        jnp.int32, (QROWS, QROWS), 0
    )
    for copy in made[:early] + ins[:4]:
        copy.wait()
    for copy in ins[4:] + made[early:]:
        copy.start()

    def place(p):
        if not own or parts == 1:
            return p
        return core_ref[0] if p == 0 else 1 - core_ref[0]

    for block in range(full // big):
        rows = pl.ds(block * big, big)
        if block > 0:
            ins[3 + block].wait()
        ub = u_s[rows, :]
        cosine, sine = cos_s[rows, :], sin_s[rows, :]
        for j, dst in enumerate((q_s, k_s, v_s)):
            lanes = pl.ds(j * width, width)
            value = dot(ub, wq_s[:, lanes]) + dot(z_s[rows, pl.ds(j * RANK, RANK)], b_s[:, lanes])
            if j < 2:
                value = turn(value, cosine, sine, 1)
            if j == 0:
                value = value * HEAD_DIM ** (-0.5)
            dst[rows, :] = value.astype(BF)
    for copy in ins[3 + full // big :] + made[early:]:
        copy.wait()
    if final:
        other_made = []
        for s in range(others):
            mine = []

            def add_other(src, dst):
                mine.append(pltpu.make_async_copy(src, dst, sem_o.at[s, len(mine)]))

            for src, dst in zip(made_h[s], made_s[s]):
                add_other(src, dst)
            weight_copies(other_sources[s], s == 0, weights_s[s], add_other, depth, wp)
            for copy in mine:
                copy.start()
            other_made += mine

    def project_back(block, carry):
        rows = rows_of(block, big)
        dc_s[rows, :] = (
            dot(g_s[rows, :], wo_s[...], NT) + dot(dz_s[rows, :], a_s[...], NT)
        ).astype(BF)
        return carry

    lax.fori_loop(0, full // big, project_back, 0)

    def pair(at, carry):
        lanes = pl.ds(pl.multiple_of(at * LANES, LANES), LANES)
        for i in range(full // QROWS):
            begin, end = i * QROWS, (i + 1) * QROWS
            rows = pl.ds(begin, QROWS)
            qb, db = q_s[rows, lanes], dc_s[rows, lanes]
            keys, vals = k_s[pl.ds(0, end), lanes], v_s[pl.ds(0, end), lanes]
            context = dq = dk = dv = None
            plus = lambda total, term: term if total is None else total + term
            for mask in masks:
                qm, dm = qb * mask, db * mask
                scores = dot(qm, keys, NT) + key_bias[:, :end]
                diag = jnp.where(causal, scores[:, begin:], -1e30)
                scores = diag if i == 0 else jnp.concatenate([scores[:, :begin], diag], axis=1)
                peak = jnp.max(scores, axis=-1, keepdims=True)
                raised = jnp.exp(scores - peak)
                total = jnp.sum(raised, axis=-1, keepdims=True)
                weights = raised * (1.0 / total)
                low_weights = weights.astype(BF)
                grad = dot(dm, vals, NT)
                inner = jnp.sum(weights * grad, axis=-1, keepdims=True)
                grad_scores = (weights * (grad - inner)).astype(BF)
                context = plus(context, dot(low_weights, vals * mask))
                dq = plus(dq, dot(grad_scores, keys * mask))
                dk = plus(dk, dot(grad_scores, qm, TN))
                dv = plus(dv, dot(low_weights, dm, TN))
            c_s[rows, lanes] = context.astype(BF)
            dp_s[rows, lanes] = turn(
                dq * HEAD_DIM ** (-0.5), cos_s[rows, :], sin_s[rows, :], -1
            ).astype(BF)
            if i > 0:
                past = pl.ds(0, begin)
                dk_s[past, :] += dk[:begin]
                dv_s[past, :] += dv[:begin]
            dk_s[rows, :] = dk[begin:]
            dv_s[rows, :] = dv[begin:]
        dp_s[:, pl.ds(pl.multiple_of(width + at * LANES, LANES), LANES)] = turn(dk_s[...], cos_s[...], sin_s[...], -1).astype(BF)
        dp_s[:, pl.ds(pl.multiple_of(2 * width + at * LANES, LANES), LANES)] = dv_s[...].astype(BF)
        return carry

    lax.fori_loop(0, width // LANES, pair, 0)
    outs = []
    if not final:
        outs = [
            pltpu.make_async_copy(c_s, c_out, sem_out.at[0, 0]),
            pltpu.make_async_copy(dp_s, dp_out, sem_out.at[0, 1]),
        ]
        for copy in outs:
            copy.start()
    ga = dot(c_s[...], dz_s[...], TN)
    for p in range(parts):
        grads[place(p), pl.ds(3 * wp, wp), :] = ga[p * wp : (p + 1) * wp].astype(BF)
    for j in range(3):
        gb = LOWRANK_SCALE * dot(
            dp_s[:, pl.ds(j * width, width)], z_s[:, pl.ds(j * RANK, RANK)], TN
        )
        for p in range(parts):
            grads[place(p), pl.ds(j * wp, wp), :] = gb[p * wp : (p + 1) * wp].astype(BF)
    if final:
        for copy in other_made:
            copy.wait()
        everything = [(c_s, dp_s, mine_s)] + [(*made_s[s], weights_s[s]) for s in range(others)]
        plus = lambda total, term: term if total is None else total + term
        for block in range(full // size):
            rows = pl.ds(block * size, size)
            out = du = zo = None
            dz = [None] * 3
            for cs, ds, (wq, b, wo, a) in everything:
                cb = cs[rows, :]
                out = plus(out, dot(cb, wo[...]))
                zo = plus(zo, dot(cb, a[...]))
                du = plus(du, dot(ds[rows, :], wq[...], NT))
                for j in range(3):
                    lanes = pl.ds(j * width, width)
                    dz[j] = plus(dz[j], dot(ds[rows, lanes], b[:, lanes], NT))
            zo = zo.astype(BF)
            dz = jnp.concatenate(dz, axis=1).astype(BF)
            out_s[rows, :] = out + dot(zo, bcat[...])
            e_s[rows, :] = (du + dot(dz, acat[...], NT)) * gain[0:1, :]
            ga = dot(u_s[rows, :], dz, TN)
            gb = dot(g_s[rows, :], zo, TN)
            for j in range(4):
                where = pl.ds(j * depth, depth)
                term = gb if j == 3 else ga[:, j * RANK : (j + 1) * RANK]
                sums_s[where, :] = term if block == 0 else sums_s[where, :] + term
            for at, (src, dst) in enumerate(((out_s, out_h), (e_s, e_h))):
                outs.append(
                    pltpu.make_async_copy(src.at[rows, :], dst.at[rows, :], sem_out.at[block, at])
                )
                outs[-1].start()
        first = pl.ds(0, 3 * depth)
        sums[first, :] = sums_s[first, :].astype(sums.dtype)
        last = pl.ds(3 * depth, depth)
        sums[last, :] = (LOWRANK_SCALE * sums_s[last, :]).astype(sums.dtype)
    for copy in outs:
        copy.wait()


def attention(length, core, acts, tables, source, own, last, width, parts):
    u1, z, g, dz = acts
    full, depth = u1.shape
    wp = width // parts
    operands = [length, core, u1, z, g, dz, *tables, *source]
    shape, vmem = jax.ShapeDtypeStruct, pltpu.VMEM
    grads = shape((parts, 4 * wp, RANK), BF)
    in_specs = [SMEM, SMEM] + [ANY] * (len(operands) - 2)
    scratch = [
        vmem((full, depth), BF), vmem((full, 3 * RANK), BF), vmem((full, depth), BF),
        vmem((full, RANK), BF), vmem((full, LANES), F32), vmem((full, LANES), F32),
        *weight_space(depth, width),
        *[vmem((full, width), BF)] * 5,
        vmem((full, 3 * width), BF), vmem((full, LANES), F32), vmem((full, LANES), F32),
    ]
    if last is None:
        others = 0
        out_shape = (shape((full, width), BF), shape((full, 3 * width), BF), grads)
        out_specs = (ANY, ANY, VMEM)
    else:
        side, sources, made = last
        others = len(sources)
        more = [r for s in sources for r in s] + [m for two in made for m in two]
        operands += [*side, *more]
        in_specs += [VMEM] * 3 + [ANY] * len(more)
        out_shape = (
            shape((full, depth), F32), shape((full, depth), F32), shape((4 * depth, RANK), BF), grads,
        )
        out_specs = (ANY, ANY, VMEM, VMEM)
        for _ in range(others):
            scratch += weight_space(depth, width)
        for _ in range(others):
            scratch += [vmem((full, width), BF), vmem((full, 3 * width), BF)]
        scratch += [vmem((full, depth), F32), vmem((full, depth), F32), vmem((4 * depth, RANK), F32)]
        copies = 2 + max(8, weight_count(False, parts, depth, wp))
        scratch.append(pltpu.SemaphoreType.DMA((others, copies)))
    scratch += [
        pltpu.SemaphoreType.DMA((5 + full // 512,)),
        pltpu.SemaphoreType.DMA((weight_count(own, parts, depth, wp),)),
        pltpu.SemaphoreType.DMA((full // 256, 2)),
    ]
    return pl.pallas_call(
        partial(attention_kernel, (own, others, width, depth, full, parts)),
        out_shape=out_shape,
        in_specs=in_specs,
        out_specs=out_specs,
        scratch_shapes=scratch,
        compiler_params=params(),
        cost_estimate=cost(18 if last is None else 36, 8 << 20),
        name="attention" if last is None else "attention_last",
    )(*operands)


def gelu_pair(x):
    size = jnp.abs(x)
    t = 1.0 / (1.0 + (0.3275911 * 2.0**-0.5) * size)
    poly = 1.061405429 * t - 1.453152027
    poly = poly * t + 1.421413741
    poly = poly * t - 0.284496736
    poly = (poly * t + 0.254829592) * t
    bell = jnp.exp(-0.5 * x * x)
    tail = 0.5 * poly * bell
    below = jnp.where(x >= 0.0, 1.0 - tail, tail)
    return x * below, below + x * bell * (2.0 * np.pi) ** -0.5


def mlp_kernel(cfg, *refs):
    kinds, carried, final, hidden, depth, full, parts = cfg
    fp, shards = hidden // parts, len(kinds)
    it = iter(refs)
    take = lambda count: [next(it) for _ in range(count)]
    core_ref, u_h, z_h, g_h, dz_h = take(5)
    sources = [take(4 if own else parts) for own in kinds]
    acc_h = take(4) if carried else None
    if final:
        x_h, attn_h, e_h, gain, acat, bcat = take(6)
    attn_grads = take(shards)
    out_h = take(2 if final else 4)
    (grads,) = take(1)
    if final:
        (sums,) = take(1)
    u_s, z_s, g_s, dz_s = take(4)
    wu_s, wd_s, b_s, a_s = take(4)
    acc_s = take(4)
    ga_s, gb_s = take(2)
    if final:
        x_s, attn_s, e_s, sums_s = take(4)
    sem_in, sem_w, sem_acc, sem_out = take(4)
    acc_o, acc_u, acc_z, acc_dz = acc_s
    size = 256
    chunk = min(1024, hidden)
    blocks = full // size

    def copies_of(pairs, sems):
        return [pltpu.make_async_copy(src, dst, sems.at[at]) for at, (src, dst) in enumerate(pairs)]

    def begin(copies):
        for copy in copies:
            copy.start()

    def finish_copies(copies):
        for copy in copies:
            copy.wait()

    ins = copies_of(zip((u_h, z_h, g_h, dz_h), (u_s, z_s, g_s, dz_s)), sem_in)

    def weights(shard):
        slot = shard % 2
        made = []

        def add(src, dst):
            made.append(pltpu.make_async_copy(src, dst, sem_w.at[slot, len(made)]))

        if kinds[shard]:
            for src, dst in zip(sources[shard], (wu_s, wd_s, b_s, a_s)):
                add(src, dst.at[slot])
            return made
        for p, ref in enumerate(sources[shard]):
            dst = pl.ds(p * fp, fp)
            add(ref.at[pl.ds(0, depth), :], wu_s.at[slot, :, dst])
            for m in range(depth // fp):
                add(ref.at[pl.ds(depth + m * fp, fp), :], wd_s.at[slot, dst, pl.ds(m * fp, fp)])
            add(ref.at[pl.ds(2 * depth, RANK), :], b_s.at[slot, :, dst])
            for m in range(fp // RANK):
                add(
                    ref.at[pl.ds(2 * depth + RANK, RANK), pl.ds(m * RANK, RANK)],
                    a_s.at[slot, pl.ds(p * fp + m * RANK, RANK), :],
                )
        return made

    first = weights(0)
    half = len(first) // 2 if not kinds[0] and hidden == 2 * chunk and parts == 2 else len(first)
    begin([*ins, *first[:half]])
    loads, outs = [], []
    for block in range(blocks):
        rows = pl.ds(block * size, size)
        pairs = list(zip(acc_h, acc_s)) if carried else []
        if final:
            pairs += [(x_h, x_s), (attn_h, attn_s), (e_h, e_s)]
        loads.append(copies_of([(src.at[rows, :], dst.at[rows, :]) for src, dst in pairs], sem_acc.at[block]))
    finish_copies([*ins, *first[:half]])
    begin(first[half:])
    begin(loads[0])
    plus = lambda total, term: term if total is None else total + term
    for s in range(shards):
        slot = s % 2
        if s > 0:
            finish_copies(weights(s))
        if s + 1 < shards:
            begin(weights(s + 1))
        ga_s[...] = jnp.zeros_like(ga_s)
        gb_s[...] = jnp.zeros_like(gb_s)

        def place(p):
            if not kinds[s] or parts == 1:
                return p
            return core_ref[0] if p == 0 else 1 - core_ref[0]

        pieces = hidden // chunk

        def expand(step):
            block, at = step // pieces, step % pieces * chunk
            if s == 0 and block == 0 and at == chunk:
                finish_copies(first[half:])
            rows, cols = pl.ds(block * size, size), pl.ds(at, chunk)
            linear = dot(u_s[rows, :], wu_s[slot, :, cols]) + dot(z_s[rows, :], b_s[slot, :, cols])
            grad = dot(g_s[rows, :], wd_s[slot, cols, :], NT) + dot(
                dz_s[rows, :], a_s[slot, cols, :], NT
            )
            return linear, grad

        ahead = expand(0)
        for step in range(blocks * pieces):
            block, at = step // pieces, step % pieces * chunk
            rows = pl.ds(block * size, size)
            ub, zb, gb, db = u_s[rows, :], z_s[rows, :], g_s[rows, :], dz_s[rows, :]
            linear, grad = ahead
            if step + 1 < blocks * pieces:
                ahead = expand(step + 1)
            if at == 0:
                out = du = zd = dz = None
                if s == 0 and block + 1 < blocks:
                    begin(loads[block + 1])
            cols = pl.ds(at, chunk)
            active, slope = gelu_pair(linear)
            active = active.astype(BF)
            grad = (grad * slope).astype(BF)
            out = plus(out, dot(active, wd_s[slot, cols, :]))
            zd = plus(zd, dot(active, a_s[slot, cols, :]))
            du = plus(du, dot(grad, wu_s[slot, :, cols], NT))
            dz = plus(dz, dot(grad, b_s[slot, :, cols], NT))
            ga_s[cols, :] += dot(active, db, TN)
            gb_s[cols, :] += dot(grad, zb, TN)
            if at + chunk < hidden:
                continue
            if s == 0:
                finish_copies(loads[block])
            new = []
            for ref, value in zip(acc_s, (out, du, zd, dz)):
                new.append(ref[rows, :] + value if carried or s > 0 else value)
            if final and s == shards - 1:
                out, du, zd, dz = new
                zd, dz = zd.astype(BF), dz.astype(BF)
                x = x_s[rows, :].astype(F32)
                acc_o[rows, :] = x + attn_s[rows, :] + out + dot(zd, bcat[...])
                both = e_s[rows, :] + (du + dot(dz, acat[...], NT)) * gain[1:2, :]
                centred, scale = norm_stats(x)
                hat = centred * scale
                mean = jnp.mean(both, axis=-1, keepdims=True)
                match = jnp.mean(both * hat, axis=-1, keepdims=True)
                acc_u[rows, :] = gb.astype(F32) + scale * (both - mean - hat * match)
                for k, term in enumerate((dot(ub, dz, TN), dot(gb, zd, TN))):
                    where = pl.ds(k * depth, depth)
                    sums_s[where, :] = term if block == 0 else sums_s[where, :] + term
            else:
                for ref, value in zip(acc_s, new):
                    ref[rows, :] = value
            if s == shards - 1:
                outs.append(
                    copies_of(
                        [(src.at[rows, :], dst.at[rows, :]) for src, dst in zip(acc_s, out_h)],
                        sem_out.at[block],
                    )
                )
                begin(outs[-1])
        for p in range(parts):
            part = pl.ds(p * fp, fp)
            grads[s, place(p), pl.ds(0, fp), :] = ga_s[part, :].astype(BF)
            grads[s, place(p), pl.ds(fp, fp), :] = (LOWRANK_SCALE * gb_s[part, :]).astype(BF)
            many = attn_grads[s].shape[1]
            grads[s, p, pl.ds(2 * fp, many), :] = attn_grads[s][p]
    if final:
        sums[pl.ds(0, depth), :] = sums_s[pl.ds(0, depth), :].astype(sums.dtype)
        sums[pl.ds(depth, depth), :] = (LOWRANK_SCALE * sums_s[pl.ds(depth, depth), :]).astype(
            sums.dtype
        )
    for copies in outs:
        finish_copies(copies)


def mlp(core, acts, sources, kinds, acc, last, attn_grads, hidden, parts):
    u2, z, g, dz = acts
    full, depth = u2.shape
    shards, fp = len(kinds), hidden // parts
    flat = [part for source in sources for part in source]
    copies = max(4, (2 + depth // fp + fp // RANK) * parts)
    slots = min(2, shards)
    carried, final = acc is not None, last is not None
    operands = [core, u2, z, g, dz, *flat, *(acc or ()), *(last or ()), *attn_grads]
    shape = jax.ShapeDtypeStruct
    first_acc = 5 + len(flat)
    out_shape = [shape((full, depth), F32), shape((full, depth), F32)]
    if not final:
        out_shape += [shape((full, RANK), F32), shape((full, RANK), F32)]
    out_specs = [ANY] * len(out_shape) + [VMEM] * (2 if final else 1)
    out_shape.append(shape((shards, parts, 2 * fp + attn_grads[0].shape[1], RANK), BF))
    if final:
        out_shape.append(shape((2 * depth, RANK), F32))
    in_specs = [SMEM] + [ANY] * (len(operands) - 1)
    in_specs[-shards:] = [VMEM] * shards
    if final:
        in_specs[-3 - shards : -shards] = [VMEM] * 3
    scratch = [
        pltpu.VMEM((full, depth), BF),
        pltpu.VMEM((full, RANK), BF),
        pltpu.VMEM((full, depth), BF),
        pltpu.VMEM((full, RANK), BF),
        pltpu.VMEM((slots, depth, hidden), BF),
        pltpu.VMEM((slots, hidden, depth), BF),
        pltpu.VMEM((slots, RANK, hidden), BF),
        pltpu.VMEM((slots, hidden, RANK), BF),
        pltpu.VMEM((full, depth), F32),
        pltpu.VMEM((full, depth), F32),
        pltpu.VMEM((full, RANK), F32),
        pltpu.VMEM((full, RANK), F32),
        pltpu.VMEM((hidden, RANK), F32),
        pltpu.VMEM((hidden, RANK), F32),
    ]
    if final:
        scratch += [
            pltpu.VMEM((full, depth), BF),
            pltpu.VMEM((full, depth), F32),
            pltpu.VMEM((full, depth), F32),
            pltpu.VMEM((2 * depth, RANK), F32),
        ]
    scratch += [
        pltpu.SemaphoreType.DMA((4,)),
        pltpu.SemaphoreType.DMA((slots, copies)),
        pltpu.SemaphoreType.DMA((full // 256, 7)),
        pltpu.SemaphoreType.DMA((full // 256, 4)),
    ]
    aliases = {first_acc + i: i for i in range(4)} if carried and not final else {}
    return pl.pallas_call(
        partial(mlp_kernel, (kinds, carried, final, hidden, depth, full, parts)),
        out_shape=out_shape,
        in_specs=in_specs,
        out_specs=out_specs,
        input_output_aliases=aliases,
        scratch_shapes=scratch,
        compiler_params=params(),
        cost_estimate=cost(17 * shards, 8 << 20),
        name="mlp",
    )(*operands)


def reduce_kernel(cfg, *refs):
    heads, planes, sets = cfg
    it = iter(refs)
    take = lambda count: [next(it) for _ in range(count)]
    own = take(heads)
    ins = take(len(sets))
    outs = [take(2) for _ in sets]
    spaces = [take(24) for _ in sets]
    dp, head = lax.axis_index("dp"), lax.axis_index("head")
    core, plane = lax.rem(dp, 2), lax.div(dp, 2)
    flip = lambda at, o: at + o - 2 * sum(
        (lax.rem(lax.div(at, 1 << k), 2) * (1 << k) for k in range(6) if o >> k & 1), 0
    )
    sibling = {"dp": plane * 2 + 1 - core}
    head_peer = lambda o: {"head": flip(head, o)}
    plane_peer = lambda o: {"dp": flip(plane, o) * 2 + core}
    peers = [sibling] + [head_peer(o) for o in range(1, heads)]
    peers += [plane_peer(o) for o in range(1, planes)]
    mesh_id = pl.DeviceIdType.MESH
    barrier = pltpu.get_barrier_semaphore()
    for peer in peers:
        pl.semaphore_signal(barrier, inc=1, device_id=peer, device_id_type=mesh_id)

    def send(src, dst, ssem, rsem, peer):
        copy = pltpu.make_async_remote_copy(
            src_ref=src, dst_ref=dst, send_sem=ssem, recv_sem=rsem,
            device_id=peer, device_id_type=mesh_id,
        )
        copy.start()
        return copy

    def flow(rows, q, out_p, out_q, space):
        at, hp, hq = rows
        (
            keep_p, keep_q, send1, recv1, send2, recv2, sum2, send3, recv3, gather,
            s1, r1, s2, r2, s3, r3, s4, r4, s5, r5, s6, r6, s7, r7,
        ) = space
        qp = hq // heads
        pz, qz = hp // planes, qp // planes
        for slot in range(2):
            total = own[0][slot, pl.ds(at, hp), :].astype(F32)
            for ref in own[1:]:
                total = total + ref[slot, pl.ds(at, hp), :].astype(F32)
            if slot == 0:
                keep_p[...] = total
            else:
                send1[pl.ds(0, hp), :] = total.astype(BF)
        send1[pl.ds(hp, hq), :] = q[rows_of(1 - core, hq), :].astype(BF)
        keep_q[...] = q[rows_of(core, hq), :].astype(F32)
        yield
        copy = send(send1, recv1, s1, r1, sibling)
        yield
        copy.wait()
        total_q = keep_q[...] + recv1[pl.ds(hp, hq), :].astype(F32)
        keep_q[...] = total_q
        send2[...] = total_q.astype(BF)
        copies = [
            send(
                send2.at[rows_of(flip(head, o), qp), :], recv2.at[o - 1], s2.at[o - 1], r2.at[o - 1],
                head_peer(o),
            )
            for o in range(1, heads)
        ]
        total_p = keep_p[...] + recv1[pl.ds(0, hp), :].astype(F32)
        keep_p[...] = total_p
        for k in range(planes):
            send3[k, pl.ds(0, pz), :] = total_p[k * pz : (k + 1) * pz].astype(BF)
        yield
        for copy in copies:
            copy.wait()
        piece = keep_q[rows_of(head, qp), :]
        for o in range(1, heads):
            piece = piece + recv2[o - 1].astype(F32)
        sum2[...] = piece
        for k in range(planes):
            send3[k, pl.ds(pz, qz), :] = piece[k * qz : (k + 1) * qz].astype(BF)
        copies = [
            send(send3.at[flip(plane, o)], recv3.at[o - 1], s3.at[o - 1], r3.at[o - 1], plane_peer(o))
            for o in range(1, planes)
        ]
        yield
        for copy in copies:
            copy.wait()
        mine_p = keep_p[rows_of(plane, pz), :]
        mine_q = sum2[rows_of(plane, qz), :]
        for o in range(1, planes):
            mine_p = mine_p + recv3[o - 1, pl.ds(0, pz), :].astype(F32)
            mine_q = mine_q + recv3[o - 1, pl.ds(pz, qz), :].astype(F32)
        gather[plane, pl.ds(0, pz), :] = mine_p.astype(BF)
        gather[plane, pl.ds(pz, qz), :] = mine_q.astype(BF)
        copies = [
            send(gather.at[plane], gather.at[plane], s4.at[o - 1], r4.at[o - 1], plane_peer(o))
            for o in range(1, planes)
        ]
        yield
        for copy in copies:
            copy.wait()
        for k in range(planes):
            out_q[core, rows_of(head * planes + k, qz), :] = gather[k, pl.ds(pz, qz), :]
            out_p[core, pl.ds(k * pz, pz), :] = gather[k, pl.ds(0, pz), :]
        mine = rows_of(head, qp)
        copies = [
            send(out_q.at[core, mine, :], out_q.at[core, mine, :], s5.at[o - 1], r5.at[o - 1], head_peer(o))
            for o in range(1, heads)
        ]
        copies.append(send(out_p.at[core], out_p.at[core], s6, r6, sibling))
        yield
        for copy in copies:
            copy.wait()
        copy = send(out_q.at[core], out_q.at[core], s7, r7, sibling)
        yield
        copy.wait()

    flows = [
        flow(rows, q, *out, space) for rows, q, out, space in zip(sets, ins, outs, spaces)
    ]
    for one in flows:
        next(one)
    pl.semaphore_wait(barrier, len(peers))
    done = object()
    while flows:
        flows = [one for one in flows if next(one, done) is not done]


def reduce_all(own, rest, sets, heads, planes):
    one = pltpu.SemaphoreType.DMA
    shape, vmem = jax.ShapeDtypeStruct, pltpu.VMEM
    sizes, scratch, out_shape, operands = [], [], [], [own, *rest]
    for at, hp, q in sets:
        hq = q.shape[0] // 2
        qp = hq // heads
        pz, qz = hp // planes, qp // planes
        sizes.append((at, hp, hq))
        operands.append(q)
        out_shape += [shape((2, hp, RANK), BF), shape((2, hq, RANK), BF)]
        scratch += [
            vmem((hp, RANK), F32), vmem((hq, RANK), F32),
            vmem((hp + hq, RANK), BF), vmem((hp + hq, RANK), BF),
            vmem((hq, RANK), BF), vmem((heads - 1, qp, RANK), BF), vmem((qp, RANK), F32),
            vmem((planes, pz + qz, RANK), BF), vmem((planes - 1, pz + qz, RANK), BF),
            vmem((planes, pz + qz, RANK), BF),
            one, one,
            one((heads - 1,)), one((heads - 1,)),
            one((planes - 1,)), one((planes - 1,)),
            one((planes - 1,)), one((planes - 1,)),
            one((heads - 1,)), one((heads - 1,)),
            one, one, one, one,
        ]
    return pl.pallas_call(
        partial(reduce_kernel, (heads, planes, sizes)),
        out_shape=out_shape,
        in_specs=[VMEM] * len(operands),
        out_specs=[VMEM] * len(out_shape),
        scratch_shapes=scratch,
        compiler_params=pltpu.CompilerParams(
            collective_id=0, has_side_effects=True, vmem_limit_bytes=60 << 20
        ),
        name="reduce",
    )(*operands)


def update_kernel(cfg, *refs):
    factors, merges, tensors, slots = cfg
    it = iter(refs)
    take = lambda count: [next(it) for _ in range(count)]
    count, wide = len(factors), max(slots) + 1
    (mask,) = take(1)
    grads = take(4)
    w_h, m_h = dict(zip(tensors, take(len(tensors)))), dict(zip(tensors, take(len(tensors))))
    resets = {t: next(it) for t in tensors if t[0] == "a"}
    frozen = take(wide)
    new_w, new_m = dict(zip(tensors, take(len(tensors)))), dict(zip(tensors, take(len(tensors))))
    out_c, out_l = take(wide), take(wide)
    w_s, m_s, n_s = take(count), take(count), take(count)
    r_s = {i: next(it) for i in range(count) if factors[i][0] == "a"}
    frozen_s, c_s, l_s = take(len(merges)), take(len(merges)), take(len(merges))
    sem_in, sem_out = take(2)
    loads, stores = [], []

    def load(src, dst):
        copy = pltpu.make_async_copy(src, dst, sem_in.at[len(loads)])
        copy.start()
        loads.append(copy)
        return copy

    def store(src, dst):
        copy = pltpu.make_async_copy(src, dst, sem_out.at[len(stores)])
        copy.start()
        stores.append(copy)

    pick = lambda ref, index: ref if index is None else ref.at[index]
    pick2 = lambda ref, k, index: ref.at[k] if index is None else ref.at[k, index]
    flag = mask[...].astype(F32)
    flag_col = jnp.broadcast_to(flag, (RANK, RANK)).T[:, :1]

    def load_factor(i):
        kind, tensor, index, _ = factors[i]
        mine = [load(pick(w_h[tensor], index), w_s[i])]
        mine += [load(pick2(m_h[tensor], k, index), m_s[i].at[k]) for k in range(2)]
        if kind == "a":
            mine.append(load(pick(resets[tensor], index), r_s[i]))
        return mine

    def step(i):
        kind, tensor, index, (source, spans) = factors[i]
        parts = [grads[source][pl.ds(at, size), :].astype(F32) for at, size in spans]
        grad = parts[0] if len(parts) == 1 else jnp.concatenate(parts, axis=0)
        if kind == "b":
            grad = grad.T
        keep = 1.0 - (flag if kind == "a" else flag_col)
        first = BETA_FIRST * m_s[i][0] + (1.0 - BETA_FIRST) * grad
        second = BETA_SECOND * m_s[i][1] + (1.0 - BETA_SECOND) * grad * grad
        scaled = first * (1.0 / (1.0 - BETA_FIRST**STEP))
        root = jnp.sqrt(second * (1.0 / (1.0 - BETA_SECOND**STEP)))
        weight = w_s[i][...]
        weight = weight - LEARN_RATE * (scaled / (root + ADAM_EPSILON) + WEIGHT_DECAY * weight)
        w_s[i][...] = weight
        m_s[i][0] = first * keep
        m_s[i][1] = second * keep
        for k in range(2):
            store(m_s[i].at[k], pick2(new_m[tensor], k, index))
        if kind == "a":
            n_s[i][...] = jnp.where(flag > 0.5, r_s[i][...].astype(F32), weight)
        else:
            n_s[i][...] = weight * keep
        store(n_s[i], pick(new_w[tensor], index))

    def split(value):
        high = value.astype(BF)
        return high, (value - high.astype(F32)).astype(BF)

    def merge(i):
        left, right, index = merges[i]
        right_high, right_low = split(w_s[right][...])
        right_all = jnp.concatenate([right_high, right_low, right_high], axis=0)
        total = w_s[left].shape[0]
        block = min(256, total)
        for at in range(0, total, block):
            rows = pl.ds(at, block)
            high, low = split(w_s[left][rows, :] * (LOWRANK_SCALE * flag))
            merged = frozen_s[i][rows, :].astype(F32) + dot(
                jnp.concatenate([high, high, low], axis=1), right_all
            )
            c_s[i][rows, :] = merged
            l_s[i][rows, :] = merged.astype(BF)
            store(c_s[i].at[rows, :], pick(out_c[slots[i]], index).at[rows, :])
            store(l_s[i].at[rows, :], pick(out_l[slots[i]], index).at[rows, :])

    waits = []
    for i, (left, right, index) in enumerate(merges):
        waits.append(load_factor(left) + load_factor(right))
        waits[-1].append(load(pick(frozen[slots[i]], index), frozen_s[i]))
    for i, (left, right, index) in enumerate(merges):
        for copy in waits[i]:
            copy.wait()
        step(left)
        step(right)
        merge(i)
    for copy in stores:
        copy.wait()


def update(mask, grads, factors, weights, merges, frozen):
    shape = jax.ShapeDtypeStruct
    tensors = sorted(weights)
    inner = lambda array, index: array.shape if index is None else array.shape[1:]
    shapes = [inner(weights[f[1]][0], f[2]) for f in factors]
    picked = [inner(w, m[2]) for m, w in zip(merges, frozen)]
    unique, slots = [], []
    for w in frozen:
        hit = [k for k, u in enumerate(unique) if u is w]
        if not hit:
            unique.append(w)
        slots.append(hit[0] if hit else len(unique) - 1)
    out_shape = [shape(weights[t][k].shape, F32) for k in range(2) for t in tensors]
    out_shape += [shape(u.shape, kind) for kind in (F32, BF) for u in unique]
    operands = [mask, *grads] + [weights[t][k] for k in range(2) for t in tensors]
    operands += [weights[t][2] for t in tensors if t[0] == "a"] + unique
    kinds = [f[0] for f in factors]
    scratch = [pltpu.VMEM(s, F32) for s in shapes]
    scratch += [pltpu.VMEM((2, *s), F32) for s in shapes]
    scratch += [pltpu.VMEM(s, F32) for s in shapes]
    scratch += [pltpu.VMEM(s, BF) for s, k in zip(shapes, kinds) if k == "a"]
    scratch += [pltpu.VMEM(s, kind) for kind in (BF, F32, BF) for s in picked]
    loads = 3 * len(factors) + kinds.count("a") + len(frozen)
    stores = 3 * len(factors) + sum(2 * (-(-s[0] // 256)) for s in picked)
    scratch += [pltpu.SemaphoreType.DMA((loads,)), pltpu.SemaphoreType.DMA((stores,))]
    return pl.pallas_call(
        partial(update_kernel, (factors, merges, tensors, slots)),
        out_shape=out_shape,
        in_specs=[VMEM] * 5 + [ANY] * (len(operands) - 5),
        out_specs=[ANY] * len(out_shape),
        scratch_shapes=scratch,
        compiler_params=params(),
        cost_estimate=cost(18, 60 << 20),
        name="update",
    )(*operands)


def rotary_tables(full):
    half = ROT_DIM // 2
    frequency = np.float32(ROPE_BASE) ** (-2.0 * np.arange(half, dtype=np.float32) / ROT_DIM)
    angles = np.arange(full, dtype=np.float32)[:, None] * frequency.astype(np.float32)[None, :]
    cosine = np.ones((full, HEAD_DIM), np.float32)
    sine = np.zeros((full, HEAD_DIM), np.float32)
    cosine[:, :half] = cosine[:, half:ROT_DIM] = np.cos(angles)
    sine[:, :half] = -np.sin(angles)
    sine[:, half:ROT_DIM] = np.sin(angles)
    return tuple(jnp.asarray(np.tile(t, (1, LANES // HEAD_DIM))) for t in (cosine, sine))


def per_device(
    layer_input_rows,
    lengths,
    cotangent,
    frozen_projection_weight,
    frozen_outproj_weight,
    frozen_up_weight,
    frozen_down_weight,
    frozen_norm_gain,
    frozen_norm_bias,
    shared_input_factors,
    outproj_input_factor,
    down_input_factor,
    projection_output_factors,
    up_output_factor,
    output_side_factors,
    input_factor_moments,
    outproj_input_factor_moments,
    down_input_factor_moments,
    projection_output_factor_moments,
    up_output_factor_moments,
    outproj_output_factor_moments,
    reset_input_factor,
    reset_outproj_input_factor,
    reset_down_input_factor,
    component_merge_mask,
):
    full, depth = layer_input_rows.shape[1:]
    x, cot = layer_input_rows[0], cotangent[0]
    width, hidden = frozen_outproj_weight.shape[0], frozen_down_weight.shape[0]
    heads, groups = lax.axis_size("head"), lax.axis_size("dp")
    parts = 2 if width % (2 * LANES) == 0 else 1
    place = lax.axis_index("head")
    core = lax.rem(lax.axis_index("dp"), 2)
    core_at = (core if parts == 2 else jnp.zeros_like(core)).reshape(1).astype(jnp.int32)
    length = lax.dynamic_slice_in_dim(lengths, place, 1)
    tables = rotary_tables(full)

    def over_head(value, offset):
        return lax.ppermute(value, "head", [(i, i ^ offset) for i in range(heads)])

    def over_core(value):
        return lax.ppermute(value, "dp", [(i, i ^ 1) for i in range(groups)])

    def relay(by_x, by_y):
        sent = jnp.where(core == 0, by_y, by_x)
        pairs = [
            (d * heads + h, d * heads + (h ^ (1 if d % 2 == 0 else 2)))
            for d in range(groups)
            for h in range(heads)
        ]
        return lax.ppermute(sent, ("dp", "head"), pairs)

    def both(value):
        return [value, over_core(value)] if parts == 2 else [value]

    pa, b4q, aob = pack(
        "attn", core_at, frozen_projection_weight, frozen_outproj_weight, projection_output_factors,
        outproj_input_factor, parts,
    )
    got_a = {o: over_head(pa, o) for o in (1, 2)}
    u1, z1, dz1, acat1, bcat1, g = prologue(
        0, length, x, cot, frozen_norm_gain, frozen_norm_bias, shared_input_factors, output_side_factors
    )
    acts1 = (u1, z1, g, dz1)
    own_a = (frozen_projection_weight, frozen_outproj_weight, b4q, aob)
    after = lax.optimization_barrier
    made, grads_a = {}, {}
    *made[0], grads_a[0] = attention(
        length, core_at, acts1, tables, own_a, True, None, width, parts
    )
    got_a[1], got_a[2], pm_in, grads_a[0] = after((got_a[1], got_a[2], frozen_up_weight, grads_a[0]))
    pm, b4up, adb = pack(
        "mlp", core_at, pm_in, frozen_down_weight, up_output_factor, down_input_factor, parts
    )
    own_m = (frozen_up_weight, frozen_down_weight, b4up, adb)
    pairs_a = {o: both(got_a[o]) for o in (1, 2)}
    acts1 = (u1, z1, g, after((dz1, pm))[0])
    if heads == 4 and parts == 2:
        got_a[3] = relay(got_a[1], got_a[2])
    else:
        for o in range(3, heads):
            got_a[o] = over_head(pa, o)
    for o in range(1, heads):
        if o == 2 and heads > 3:
            got_a[3], pm, grads_a[1] = after((got_a[3], pm, grads_a[1]))
            pairs_a[3] = both(got_a[3])
        elif o > 3:
            pairs_a[o] = both(got_a[o])
        if o == 2:
            got_m = {k: over_head(pm, k) for k in (1, 2)}
        pairs_a[o][0] = after((pairs_a[o][0], grads_a[o - 1]))[0]
        last = None
        if o == heads - 1:
            last = (
                (frozen_norm_gain, acat1, bcat1),
                [own_a] + [pairs_a[k] for k in range(1, o)],
                [made[k] for k in range(o)],
            )
        *made[o], grads_a[o] = attention(
            length, core_at, acts1, tables, pairs_a[o], False, last, width, parts
        )
    attn, e_one, q_attn = made[heads - 1]
    got_m[1], got_m[2], g_in, q_attn = after((got_m[1], got_m[2], g, q_attn))
    u2, z2, dz2, acat2, bcat2 = prologue(
        1, length, x, g_in, frozen_norm_gain, frozen_norm_bias, shared_input_factors,
        output_side_factors,
    )
    acts2 = (u2, z2, g, dz2)
    pairs_m = {o: both(got_m[o]) for o in (1, 2)}
    if heads == 4 and parts == 2:
        got_m[3] = relay(got_m[1], got_m[2])
    else:
        for o in range(3, heads):
            got_m[o] = over_head(pm, o)
    grads_m = {}
    *acc_m, grad = mlp(
        core_at, acts2, [pairs_m[1], pairs_m[2]], (False, False), None, None, [grads_a[1], grads_a[2]],
        hidden, parts,
    )
    grads_m[1], grads_m[2] = grad[0], grad[1]
    for o in range(3, heads):
        got_m[o], acc_m[2] = after((got_m[o], acc_m[2]))
        *acc_m, grad = mlp(
            core_at, acts2, [both(got_m[o])], (False,), acc_m, None, [grads_a[o]], hidden, parts
        )
        grads_m[o] = grad[0]
    layer_out, grad_in, grad, q_mlp = mlp(
        core_at, acts2, [own_m], (True,), acc_m, (x, attn, e_one, frozen_norm_gain, acat2, bcat2),
        [grads_a[0]], hidden, parts,
    )
    grads_m[0] = grad[0]

    def gather(grads):
        flat = {o: grad.reshape(grad.shape[0], -1, RANK) for o, grad in grads.items()}
        return flat[0], [over_head(flat[o], o) for o in range(1, heads)]

    def over_head_sum(own, rest):
        total = own.astype(F32)
        for other in rest:
            total = total + other.astype(F32)
        if parts == 2:
            total = jnp.where(core == 0, total, total[::-1])
        return total.astype(BF)

    own_all, rest_all = gather(grads_m)
    planes = groups // 2
    wp, fp = width // parts, hidden // parts
    rows_a, rows_m = 4 * wp, 2 * fp
    pieces = 2 * heads * planes
    if parts == 2 and q_attn.shape[0] // pieces % 16 == 0 and q_mlp.shape[0] // pieces % 16 == 0:
        p_attn, q_attn, p_mlp, q_mlp = reduce_all(
            own_all, rest_all, [(rows_m, rows_a, q_attn), (0, rows_m, q_mlp)], heads, planes
        )
    else:
        p_all = lax.psum(over_head_sum(own_all, rest_all), "dp")
        p_attn, p_mlp = p_all[:, rows_m:], p_all[:, :rows_m]
        q_attn, q_mlp = lax.psum((q_attn, q_mlp.astype(BF)), ("dp", "head"))
    mask = component_merge_mask.reshape(1, RANK)
    from_a = lambda k: (0, tuple((p * rows_a + k * wp, wp) for p in range(parts)))
    from_m = lambda k: (2, tuple((p * rows_m + k * fp, fp) for p in range(parts)))
    from_q = lambda half, k: (1, (((2 * half + k) * depth, depth),))
    from_r = lambda k: (3, ((k * depth, depth),))
    factors = (
        ("a", "a_in", 0, from_q(0, 0)),
        ("b", "b_qkv", 0, from_a(0)),
        ("a", "a_in", 1, from_q(0, 1)),
        ("b", "b_qkv", 1, from_a(1)),
        ("a", "a_in", 2, from_q(1, 0)),
        ("b", "b_qkv", 2, from_a(2)),
        ("a", "a_out", None, from_a(3)),
        ("b", "b_out", 0, from_q(1, 1)),
        ("a", "a_in", 3, from_r(0)),
        ("b", "b_up", None, from_m(1)),
        ("a", "a_down", None, from_m(0)),
        ("b", "b_out", 1, from_r(1)),
    )
    weights = {
        "a_in": (shared_input_factors, input_factor_moments, reset_input_factor),
        "a_out": (outproj_input_factor, outproj_input_factor_moments, reset_outproj_input_factor),
        "a_down": (down_input_factor, down_input_factor_moments, reset_down_input_factor),
        "b_qkv": (projection_output_factors, projection_output_factor_moments, None),
        "b_up": (up_output_factor, up_output_factor_moments, None),
        "b_out": (output_side_factors, outproj_output_factor_moments, None),
    }
    (
        new_a_down, new_a_in, new_a_out, new_b_out, new_b_qkv, new_b_up,
        new_m_a_down, new_m_a_in, new_m_a_out, new_m_b_out, new_m_b_qkv, new_m_b_up,
        comb_qkv, comb_out, comb_up, comb_down, copy_qkv, copy_out, copy_up, copy_down,
    ) = update(
        mask, [v.reshape(-1, RANK) for v in (p_attn, q_attn, p_mlp, q_mlp)], factors, weights,
        ((0, 1, 0), (2, 3, 1), (4, 5, 2), (6, 7, None), (8, 9, None), (10, 11, None)),
        (frozen_projection_weight,) * 3
        + (frozen_outproj_weight, frozen_up_weight, frozen_down_weight),
    )
    return (
        layer_out[None], grad_in[None],
        new_a_in, new_a_out, new_a_down, new_b_qkv, new_b_up, new_b_out,
        new_m_a_in, new_m_a_out, new_m_a_down, new_m_b_qkv, new_m_b_up, new_m_b_out,
        comb_qkv, comb_out, comb_up, comb_down, copy_qkv, copy_out, copy_up, copy_down,
    )


def solution(mesh):
    return jax.shard_map(
        per_device,
        mesh=mesh,
        in_specs=(
            P(("dp", "head"), None, None),
            P("dp"),
            P(("dp", "head"), None, None),
            P(None, None, "head"),
            P("head", None),
            P(None, "head"),
            P("head", None),
            P(),
            P(),
            P(),
            P("head", None),
            P("head", None),
            P(None, None, "head"),
            P(None, "head"),
            P(),
            P(),
            P(None, "head", None),
            P(None, "head", None),
            P(None, None, None, "head"),
            P(None, None, "head"),
            P(),
            P(),
            P("head", None),
            P("head", None),
            P(),
        ),
        out_specs=(
            P(("dp", "head"), None, None),
            P(("dp", "head"), None, None),
            P(),
            P("head", None),
            P("head", None),
            P(None, None, "head"),
            P(None, "head"),
            P(),
            P(),
            P(None, "head", None),
            P(None, "head", None),
            P(None, None, None, "head"),
            P(None, None, "head"),
            P(),
            P(None, None, "head"),
            P("head", None),
            P(None, "head"),
            P("head", None),
            P(None, None, "head"),
            P("head", None),
            P(None, "head"),
            P("head", None),
        ),
        check_vma=False,
    )
```

```python
from functools import partial

import jax
import jax.numpy as jnp
import numpy as np
from jax import lax
from jax.experimental import pallas as pl
from jax.experimental.pallas import tpu as pltpu
from jax.sharding import PartitionSpec as P

HEAD_DIM = 64
ROT_DIM = 16
STEP = 10
RANK = 128
LANES = 128
QROWS = 256


NORM_EPSILON = 1e-05
LOWRANK_SCALE = 0.25
LEARN_RATE = 0.15
BETA_FIRST = 0.9
BETA_SECOND = 0.999
WEIGHT_DECAY = 0.01
ADAM_EPSILON = 1e-08
ROPE_BASE = 10000.0

BF = jnp.bfloat16
F32 = jnp.float32
ANY = pl.BlockSpec(memory_space=pltpu.HBM)
VMEM = pl.BlockSpec(memory_space=pltpu.VMEM)
SMEM = pl.BlockSpec(memory_space=pltpu.SMEM)
NN = (((1,), (0,)), ((), ()))
NT = (((1,), (1,)), ((), ()))
TN = (((0,), (0,)), ((), ()))


def dot(left, right, dims=NN):
    return lax.dot_general(left, right, dims, preferred_element_type=F32)


def params(mib=60):
    return pltpu.CompilerParams(vmem_limit_bytes=mib * 1024 * 1024)


def cost(micros, nbytes):
    return pl.CostEstimate(flops=int(micros * 1.15e9), bytes_accessed=nbytes, transcendentals=0)


def rows_of(block, size):
    return pl.ds(pl.multiple_of(block * size, size), size)


def pack_kernel(kind, shape, core_ref, *refs):
    width, depth, parts = shape
    part = width // parts
    w1, w2, b, a, packed, b_low, a_low, w1_s, w2_s, load, sems = refs
    core = core_ref[0]
    loads = [
        pltpu.make_async_copy(src, dst, load.at[at])
        for at, (src, dst) in enumerate(((w1, w1_s), (w2, w2_s)))
    ]
    for copy in loads:
        copy.start()
    copies = []

    def start(src, dst):
        copy = pltpu.make_async_copy(src, dst, sems.at[len(copies)])
        copy.start()
        copies.append(copy)

    lanes = pl.ds(pl.multiple_of(core * part, part), part)
    b_low[...] = (b[...] * LOWRANK_SCALE).astype(BF)
    a_low[...] = a[...].astype(BF)
    many = 3 if kind == "attn" else 1
    loads[0].wait()
    for j in range(many):
        src = (w1_s.at[j], b_low.at[j]) if kind == "attn" else (w1_s, b_low)
        start(src[0].at[:, lanes], packed.at[pl.ds(j * depth, depth), :])
        start(src[1].at[:, lanes], packed.at[pl.ds((many + 1) * depth + j * RANK, RANK), :])
    at = (many + 1) * depth + many * RANK
    for m in range(part // RANK):
        start(
            a_low.at[pl.ds(pl.multiple_of(core * part + m * RANK, RANK), RANK), :],
            packed.at[pl.ds(at, RANK), pl.ds(m * RANK, RANK)],
        )
    loads[1].wait()
    for m in range(depth // part):
        start(w2_s.at[lanes, pl.ds(m * part, part)], packed.at[pl.ds(many * depth + m * part, part), :])
    for copy in copies:
        copy.wait()


def pack(kind, core, w1, w2, b, a, parts):
    depth, width = w1.shape[-2:]
    part = width // parts
    many = 3 if kind == "attn" else 1
    count = 2 * many + part // RANK + depth // part
    return pl.pallas_call(
        partial(pack_kernel, kind, (width, depth, parts)),
        out_shape=(
            jax.ShapeDtypeStruct(((many + 1) * depth + (many + 1) * RANK, part), BF),
            jax.ShapeDtypeStruct(b.shape, BF),
            jax.ShapeDtypeStruct(a.shape, BF),
        ),
        in_specs=[SMEM, ANY, ANY, VMEM, VMEM],
        out_specs=(ANY, VMEM, VMEM),
        scratch_shapes=[
            pltpu.VMEM(w1.shape, BF),
            pltpu.VMEM(w2.shape, BF),
            pltpu.SemaphoreType.DMA((2,)),
            pltpu.SemaphoreType.DMA((count,)),
        ],
        compiler_params=params(),
        cost_estimate=cost(3, 4 << 20),
        name="pack_" + kind,
    )(core, w1, w2, b, a)


def norm_stats(x):
    mean = jnp.mean(x, axis=-1, keepdims=True)
    centred = x - mean
    spread = jnp.mean(centred * centred, axis=-1, keepdims=True)
    return centred, lax.rsqrt(spread + NORM_EPSILON)


def prologue_kernel(which, length, x, cot, gain, bias, a_in, b_out, u, z, dz, acat, bcat, *g):
    step = pl.program_id(0)

    @pl.when(step == 0)
    def _():
        for j in range(a_in.shape[0]):
            acat[:, j * RANK : (j + 1) * RANK] = a_in[j].astype(BF)
        bcat[...] = (b_out[0] * LOWRANK_SCALE).astype(BF)

    rows = x.shape[0]
    centred, scale = norm_stats(x[...].astype(F32))
    low = (centred * scale * gain[which : which + 1, :] + bias[which : which + 1, :]).astype(BF)
    u[...] = low
    z[...] = dot(low, acat[...]).astype(BF)
    if g:
        place = step * rows + lax.broadcasted_iota(jnp.int32, (rows, 1), 0)
        live = (place < length[0]).astype(F32)
        grad = (cot[...].astype(F32) * live).astype(BF)
        g[0][...] = grad
    else:
        grad = cot[...]
    dz[...] = dot(grad, bcat[...], NT).astype(BF)


def prologue(which, length, x, cot, gain, bias, a_in, b_out):
    full, depth = x.shape
    rows = 512
    many = 3 if which == 0 else 1
    blk = lambda cols: pl.BlockSpec((rows, cols), lambda i: (i, 0))
    const = lambda shape: pl.BlockSpec(shape, lambda i: (0,) * len(shape))
    shape = jax.ShapeDtypeStruct
    out_shape = [
        shape((full, depth), BF),
        shape((full, many * RANK), BF),
        shape((full, RANK), BF),
        shape((depth, many * RANK), BF),
        shape((RANK, depth), BF),
    ]
    out_specs = [blk(depth), blk(many * RANK), blk(RANK), const((depth, many * RANK)), const((RANK, depth))]
    if which == 0:
        out_shape.append(shape((full, depth), BF))
        out_specs.append(blk(depth))
    return pl.pallas_call(
        partial(prologue_kernel, which),
        grid=(full // rows,),
        out_shape=out_shape,
        in_specs=[
            SMEM, blk(depth), blk(depth), const(gain.shape), const(bias.shape),
            pl.BlockSpec((many, depth, RANK), lambda i: (which, 0, 0) if which == 0 else (3, 0, 0)),
            pl.BlockSpec((1, RANK, depth), lambda i: (which, 0, 0)),
        ],
        out_specs=out_specs,
        compiler_params=params(),
        cost_estimate=cost(4, 12 << 20),
        name=("prologue_attn", "prologue_mlp")[which],
    )(length, x, cot, gain, bias, a_in, b_out)


def turn(x, cosine, sine, sign):
    lower = lax.rem(lax.broadcasted_iota(jnp.int32, (1, LANES), 1), HEAD_DIM) < ROT_DIM // 2
    done = []
    for at in range(0, x.shape[1], LANES):
        part = x[:, at : at + LANES]
        other = jnp.where(
            lower, pltpu.roll(part, LANES - ROT_DIM // 2, 1), pltpu.roll(part, ROT_DIM // 2, 1)
        )
        shifted = other * sine
        done.append(part * cosine + shifted if sign > 0 else part * cosine - shifted)
    return done[0] if len(done) == 1 else jnp.concatenate(done, axis=1)


def weight_copies(source, own, dsts, add, depth, wp):
    wq_s, b_s, wo_s, a_s = dsts
    width = wo_s.shape[0]
    if own:
        w1, w2, b1, a1 = source
        for j in range(3):
            add(w1.at[j], wq_s.at[:, pl.ds(j * width, width)])
            add(b1.at[j], b_s.at[:, pl.ds(j * width, width)])
        add(w2, wo_s)
        add(a1, a_s)
        return 6
    for p, ref in enumerate(source):
        for j in range(3):
            dst = pl.ds(j * width + p * wp, wp)
            add(ref.at[pl.ds(j * depth, depth), :], wq_s.at[:, dst])
            add(ref.at[pl.ds(4 * depth + j * RANK, RANK), :], b_s.at[:, dst])
    for p, ref in enumerate(source):
        dst = pl.ds(p * wp, wp)
        for m in range(depth // wp):
            add(ref.at[pl.ds(3 * depth + m * wp, wp), :], wo_s.at[dst, pl.ds(m * wp, wp)])
        add(ref.at[pl.ds(4 * depth + 3 * RANK, wp), :], a_s.at[dst, :])
    return 6 * len(source)


def weight_count(own, parts, depth, wp):
    return 8 if own else (7 + depth // wp) * parts


def weight_space(depth, width):
    return [
        pltpu.VMEM((depth, 3 * width), BF),
        pltpu.VMEM((RANK, 3 * width), BF),
        pltpu.VMEM((width, depth), BF),
        pltpu.VMEM((width, RANK), BF),
    ]


def attention_kernel(cfg, *refs):
    own, others, width, depth, full, parts = cfg
    final = others > 0
    wp = width // parts
    it = iter(refs)
    take = lambda count: [next(it) for _ in range(count)]
    length, core_ref, u_h, z_h, g_h, dz_h, cos_h, sin_h = take(8)
    source = take(4 if own else parts)
    if final:
        gain, acat, bcat = take(3)
        other_sources = [take(4 if s == 0 else parts) for s in range(others)]
        made_h = [take(2) for _ in range(others)]
        out_h, e_h, sums, grads = take(4)
    else:
        c_out, dp_out, grads = take(3)
    u_s, z_s, g_s, dz_s, cos_s, sin_s = take(6)
    mine_s = take(4)
    wq_s, b_s, wo_s, a_s = mine_s
    q_s, k_s, v_s, dc_s, c_s, dp_s, dk_s, dv_s = take(8)
    if final:
        weights_s = [take(4) for _ in range(others)]
        made_s = [take(2) for _ in range(others)]
        out_s, e_s, sums_s = take(3)
        sem_o = take(1)[0]
    sem_in, sem_w, sem_out = take(3)
    big, size = 512, 256
    ins = []

    def fetch(src, dst):
        ins.append(pltpu.make_async_copy(src, dst, sem_in.at[len(ins)]))

    for src, dst in ((z_h, z_s), (cos_h, cos_s), (sin_h, sin_s)):
        fetch(src, dst)
    for block in range(full // big):
        rows = pl.ds(block * big, big)
        fetch(u_h.at[rows, :], u_s.at[rows, :])
    for src, dst in ((g_h, g_s), (dz_h, dz_s)):
        fetch(src, dst)
    made = []

    def add(src, dst):
        made.append(pltpu.make_async_copy(src, dst, sem_w.at[len(made)]))

    early = weight_copies(source, own, mine_s, add, depth, wp)
    for copy in made[:early] + ins[:4]:
        copy.start()
    key_place = lax.broadcasted_iota(jnp.int32, (1, full), 1)
    key_bias = jnp.where(key_place < length[0], 0.0, -1e30).astype(F32)
    lane_place = lax.broadcasted_iota(jnp.int32, (1, LANES), 1)
    masks = [
        (lane_place // HEAD_DIM == h).astype(F32).astype(BF) for h in range(LANES // HEAD_DIM)
    ]
    causal = lax.broadcasted_iota(jnp.int32, (QROWS, QROWS), 1) <= lax.broadcasted_iota(
        jnp.int32, (QROWS, QROWS), 0
    )
    for copy in made[:early] + ins[:4]:
        copy.wait()
    for copy in ins[4:] + made[early:]:
        copy.start()

    def place(p):
        if not own or parts == 1:
            return p
        return core_ref[0] if p == 0 else 1 - core_ref[0]

    for block in range(full // big):
        rows = pl.ds(block * big, big)
        if block > 0:
            ins[3 + block].wait()
        ub = u_s[rows, :]
        cosine, sine = cos_s[rows, :], sin_s[rows, :]
        for j, dst in enumerate((q_s, k_s, v_s)):
            lanes = pl.ds(j * width, width)
            value = dot(ub, wq_s[:, lanes]) + dot(z_s[rows, pl.ds(j * RANK, RANK)], b_s[:, lanes])
            if j < 2:
                value = turn(value, cosine, sine, 1)
            if j == 0:
                value = value * HEAD_DIM ** (-0.5)
            dst[rows, :] = value.astype(BF)
    for copy in ins[3 + full // big :] + made[early:]:
        copy.wait()
    if final:
        other_made = []
        for s in range(others):
            mine = []

            def add_other(src, dst):
                mine.append(pltpu.make_async_copy(src, dst, sem_o.at[s, len(mine)]))

            for src, dst in zip(made_h[s], made_s[s]):
                add_other(src, dst)
            weight_copies(other_sources[s], s == 0, weights_s[s], add_other, depth, wp)
            for copy in mine:
                copy.start()
            other_made += mine

    def project_back(block, carry):
        rows = rows_of(block, big)
        dc_s[rows, :] = (
            dot(g_s[rows, :], wo_s[...], NT) + dot(dz_s[rows, :], a_s[...], NT)
        ).astype(BF)
        return carry

    lax.fori_loop(0, full // big, project_back, 0)

    def pair(at, carry):
        lanes = pl.ds(pl.multiple_of(at * LANES, LANES), LANES)
        for i in range(full // QROWS):
            begin, end = i * QROWS, (i + 1) * QROWS
            rows = pl.ds(begin, QROWS)
            qb, db = q_s[rows, lanes], dc_s[rows, lanes]
            keys, vals = k_s[pl.ds(0, end), lanes], v_s[pl.ds(0, end), lanes]
            context = dq = dk = dv = None
            plus = lambda total, term: term if total is None else total + term
            for mask in masks:
                qm, dm = qb * mask, db * mask
                scores = dot(qm, keys, NT) + key_bias[:, :end]
                diag = jnp.where(causal, scores[:, begin:], -1e30)
                scores = diag if i == 0 else jnp.concatenate([scores[:, :begin], diag], axis=1)
                peak = jnp.max(scores, axis=-1, keepdims=True)
                raised = jnp.exp(scores - peak)
                total = jnp.sum(raised, axis=-1, keepdims=True)
                weights = raised * (1.0 / total)
                low_weights = weights.astype(BF)
                grad = dot(dm, vals, NT)
                inner = jnp.sum(weights * grad, axis=-1, keepdims=True)
                grad_scores = (weights * (grad - inner)).astype(BF)
                context = plus(context, dot(low_weights, vals * mask))
                dq = plus(dq, dot(grad_scores, keys * mask))
                dk = plus(dk, dot(grad_scores, qm, TN))
                dv = plus(dv, dot(low_weights, dm, TN))
            c_s[rows, lanes] = context.astype(BF)
            dp_s[rows, lanes] = turn(
                dq * HEAD_DIM ** (-0.5), cos_s[rows, :], sin_s[rows, :], -1
            ).astype(BF)
            if i > 0:
                past = pl.ds(0, begin)
                dk_s[past, :] += dk[:begin]
                dv_s[past, :] += dv[:begin]
            dk_s[rows, :] = dk[begin:]
            dv_s[rows, :] = dv[begin:]
        dp_s[:, pl.ds(pl.multiple_of(width + at * LANES, LANES), LANES)] = turn(dk_s[...], cos_s[...], sin_s[...], -1).astype(BF)
        dp_s[:, pl.ds(pl.multiple_of(2 * width + at * LANES, LANES), LANES)] = dv_s[...].astype(BF)
        return carry

    lax.fori_loop(0, width // LANES, pair, 0)
    outs = []
    if not final:
        outs = [
            pltpu.make_async_copy(c_s, c_out, sem_out.at[0, 0]),
            pltpu.make_async_copy(dp_s, dp_out, sem_out.at[0, 1]),
        ]
        for copy in outs:
            copy.start()
    ga = dot(c_s[...], dz_s[...], TN)
    for p in range(parts):
        grads[place(p), pl.ds(3 * wp, wp), :] = ga[p * wp : (p + 1) * wp].astype(BF)
    for j in range(3):
        gb = LOWRANK_SCALE * dot(
            dp_s[:, pl.ds(j * width, width)], z_s[:, pl.ds(j * RANK, RANK)], TN
        )
        for p in range(parts):
            grads[place(p), pl.ds(j * wp, wp), :] = gb[p * wp : (p + 1) * wp].astype(BF)
    if final:
        for copy in other_made:
            copy.wait()
        everything = [(c_s, dp_s, mine_s)] + [(*made_s[s], weights_s[s]) for s in range(others)]
        plus = lambda total, term: term if total is None else total + term
        for block in range(full // size):
            rows = pl.ds(block * size, size)
            out = du = zo = None
            dz = [None] * 3
            for cs, ds, (wq, b, wo, a) in everything:
                cb = cs[rows, :]
                out = plus(out, dot(cb, wo[...]))
                zo = plus(zo, dot(cb, a[...]))
                du = plus(du, dot(ds[rows, :], wq[...], NT))
                for j in range(3):
                    lanes = pl.ds(j * width, width)
                    dz[j] = plus(dz[j], dot(ds[rows, lanes], b[:, lanes], NT))
            zo = zo.astype(BF)
            dz = jnp.concatenate(dz, axis=1).astype(BF)
            out_s[rows, :] = out + dot(zo, bcat[...])
            e_s[rows, :] = (du + dot(dz, acat[...], NT)) * gain[0:1, :]
            ga = dot(u_s[rows, :], dz, TN)
            gb = dot(g_s[rows, :], zo, TN)
            for j in range(4):
                where = pl.ds(j * depth, depth)
                term = gb if j == 3 else ga[:, j * RANK : (j + 1) * RANK]
                sums_s[where, :] = term if block == 0 else sums_s[where, :] + term
            for at, (src, dst) in enumerate(((out_s, out_h), (e_s, e_h))):
                outs.append(
                    pltpu.make_async_copy(src.at[rows, :], dst.at[rows, :], sem_out.at[block, at])
                )
                outs[-1].start()
        first = pl.ds(0, 3 * depth)
        sums[first, :] = sums_s[first, :].astype(sums.dtype)
        last = pl.ds(3 * depth, depth)
        sums[last, :] = (LOWRANK_SCALE * sums_s[last, :]).astype(sums.dtype)
    for copy in outs:
        copy.wait()


def attention(length, core, acts, tables, source, own, last, width, parts):
    u1, z, g, dz = acts
    full, depth = u1.shape
    wp = width // parts
    operands = [length, core, u1, z, g, dz, *tables, *source]
    shape, vmem = jax.ShapeDtypeStruct, pltpu.VMEM
    grads = shape((parts, 4 * wp, RANK), BF)
    in_specs = [SMEM, SMEM] + [ANY] * (len(operands) - 2)
    scratch = [
        vmem((full, depth), BF), vmem((full, 3 * RANK), BF), vmem((full, depth), BF),
        vmem((full, RANK), BF), vmem((full, LANES), F32), vmem((full, LANES), F32),
        *weight_space(depth, width),
        *[vmem((full, width), BF)] * 5,
        vmem((full, 3 * width), BF), vmem((full, LANES), F32), vmem((full, LANES), F32),
    ]
    if last is None:
        others = 0
        out_shape = (shape((full, width), BF), shape((full, 3 * width), BF), grads)
        out_specs = (ANY, ANY, VMEM)
    else:
        side, sources, made = last
        others = len(sources)
        more = [r for s in sources for r in s] + [m for two in made for m in two]
        operands += [*side, *more]
        in_specs += [VMEM] * 3 + [ANY] * len(more)
        out_shape = (
            shape((full, depth), F32), shape((full, depth), F32), shape((4 * depth, RANK), BF), grads,
        )
        out_specs = (ANY, ANY, VMEM, VMEM)
        for _ in range(others):
            scratch += weight_space(depth, width)
        for _ in range(others):
            scratch += [vmem((full, width), BF), vmem((full, 3 * width), BF)]
        scratch += [vmem((full, depth), F32), vmem((full, depth), F32), vmem((4 * depth, RANK), F32)]
        copies = 2 + max(8, weight_count(False, parts, depth, wp))
        scratch.append(pltpu.SemaphoreType.DMA((others, copies)))
    scratch += [
        pltpu.SemaphoreType.DMA((5 + full // 512,)),
        pltpu.SemaphoreType.DMA((weight_count(own, parts, depth, wp),)),
        pltpu.SemaphoreType.DMA((full // 256, 2)),
    ]
    return pl.pallas_call(
        partial(attention_kernel, (own, others, width, depth, full, parts)),
        out_shape=out_shape,
        in_specs=in_specs,
        out_specs=out_specs,
        scratch_shapes=scratch,
        compiler_params=params(),
        cost_estimate=cost(18 if last is None else 36, 8 << 20),
        name="attention" if last is None else "attention_last",
    )(*operands)


def gelu_pair(x):
    size = jnp.abs(x)
    t = 1.0 / (1.0 + (0.3275911 * 2.0**-0.5) * size)
    poly = 1.061405429 * t - 1.453152027
    poly = poly * t + 1.421413741
    poly = poly * t - 0.284496736
    poly = (poly * t + 0.254829592) * t
    bell = jnp.exp(-0.5 * x * x)
    tail = 0.5 * poly * bell
    below = jnp.where(x >= 0.0, 1.0 - tail, tail)
    return x * below, below + x * bell * (2.0 * np.pi) ** -0.5


def mlp_kernel(cfg, *refs):
    kinds, carried, final, hidden, depth, full, parts = cfg
    fp, shards = hidden // parts, len(kinds)
    it = iter(refs)
    take = lambda count: [next(it) for _ in range(count)]
    core_ref, u_h, z_h, g_h, dz_h = take(5)
    sources = [take(4 if own else parts) for own in kinds]
    acc_h = take(4) if carried else None
    if final:
        x_h, attn_h, e_h, gain, acat, bcat = take(6)
    attn_grads = take(shards)
    out_h = take(2 if final else 4)
    (grads,) = take(1)
    if final:
        (sums,) = take(1)
    u_s, z_s, g_s, dz_s = take(4)
    wu_s, wd_s, b_s, a_s = take(4)
    acc_s = take(4)
    ga_s, gb_s = take(2)
    if final:
        x_s, attn_s, e_s, sums_s = take(4)
    sem_in, sem_w, sem_acc, sem_out = take(4)
    acc_o, acc_u, acc_z, acc_dz = acc_s
    size = 256
    chunk = min(1024, hidden)
    blocks = full // size

    def copies_of(pairs, sems):
        return [pltpu.make_async_copy(src, dst, sems.at[at]) for at, (src, dst) in enumerate(pairs)]

    def begin(copies):
        for copy in copies:
            copy.start()

    def finish_copies(copies):
        for copy in copies:
            copy.wait()

    ins = copies_of(zip((u_h, z_h, g_h, dz_h), (u_s, z_s, g_s, dz_s)), sem_in)

    def weights(shard):
        slot = shard % 2
        made = []

        def add(src, dst):
            made.append(pltpu.make_async_copy(src, dst, sem_w.at[slot, len(made)]))

        if kinds[shard]:
            for src, dst in zip(sources[shard], (wu_s, wd_s, b_s, a_s)):
                add(src, dst.at[slot])
            return made
        for p, ref in enumerate(sources[shard]):
            dst = pl.ds(p * fp, fp)
            add(ref.at[pl.ds(0, depth), :], wu_s.at[slot, :, dst])
            for m in range(depth // fp):
                add(ref.at[pl.ds(depth + m * fp, fp), :], wd_s.at[slot, dst, pl.ds(m * fp, fp)])
            add(ref.at[pl.ds(2 * depth, RANK), :], b_s.at[slot, :, dst])
            for m in range(fp // RANK):
                add(
                    ref.at[pl.ds(2 * depth + RANK, RANK), pl.ds(m * RANK, RANK)],
                    a_s.at[slot, pl.ds(p * fp + m * RANK, RANK), :],
                )
        return made

    first = weights(0)
    half = len(first) // 2 if not kinds[0] and hidden == 2 * chunk and parts == 2 else len(first)
    begin([*ins, *first[:half]])
    loads, outs = [], []
    for block in range(blocks):
        rows = pl.ds(block * size, size)
        pairs = list(zip(acc_h, acc_s)) if carried else []
        if final:
            pairs += [(x_h, x_s), (attn_h, attn_s), (e_h, e_s)]
        loads.append(copies_of([(src.at[rows, :], dst.at[rows, :]) for src, dst in pairs], sem_acc.at[block]))
    finish_copies([*ins, *first[:half]])
    begin(first[half:])
    begin(loads[0])
    plus = lambda total, term: term if total is None else total + term
    for s in range(shards):
        slot = s % 2
        if s > 0:
            finish_copies(weights(s))
        if s + 1 < shards:
            begin(weights(s + 1))
        ga_s[...] = jnp.zeros_like(ga_s)
        gb_s[...] = jnp.zeros_like(gb_s)

        def place(p):
            if not kinds[s] or parts == 1:
                return p
            return core_ref[0] if p == 0 else 1 - core_ref[0]

        pieces = hidden // chunk

        def expand(step):
            block, at = step // pieces, step % pieces * chunk
            if s == 0 and block == 0 and at == chunk:
                finish_copies(first[half:])
            rows, cols = pl.ds(block * size, size), pl.ds(at, chunk)
            linear = dot(u_s[rows, :], wu_s[slot, :, cols]) + dot(z_s[rows, :], b_s[slot, :, cols])
            grad = dot(g_s[rows, :], wd_s[slot, cols, :], NT) + dot(
                dz_s[rows, :], a_s[slot, cols, :], NT
            )
            return linear, grad

        ahead = expand(0)
        for step in range(blocks * pieces):
            block, at = step // pieces, step % pieces * chunk
            rows = pl.ds(block * size, size)
            ub, zb, gb, db = u_s[rows, :], z_s[rows, :], g_s[rows, :], dz_s[rows, :]
            linear, grad = ahead
            if step + 1 < blocks * pieces:
                ahead = expand(step + 1)
            if at == 0:
                out = du = zd = dz = None
                if s == 0 and block + 1 < blocks:
                    begin(loads[block + 1])
            cols = pl.ds(at, chunk)
            active, slope = gelu_pair(linear)
            active = active.astype(BF)
            grad = (grad * slope).astype(BF)
            out = plus(out, dot(active, wd_s[slot, cols, :]))
            zd = plus(zd, dot(active, a_s[slot, cols, :]))
            du = plus(du, dot(grad, wu_s[slot, :, cols], NT))
            dz = plus(dz, dot(grad, b_s[slot, :, cols], NT))
            ga_s[cols, :] += dot(active, db, TN)
            gb_s[cols, :] += dot(grad, zb, TN)
            if at + chunk < hidden:
                continue
            if s == 0:
                finish_copies(loads[block])
            new = []
            for ref, value in zip(acc_s, (out, du, zd, dz)):
                new.append(ref[rows, :] + value if carried or s > 0 else value)
            if final and s == shards - 1:
                out, du, zd, dz = new
                zd, dz = zd.astype(BF), dz.astype(BF)
                x = x_s[rows, :].astype(F32)
                acc_o[rows, :] = x + attn_s[rows, :] + out + dot(zd, bcat[...])
                both = e_s[rows, :] + (du + dot(dz, acat[...], NT)) * gain[1:2, :]
                centred, scale = norm_stats(x)
                hat = centred * scale
                mean = jnp.mean(both, axis=-1, keepdims=True)
                match = jnp.mean(both * hat, axis=-1, keepdims=True)
                acc_u[rows, :] = gb.astype(F32) + scale * (both - mean - hat * match)
                for k, term in enumerate((dot(ub, dz, TN), dot(gb, zd, TN))):
                    where = pl.ds(k * depth, depth)
                    sums_s[where, :] = term if block == 0 else sums_s[where, :] + term
            else:
                for ref, value in zip(acc_s, new):
                    ref[rows, :] = value
            if s == shards - 1:
                outs.append(
                    copies_of(
                        [(src.at[rows, :], dst.at[rows, :]) for src, dst in zip(acc_s, out_h)],
                        sem_out.at[block],
                    )
                )
                begin(outs[-1])
        for p in range(parts):
            part = pl.ds(p * fp, fp)
            grads[s, place(p), pl.ds(0, fp), :] = ga_s[part, :].astype(BF)
            grads[s, place(p), pl.ds(fp, fp), :] = (LOWRANK_SCALE * gb_s[part, :]).astype(BF)
            many = attn_grads[s].shape[1]
            grads[s, p, pl.ds(2 * fp, many), :] = attn_grads[s][p]
    if final:
        sums[pl.ds(0, depth), :] = sums_s[pl.ds(0, depth), :].astype(sums.dtype)
        sums[pl.ds(depth, depth), :] = (LOWRANK_SCALE * sums_s[pl.ds(depth, depth), :]).astype(
            sums.dtype
        )
    for copies in outs:
        finish_copies(copies)


def mlp(core, acts, sources, kinds, acc, last, attn_grads, hidden, parts):
    u2, z, g, dz = acts
    full, depth = u2.shape
    shards, fp = len(kinds), hidden // parts
    flat = [part for source in sources for part in source]
    copies = max(4, (2 + depth // fp + fp // RANK) * parts)
    slots = min(2, shards)
    carried, final = acc is not None, last is not None
    operands = [core, u2, z, g, dz, *flat, *(acc or ()), *(last or ()), *attn_grads]
    shape = jax.ShapeDtypeStruct
    first_acc = 5 + len(flat)
    out_shape = [shape((full, depth), F32), shape((full, depth), F32)]
    if not final:
        out_shape += [shape((full, RANK), F32), shape((full, RANK), F32)]
    out_specs = [ANY] * len(out_shape) + [VMEM] * (2 if final else 1)
    out_shape.append(shape((shards, parts, 2 * fp + attn_grads[0].shape[1], RANK), BF))
    if final:
        out_shape.append(shape((2 * depth, RANK), F32))
    in_specs = [SMEM] + [ANY] * (len(operands) - 1)
    in_specs[-shards:] = [VMEM] * shards
    if final:
        in_specs[-3 - shards : -shards] = [VMEM] * 3
    scratch = [
        pltpu.VMEM((full, depth), BF),
        pltpu.VMEM((full, RANK), BF),
        pltpu.VMEM((full, depth), BF),
        pltpu.VMEM((full, RANK), BF),
        pltpu.VMEM((slots, depth, hidden), BF),
        pltpu.VMEM((slots, hidden, depth), BF),
        pltpu.VMEM((slots, RANK, hidden), BF),
        pltpu.VMEM((slots, hidden, RANK), BF),
        pltpu.VMEM((full, depth), F32),
        pltpu.VMEM((full, depth), F32),
        pltpu.VMEM((full, RANK), F32),
        pltpu.VMEM((full, RANK), F32),
        pltpu.VMEM((hidden, RANK), F32),
        pltpu.VMEM((hidden, RANK), F32),
    ]
    if final:
        scratch += [
            pltpu.VMEM((full, depth), BF),
            pltpu.VMEM((full, depth), F32),
            pltpu.VMEM((full, depth), F32),
            pltpu.VMEM((2 * depth, RANK), F32),
        ]
    scratch += [
        pltpu.SemaphoreType.DMA((4,)),
        pltpu.SemaphoreType.DMA((slots, copies)),
        pltpu.SemaphoreType.DMA((full // 256, 7)),
        pltpu.SemaphoreType.DMA((full // 256, 4)),
    ]
    aliases = {first_acc + i: i for i in range(4)} if carried and not final else {}
    return pl.pallas_call(
        partial(mlp_kernel, (kinds, carried, final, hidden, depth, full, parts)),
        out_shape=out_shape,
        in_specs=in_specs,
        out_specs=out_specs,
        input_output_aliases=aliases,
        scratch_shapes=scratch,
        compiler_params=params(),
        cost_estimate=cost(17 * shards, 8 << 20),
        name="mlp",
    )(*operands)


def reduce_kernel(cfg, *refs):
    heads, planes, sets = cfg
    it = iter(refs)
    take = lambda count: [next(it) for _ in range(count)]
    own = take(heads)
    ins = take(1 + max(rows[2] for rows in sets))
    outs = [take(2) for _ in sets]
    spaces = [take(24) for _ in sets]
    dp, head = lax.axis_index("dp"), lax.axis_index("head")
    core, plane = lax.rem(dp, 2), lax.div(dp, 2)
    flip = lambda at, o: at + o - 2 * sum(
        (lax.rem(lax.div(at, 1 << k), 2) * (1 << k) for k in range(6) if o >> k & 1), 0
    )
    sibling = {"dp": plane * 2 + 1 - core}
    head_peer = lambda o: {"head": flip(head, o)}
    plane_peer = lambda o: {"dp": flip(plane, o) * 2 + core}
    peers = [sibling] + [head_peer(o) for o in range(1, heads)]
    peers += [plane_peer(o) for o in range(1, planes)]
    mesh_id = pl.DeviceIdType.MESH
    barrier = pltpu.get_barrier_semaphore()
    for peer in peers:
        pl.semaphore_signal(barrier, inc=1, device_id=peer, device_id_type=mesh_id)

    def send(src, dst, ssem, rsem, peer):
        copy = pltpu.make_async_remote_copy(
            src_ref=src, dst_ref=dst, send_sem=ssem, recv_sem=rsem,
            device_id=peer, device_id_type=mesh_id,
        )
        copy.start()
        return copy

    def flow(rows, out_p, out_q, space):
        at, hp, which, start, hq = rows
        q = ins[which]
        half = q.shape[0] // 2
        (
            keep_p, keep_q, send1, recv1, send2, recv2, sum2, send3, recv3, gather,
            s1, r1, s2, r2, s3, r3, s4, r4, s5, r5, s6, r6, s7, r7,
        ) = space
        qp = hq // heads
        pz, qz = hp // planes, qp // planes
        for slot in range(2):
            total = own[0][slot, pl.ds(at, hp), :].astype(F32)
            for ref in own[1:]:
                total = total + ref[slot, pl.ds(at, hp), :].astype(F32)
            if slot == 0:
                keep_p[...] = total
            else:
                send1[pl.ds(0, hp), :] = total.astype(BF)
        share = lambda side: pl.ds(pl.multiple_of(side * half + start, hq), hq)
        send1[pl.ds(hp, hq), :] = q[share(1 - core), :].astype(BF)
        keep_q[...] = q[share(core), :].astype(F32)
        yield
        copy = send(send1, recv1, s1, r1, sibling)
        yield
        copy.wait()
        total_q = keep_q[...] + recv1[pl.ds(hp, hq), :].astype(F32)
        keep_q[...] = total_q
        send2[...] = total_q.astype(BF)
        copies = [
            send(
                send2.at[rows_of(flip(head, o), qp), :], recv2.at[o - 1], s2.at[o - 1], r2.at[o - 1],
                head_peer(o),
            )
            for o in range(1, heads)
        ]
        total_p = keep_p[...] + recv1[pl.ds(0, hp), :].astype(F32)
        keep_p[...] = total_p
        for k in range(planes):
            send3[k, pl.ds(0, pz), :] = total_p[k * pz : (k + 1) * pz].astype(BF)
        yield
        for copy in copies:
            copy.wait()
        piece = keep_q[rows_of(head, qp), :]
        for o in range(1, heads):
            piece = piece + recv2[o - 1].astype(F32)
        sum2[...] = piece
        for k in range(planes):
            send3[k, pl.ds(pz, qz), :] = piece[k * qz : (k + 1) * qz].astype(BF)
        copies = [
            send(send3.at[flip(plane, o)], recv3.at[o - 1], s3.at[o - 1], r3.at[o - 1], plane_peer(o))
            for o in range(1, planes)
        ]
        yield
        for copy in copies:
            copy.wait()
        mine_p = keep_p[rows_of(plane, pz), :]
        mine_q = sum2[rows_of(plane, qz), :]
        for o in range(1, planes):
            mine_p = mine_p + recv3[o - 1, pl.ds(0, pz), :].astype(F32)
            mine_q = mine_q + recv3[o - 1, pl.ds(pz, qz), :].astype(F32)
        gather[plane, pl.ds(0, pz), :] = mine_p.astype(BF)
        gather[plane, pl.ds(pz, qz), :] = mine_q.astype(BF)
        copies = [
            send(gather.at[plane], gather.at[plane], s4.at[o - 1], r4.at[o - 1], plane_peer(o))
            for o in range(1, planes)
        ]
        yield
        for copy in copies:
            copy.wait()
        for k in range(planes):
            out_q[core, rows_of(head * planes + k, qz), :] = gather[k, pl.ds(pz, qz), :]
            out_p[core, pl.ds(k * pz, pz), :] = gather[k, pl.ds(0, pz), :]
        mine = rows_of(head, qp)
        copies = [
            send(out_q.at[core, mine, :], out_q.at[core, mine, :], s5.at[o - 1], r5.at[o - 1], head_peer(o))
            for o in range(1, heads)
        ]
        copies.append(send(out_p.at[core], out_p.at[core], s6, r6, sibling))
        yield
        for copy in copies:
            copy.wait()
        copy = send(out_q.at[core], out_q.at[core], s7, r7, sibling)
        yield
        copy.wait()

    flows = [
        flow(rows, *out, space) for rows, out, space in zip(sets, outs, spaces)
    ]
    for one in flows:
        next(one)
    pl.semaphore_wait(barrier, len(peers))
    done = object()
    while flows:
        flows = [one for one in flows if next(one, done) is not done]


def reduce_all(own, rest, qs, sets, heads, planes):
    one = pltpu.SemaphoreType.DMA
    shape, vmem = jax.ShapeDtypeStruct, pltpu.VMEM
    scratch, out_shape, operands = [], [], [own, *rest, *qs]
    for _, hp, _, _, hq in sets:
        qp = hq // heads
        pz, qz = hp // planes, qp // planes
        out_shape += [shape((2, hp, RANK), BF), shape((2, hq, RANK), BF)]
        scratch += [
            vmem((hp, RANK), F32), vmem((hq, RANK), F32),
            vmem((hp + hq, RANK), BF), vmem((hp + hq, RANK), BF),
            vmem((hq, RANK), BF), vmem((heads - 1, qp, RANK), BF), vmem((qp, RANK), F32),
            vmem((planes, pz + qz, RANK), BF), vmem((planes - 1, pz + qz, RANK), BF),
            vmem((planes, pz + qz, RANK), BF),
            one, one,
            one((heads - 1,)), one((heads - 1,)),
            one((planes - 1,)), one((planes - 1,)),
            one((planes - 1,)), one((planes - 1,)),
            one((heads - 1,)), one((heads - 1,)),
            one, one, one, one,
        ]
    return pl.pallas_call(
        partial(reduce_kernel, (heads, planes, sets)),
        out_shape=out_shape,
        in_specs=[VMEM] * len(operands),
        out_specs=[VMEM] * len(out_shape),
        scratch_shapes=scratch,
        compiler_params=pltpu.CompilerParams(
            collective_id=0, has_side_effects=True, vmem_limit_bytes=60 << 20
        ),
        name="reduce",
    )(*operands)


def update_kernel(cfg, *refs):
    factors, merges, tensors, slots = cfg
    it = iter(refs)
    take = lambda count: [next(it) for _ in range(count)]
    count, wide = len(factors), max(slots) + 1
    (mask,) = take(1)
    grads = take(6)
    w_h, m_h = dict(zip(tensors, take(len(tensors)))), dict(zip(tensors, take(len(tensors))))
    resets = {t: next(it) for t in tensors if t[0] == "a"}
    frozen = take(wide)
    new_w, new_m = dict(zip(tensors, take(len(tensors)))), dict(zip(tensors, take(len(tensors))))
    out_c, out_l = take(wide), take(wide)
    w_s, m_s, n_s = take(count), take(count), take(count)
    r_s = {i: next(it) for i in range(count) if factors[i][0] == "a"}
    frozen_s, c_s, l_s = take(len(merges)), take(len(merges)), take(len(merges))
    sem_in, sem_out = take(2)
    loads, stores = [], []

    def load(src, dst):
        copy = pltpu.make_async_copy(src, dst, sem_in.at[len(loads)])
        copy.start()
        loads.append(copy)
        return copy

    def store(src, dst):
        copy = pltpu.make_async_copy(src, dst, sem_out.at[len(stores)])
        copy.start()
        stores.append(copy)

    pick = lambda ref, index: ref if index is None else ref.at[index]
    pick2 = lambda ref, k, index: ref.at[k] if index is None else ref.at[k, index]
    flag = mask[...].astype(F32)
    flag_col = jnp.broadcast_to(flag, (RANK, RANK)).T[:, :1]

    def load_factor(i):
        kind, tensor, index, _ = factors[i]
        mine = [load(pick(w_h[tensor], index), w_s[i])]
        mine += [load(pick2(m_h[tensor], k, index), m_s[i].at[k]) for k in range(2)]
        if kind == "a":
            mine.append(load(pick(resets[tensor], index), r_s[i]))
        return mine

    def step(i):
        kind, tensor, index, (source, spans) = factors[i]
        parts = [grads[source][pl.ds(at, size), :].astype(F32) for at, size in spans]
        grad = parts[0] if len(parts) == 1 else jnp.concatenate(parts, axis=0)
        if kind == "b":
            grad = grad.T
        keep = 1.0 - (flag if kind == "a" else flag_col)
        first = BETA_FIRST * m_s[i][0] + (1.0 - BETA_FIRST) * grad
        second = BETA_SECOND * m_s[i][1] + (1.0 - BETA_SECOND) * grad * grad
        scaled = first * (1.0 / (1.0 - BETA_FIRST**STEP))
        root = jnp.sqrt(second * (1.0 / (1.0 - BETA_SECOND**STEP)))
        weight = w_s[i][...]
        weight = weight - LEARN_RATE * (scaled / (root + ADAM_EPSILON) + WEIGHT_DECAY * weight)
        w_s[i][...] = weight
        m_s[i][0] = first * keep
        m_s[i][1] = second * keep
        for k in range(2):
            store(m_s[i].at[k], pick2(new_m[tensor], k, index))
        if kind == "a":
            n_s[i][...] = jnp.where(flag > 0.5, r_s[i][...].astype(F32), weight)
        else:
            n_s[i][...] = weight * keep
        store(n_s[i], pick(new_w[tensor], index))

    def split(value):
        high = value.astype(BF)
        return high, (value - high.astype(F32)).astype(BF)

    def merge(i):
        left, right, index = merges[i]
        right_high, right_low = split(w_s[right][...])
        right_all = jnp.concatenate([right_high, right_low, right_high], axis=0)
        total = w_s[left].shape[0]
        block = min(256, total)
        for at in range(0, total, block):
            rows = pl.ds(at, block)
            high, low = split(w_s[left][rows, :] * (LOWRANK_SCALE * flag))
            merged = frozen_s[i][rows, :].astype(F32) + dot(
                jnp.concatenate([high, high, low], axis=1), right_all
            )
            c_s[i][rows, :] = merged
            l_s[i][rows, :] = merged.astype(BF)
            store(c_s[i].at[rows, :], pick(out_c[slots[i]], index).at[rows, :])
            store(l_s[i].at[rows, :], pick(out_l[slots[i]], index).at[rows, :])

    waits = []

    def fetch(i):
        left, right, index = merges[i]
        waits.append(load_factor(left) + load_factor(right))
        waits[-1].append(load(pick(frozen[slots[i]], index), frozen_s[i]))

    for i in range(min(2, len(merges))):
        fetch(i)
    for i, (left, right, index) in enumerate(merges):
        if i + 2 < len(merges):
            fetch(i + 2)
        for copy in waits[i]:
            copy.wait()
        step(left)
        step(right)
        merge(i)
    for copy in stores:
        copy.wait()


def update(mask, grads, factors, weights, merges, frozen):
    shape = jax.ShapeDtypeStruct
    tensors = sorted(weights)
    inner = lambda array, index: array.shape if index is None else array.shape[1:]
    shapes = [inner(weights[f[1]][0], f[2]) for f in factors]
    picked = [inner(w, m[2]) for m, w in zip(merges, frozen)]
    unique, slots = [], []
    for w in frozen:
        hit = [k for k, u in enumerate(unique) if u is w]
        if not hit:
            unique.append(w)
        slots.append(hit[0] if hit else len(unique) - 1)
    out_shape = [shape(weights[t][k].shape, F32) for k in range(2) for t in tensors]
    out_shape += [shape(u.shape, kind) for kind in (F32, BF) for u in unique]
    operands = [mask, *grads] + [weights[t][k] for k in range(2) for t in tensors]
    operands += [weights[t][2] for t in tensors if t[0] == "a"] + unique
    kinds = [f[0] for f in factors]
    scratch = [pltpu.VMEM(s, F32) for s in shapes]
    scratch += [pltpu.VMEM((2, *s), F32) for s in shapes]
    scratch += [pltpu.VMEM(s, F32) for s in shapes]
    scratch += [pltpu.VMEM(s, BF) for s, k in zip(shapes, kinds) if k == "a"]
    scratch += [pltpu.VMEM(s, kind) for kind in (BF, F32, BF) for s in picked]
    loads = 3 * len(factors) + kinds.count("a") + len(frozen)
    stores = 3 * len(factors) + sum(2 * (-(-s[0] // 256)) for s in picked)
    scratch += [pltpu.SemaphoreType.DMA((loads,)), pltpu.SemaphoreType.DMA((stores,))]
    return pl.pallas_call(
        partial(update_kernel, (factors, merges, tensors, slots)),
        out_shape=out_shape,
        in_specs=[VMEM] * 7 + [ANY] * (len(operands) - 7),
        out_specs=[ANY] * len(out_shape),
        scratch_shapes=scratch,
        compiler_params=params(),
        cost_estimate=cost(18, 60 << 20),
        name="update",
    )(*operands)


def rotary_tables(full):
    half = ROT_DIM // 2
    frequency = np.float32(ROPE_BASE) ** (-2.0 * np.arange(half, dtype=np.float32) / ROT_DIM)
    angles = np.arange(full, dtype=np.float32)[:, None] * frequency.astype(np.float32)[None, :]
    cosine = np.ones((full, HEAD_DIM), np.float32)
    sine = np.zeros((full, HEAD_DIM), np.float32)
    cosine[:, :half] = cosine[:, half:ROT_DIM] = np.cos(angles)
    sine[:, :half] = -np.sin(angles)
    sine[:, half:ROT_DIM] = np.sin(angles)
    return tuple(jnp.asarray(np.tile(t, (1, LANES // HEAD_DIM))) for t in (cosine, sine))


def per_device(
    layer_input_rows,
    lengths,
    cotangent,
    frozen_projection_weight,
    frozen_outproj_weight,
    frozen_up_weight,
    frozen_down_weight,
    frozen_norm_gain,
    frozen_norm_bias,
    shared_input_factors,
    outproj_input_factor,
    down_input_factor,
    projection_output_factors,
    up_output_factor,
    output_side_factors,
    input_factor_moments,
    outproj_input_factor_moments,
    down_input_factor_moments,
    projection_output_factor_moments,
    up_output_factor_moments,
    outproj_output_factor_moments,
    reset_input_factor,
    reset_outproj_input_factor,
    reset_down_input_factor,
    component_merge_mask,
):
    full, depth = layer_input_rows.shape[1:]
    x, cot = layer_input_rows[0], cotangent[0]
    width, hidden = frozen_outproj_weight.shape[0], frozen_down_weight.shape[0]
    heads, groups = lax.axis_size("head"), lax.axis_size("dp")
    parts = 2 if width % (2 * LANES) == 0 else 1
    place = lax.axis_index("head")
    core = lax.rem(lax.axis_index("dp"), 2)
    core_at = (core if parts == 2 else jnp.zeros_like(core)).reshape(1).astype(jnp.int32)
    length = lax.dynamic_slice_in_dim(lengths, place, 1)
    tables = rotary_tables(full)

    def over_head(value, offset):
        return lax.ppermute(value, "head", [(i, i ^ offset) for i in range(heads)])

    def over_core(value):
        return lax.ppermute(value, "dp", [(i, i ^ 1) for i in range(groups)])

    def relay(by_x, by_y):
        sent = jnp.where(core == 0, by_y, by_x)
        pairs = [
            (d * heads + h, d * heads + (h ^ (1 if d % 2 == 0 else 2)))
            for d in range(groups)
            for h in range(heads)
        ]
        return lax.ppermute(sent, ("dp", "head"), pairs)

    def both(value):
        return [value, over_core(value)] if parts == 2 else [value]

    pa, b4q, aob = pack(
        "attn", core_at, frozen_projection_weight, frozen_outproj_weight, projection_output_factors,
        outproj_input_factor, parts,
    )
    got_a = {o: over_head(pa, o) for o in (1, 2)}
    u1, z1, dz1, acat1, bcat1, g = prologue(
        0, length, x, cot, frozen_norm_gain, frozen_norm_bias, shared_input_factors, output_side_factors
    )
    acts1 = (u1, z1, g, dz1)
    own_a = (frozen_projection_weight, frozen_outproj_weight, b4q, aob)
    after = lax.optimization_barrier
    made, grads_a = {}, {}
    *made[0], grads_a[0] = attention(
        length, core_at, acts1, tables, own_a, True, None, width, parts
    )
    got_a[1], got_a[2], pm_in, grads_a[0] = after((got_a[1], got_a[2], frozen_up_weight, grads_a[0]))
    pm, b4up, adb = pack(
        "mlp", core_at, pm_in, frozen_down_weight, up_output_factor, down_input_factor, parts
    )
    own_m = (frozen_up_weight, frozen_down_weight, b4up, adb)
    pairs_a = {o: both(got_a[o]) for o in (1, 2)}
    acts1 = (u1, z1, g, after((dz1, pm))[0])
    if heads == 4 and parts == 2:
        got_a[3] = relay(got_a[1], got_a[2])
    else:
        for o in range(3, heads):
            got_a[o] = over_head(pa, o)
    for o in range(1, heads):
        if o == 2 and heads > 3:
            got_a[3], pm, grads_a[1] = after((got_a[3], pm, grads_a[1]))
            pairs_a[3] = both(got_a[3])
        elif o > 3:
            pairs_a[o] = both(got_a[o])
        if o == 2:
            got_m = {k: over_head(pm, k) for k in (1, 2)}
        pairs_a[o][0] = after((pairs_a[o][0], grads_a[o - 1]))[0]
        last = None
        if o == heads - 1:
            last = (
                (frozen_norm_gain, acat1, bcat1),
                [own_a] + [pairs_a[k] for k in range(1, o)],
                [made[k] for k in range(o)],
            )
        *made[o], grads_a[o] = attention(
            length, core_at, acts1, tables, pairs_a[o], False, last, width, parts
        )
    attn, e_one, q_attn = made[heads - 1]
    got_m[1], got_m[2], g_in, q_attn = after((got_m[1], got_m[2], g, q_attn))
    u2, z2, dz2, acat2, bcat2 = prologue(
        1, length, x, g_in, frozen_norm_gain, frozen_norm_bias, shared_input_factors,
        output_side_factors,
    )
    acts2 = (u2, z2, g, dz2)
    pairs_m = {o: both(got_m[o]) for o in (1, 2)}
    if heads == 4 and parts == 2:
        got_m[3] = relay(got_m[1], got_m[2])
    else:
        for o in range(3, heads):
            got_m[o] = over_head(pm, o)
    grads_m = {}
    *acc_m, grad = mlp(
        core_at, acts2, [pairs_m[1], pairs_m[2]], (False, False), None, None, [grads_a[1], grads_a[2]],
        hidden, parts,
    )
    grads_m[1], grads_m[2] = grad[0], grad[1]
    for o in range(3, heads):
        got_m[o], acc_m[2] = after((got_m[o], acc_m[2]))
        *acc_m, grad = mlp(
            core_at, acts2, [both(got_m[o])], (False,), acc_m, None, [grads_a[o]], hidden, parts
        )
        grads_m[o] = grad[0]
    layer_out, grad_in, grad, q_mlp = mlp(
        core_at, acts2, [own_m], (True,), acc_m, (x, attn, e_one, frozen_norm_gain, acat2, bcat2),
        [grads_a[0]], hidden, parts,
    )
    grads_m[0] = grad[0]

    def gather(grads):
        flat = {o: grad.reshape(grad.shape[0], -1, RANK) for o, grad in grads.items()}
        return flat[0], [over_head(flat[o], o) for o in range(1, heads)]

    def over_head_sum(own, rest):
        total = own.astype(F32)
        for other in rest:
            total = total + other.astype(F32)
        if parts == 2:
            total = jnp.where(core == 0, total, total[::-1])
        return total.astype(BF)

    own_all, rest_all = gather(grads_m)
    planes = groups // 2
    wp, fp = width // parts, hidden // parts
    rows_a, rows_m = 4 * wp, 2 * fp
    if parts == 2 and depth // (heads * planes) % 16 == 0 and fp // planes % 16 == 0:
        p_attn, q_one, p_down, q_two, p_up, q_mlp = reduce_all(
            own_all, rest_all, (q_attn, q_mlp),
            ((rows_m, rows_a, 0, 0, depth), (0, fp, 0, depth, depth), (fp, fp, 1, 0, depth)),
            heads, planes,
        )
    else:
        p_all = lax.psum(over_head_sum(own_all, rest_all), "dp")
        p_down, p_up, p_attn = p_all[:, :fp], p_all[:, fp:rows_m], p_all[:, rows_m:]
        q_attn, q_mlp = lax.psum((q_attn, q_mlp.astype(BF)), ("dp", "head"))
        q_attn = q_attn.reshape(2, 2, depth, RANK)
        q_one, q_two = q_attn[:, 0], q_attn[:, 1]
    mask = component_merge_mask.reshape(1, RANK)
    from_a = lambda k: (0, tuple((p * rows_a + k * wp, wp) for p in range(parts)))
    from_m = lambda k: (2 + k, ((0, hidden),))
    from_q = lambda half, k: (1 if k == 0 else 4, ((half * depth, depth),))
    from_r = lambda k: (5, ((k * depth, depth),))
    factors = (
        ("a", "a_in", 0, from_q(0, 0)),
        ("b", "b_qkv", 0, from_a(0)),
        ("a", "a_in", 1, from_q(0, 1)),
        ("b", "b_qkv", 1, from_a(1)),
        ("a", "a_in", 2, from_q(1, 0)),
        ("b", "b_qkv", 2, from_a(2)),
        ("a", "a_out", None, from_a(3)),
        ("b", "b_out", 0, from_q(1, 1)),
        ("a", "a_in", 3, from_r(0)),
        ("b", "b_up", None, from_m(1)),
        ("a", "a_down", None, from_m(0)),
        ("b", "b_out", 1, from_r(1)),
    )
    weights = {
        "a_in": (shared_input_factors, input_factor_moments, reset_input_factor),
        "a_out": (outproj_input_factor, outproj_input_factor_moments, reset_outproj_input_factor),
        "a_down": (down_input_factor, down_input_factor_moments, reset_down_input_factor),
        "b_qkv": (projection_output_factors, projection_output_factor_moments, None),
        "b_up": (up_output_factor, up_output_factor_moments, None),
        "b_out": (output_side_factors, outproj_output_factor_moments, None),
    }
    (
        new_a_down, new_a_in, new_a_out, new_b_out, new_b_qkv, new_b_up,
        new_m_a_down, new_m_a_in, new_m_a_out, new_m_b_out, new_m_b_qkv, new_m_b_up,
        comb_qkv, comb_out, comb_up, comb_down, copy_qkv, copy_out, copy_up, copy_down,
    ) = update(
        mask, [v.reshape(-1, RANK) for v in (p_attn, q_one, p_down, p_up, q_two, q_mlp)], factors, weights,
        ((0, 1, 0), (2, 3, 1), (4, 5, 2), (6, 7, None), (8, 9, None), (10, 11, None)),
        (frozen_projection_weight,) * 3
        + (frozen_outproj_weight, frozen_up_weight, frozen_down_weight),
    )
    return (
        layer_out[None], grad_in[None],
        new_a_in, new_a_out, new_a_down, new_b_qkv, new_b_up, new_b_out,
        new_m_a_in, new_m_a_out, new_m_a_down, new_m_b_qkv, new_m_b_up, new_m_b_out,
        comb_qkv, comb_out, comb_up, comb_down, copy_qkv, copy_out, copy_up, copy_down,
    )


def solution(mesh):
    return jax.shard_map(
        per_device,
        mesh=mesh,
        in_specs=(
            P(("dp", "head"), None, None),
            P("dp"),
            P(("dp", "head"), None, None),
            P(None, None, "head"),
            P("head", None),
            P(None, "head"),
            P("head", None),
            P(),
            P(),
            P(),
            P("head", None),
            P("head", None),
            P(None, None, "head"),
            P(None, "head"),
            P(),
            P(),
            P(None, "head", None),
            P(None, "head", None),
            P(None, None, None, "head"),
            P(None, None, "head"),
            P(),
            P(),
            P("head", None),
            P("head", None),
            P(),
        ),
        out_specs=(
            P(("dp", "head"), None, None),
            P(("dp", "head"), None, None),
            P(),
            P("head", None),
            P("head", None),
            P(None, None, "head"),
            P(None, "head"),
            P(),
            P(),
            P(None, "head", None),
            P(None, "head", None),
            P(None, None, None, "head"),
            P(None, None, "head"),
            P(),
            P(None, None, "head"),
            P("head", None),
            P(None, "head"),
            P("head", None),
            P(None, None, "head"),
            P("head", None),
            P(None, "head"),
            P("head", None),
        ),
        check_vma=False,
    )
```
